256 devices in a mesh: round: 32 (over x, z_lo, core), head: 4 (over y), rep: 2 (over z_hi).
Axes of the slice: x: 4, y: 4, z: 8 (z_hi: 2, z_lo: 4; z = z_hi * 4 + z_lo), core: 2. Of those that a mesh axis runs over, the one named last changes fastest.
Arguments:
- query_rows: bfloat16 [8192, 8192], P(('rep', 'round'), 'head'), parts along dimension 0, may hold values from -12 to 12
- table_key_rows: bfloat16 [8192, 1024], P(('rep', 'round'), 'head'), parts along dimension 0, may hold values from -4 to 4
- table_value_rows: bfloat16 [8192, 1024], P(('rep', 'round'), 'head'), parts along dimension 0, may hold values from -6 to 6
- out_grad: bfloat16 [8192, 8192], P(('rep', 'round'), 'head'), parts along dimension 0, may hold values from -96 to 96
- round_lengths: int32 [32], P('rep'), parts along dimension 0, may hold values from 1 to 768, 4096 in all
- assignment: int32 [128], P('rep'), parts along dimension 0, may hold values from 0 to 63, as said below
Outputs:
- query_grad: bfloat16 [8192, 8192], P(('rep', 'round'), 'head'), parts along dimension 0
- key_gradient: bfloat16 [8192, 1024], P(('rep', 'round'), 'head'), parts along dimension 0
- value_gradient: bfloat16 [8192, 1024], P(('rep', 'round'), 'head'), parts along dimension 0
The draws below stay inside these ranges and needn't reach their ends.
There are 2 independent parts, one for each index of `rep`. The reference program is written for one: setup_inputs(seed, part) draws one part's arguments, and reference() takes and returns one part's arrays. A program takes and returns all parts, laid end to end along the dimension named above; each array names one. Nothing has to cross between parts.
Inputs may be any that keep to these rules, and one draw needn't show every extreme that they name: `round_lengths`: the 16 lengths sum to 4096; the longest is exactly 768. `assignment`: each block number appears once; entries 2i and 2i + 1 sum to 63.
All inputs are finite; a program needn't handle non-finite values.
Results may differ from the reference program's by a relative error of at most 0.005.
Values may be sent and summed in bfloat16 or wider, within the bound.
A program may use at most 128 MiB of HBM per device.

```python
import math
import jax
import jax.numpy as jnp
import numpy as np
from jax import lax

QUERY_HEADS = 64
KEY_VALUE_HEADS = 8
HEAD_SIZE = 128
ROUNDS = 16
RWIN = 8
TRAJECTORY_LEN = 4096
HALF = 64
BLOCKS = 64


def assignment_pairs(key):
    pair_key = jax.random.fold_in(key, 11)
    shuffled = jax.random.permutation(pair_key, BLOCKS // 2).astype(jnp.int32)
    mirrored = (BLOCKS - 1 - shuffled).astype(jnp.int32)
    return jnp.stack([shuffled, mirrored], axis=1).reshape(BLOCKS)


def draw_assignment(key, part):
    return assignment_pairs(key)


def draw_query_rows(key, part):
    key = jax.random.fold_in(key, 31)
    value_entries = jnp.clip(jax.random.normal(key, (TRAJECTORY_LEN, QUERY_HEADS, HEAD_SIZE)), -4.0, 4.0)
    return value_entries.reshape(TRAJECTORY_LEN, QUERY_HEADS * HEAD_SIZE).astype(jnp.bfloat16)


def draw_table_key_rows(key, part):
    key = jax.random.fold_in(key, 47)
    value_entries = jnp.clip(jax.random.normal(key, (TRAJECTORY_LEN, KEY_VALUE_HEADS, HEAD_SIZE)), -4.0, 4.0)
    return value_entries.reshape(TRAJECTORY_LEN, KEY_VALUE_HEADS * HEAD_SIZE).astype(jnp.bfloat16)


def steps_of(stream_key, shape, pieces, least, high):
    gain, own = 1.0, jax.random.fold_in(stream_key, 6)
    for dim, parts in pieces:
        steps = jnp.exp(jax.random.uniform(jax.random.fold_in(own, dim), (parts,), jnp.float32, least / len(pieces), high / len(pieces)))
        gain = gain * jnp.repeat(steps, shape[dim] // parts).reshape([-1 if axis == dim else 1 for axis in range(len(shape))])
    return gain


def length_profile(count, total, most, slope):
    weights = [(1 << 20) // math.isqrt(grade ** slope) + 1 for grade in range(2, count + 1)]
    spare, given = total - most - (count - 1), [1] * (count - 1)
    while spare > 0:
        candidates = [i for i in range(count - 1) if given[i] < most]
        whole, left = sum([weights[i] for i in candidates]), spare
        for i in candidates:
            more = min(most - given[i], max(1, left * weights[i] // whole), spare)
            given[i] = given[i] + more
            spare = spare - more
    return np.array([most] + given)


def ragged(own_key, amount, total, bound, slope):
    if amount == 2:
        one = jax.random.randint(own_key, (), max(1, total - bound), min(bound, total - 1) + 1)
        return jnp.stack([one, total - one])
    tallies = jnp.asarray(length_profile(amount, total, bound, slope), jnp.int32)
    twos = (amount - 1) // 2
    donor, taker = tallies[1:1 + 2 * twos:2], tallies[2:2 + 2 * twos:2]
    room = jnp.minimum(donor - 1, bound - taker)
    moved = jax.random.randint(jax.random.fold_in(own_key, 1), (twos,), 0, 1 << 20) % (room + 1)
    tallies = tallies.at[1:1 + 2 * twos:2].set(donor - moved).at[2:2 + 2 * twos:2].set(taker + moved)
    return tallies[jax.random.permutation(jax.random.fold_in(own_key, 2), amount)]


def normal_values(key, dims, deviation, limit, pieces=(), kind=jnp.bfloat16):
    loudness = steps_of(key, dims, pieces, -0.22, 0.18) if pieces else 1.0
    values = jax.random.normal(key, dims, jnp.float32) * deviation * loudness
    return jnp.minimum(jnp.maximum(values, -limit), limit).astype(kind)


def setup_inputs(seed: int = 0, part: int = 0) -> dict:
    keys = jax.random.split(jax.random.key(seed), 7)
    part_keys = jax.random.split(jax.random.fold_in(keys[6], part), 7)
    return {
        "query_rows": draw_query_rows(jax.random.fold_in(jax.random.fold_in(keys[6], part), 71), part),
        "table_key_rows": draw_table_key_rows(jax.random.fold_in(jax.random.fold_in(keys[6], part), 71), part),
        "table_value_rows": normal_values(part_keys[2], (TRAJECTORY_LEN, KEY_VALUE_HEADS * HEAD_SIZE), 1.0, 6.0, ((0, 32), (1, 4))),
        "out_grad": normal_values(part_keys[3], (TRAJECTORY_LEN, QUERY_HEADS * HEAD_SIZE), (TRAJECTORY_LEN ** 0.5 / 4), 96.0, ((0, 32), (1, 4))),
        "round_lengths": ragged(part_keys[4], ROUNDS, TRAJECTORY_LEN, 3 * TRAJECTORY_LEN // ROUNDS, 2).astype(jnp.int32),
        "assignment": draw_assignment(jax.random.fold_in(jax.random.fold_in(keys[6], part), 71), part),
    }


def row_positions(assignment):
    row_index = jnp.arange(TRAJECTORY_LEN, dtype=jnp.int32)
    return (assignment[row_index // HALF] * HALF + row_index % HALF).astype(jnp.int32)


def round_ids(positions, round_lengths):
    round_ends = jnp.cumsum(round_lengths).astype(jnp.int32)[:-1]
    return jnp.sum((positions[:, None] >= round_ends[None, :]).astype(jnp.int32), axis=1).astype(jnp.int32)


def reference(query_rows, table_key_rows, table_value_rows, out_grad, round_lengths, assignment):
    score_scale = HEAD_SIZE ** -0.5
    positions = row_positions(assignment)
    rounds = round_ids(positions, round_lengths)
    visible = (positions[None, :] <= positions[:, None]) & (rounds[None, :] > rounds[:, None] - RWIN)
    query_group_width = QUERY_HEADS // KEY_VALUE_HEADS
    query_heads = query_rows.reshape(TRAJECTORY_LEN, QUERY_HEADS, HEAD_SIZE).transpose(1, 0, 2)
    grad_heads = out_grad.reshape(TRAJECTORY_LEN, QUERY_HEADS, HEAD_SIZE).transpose(1, 0, 2)
    heads_of_key = jnp.repeat(table_key_rows.reshape(TRAJECTORY_LEN, KEY_VALUE_HEADS, HEAD_SIZE), query_group_width, axis=1).transpose(1, 0, 2)
    heads_of_value = jnp.repeat(table_value_rows.reshape(TRAJECTORY_LEN, KEY_VALUE_HEADS, HEAD_SIZE), query_group_width, axis=1).transpose(1, 0, 2)

    def one_head(head_item):
        query_h, key_h, value_h, grad_h = head_item
        scores = jnp.dot(query_h, key_h.T, preferred_element_type=jnp.float32) * score_scale
        scores = jnp.where(visible, scores, -jnp.inf)
        log_total = jax.nn.logsumexp(scores, axis=1)
        weights = jnp.exp(scores - log_total[:, None])
        dprobs = jnp.dot(grad_h, value_h.T, preferred_element_type=jnp.float32)
        row_delta = jnp.sum(weights * dprobs, axis=1)
        dscores = weights * (dprobs - row_delta[:, None])
        weights_b = weights.astype(jnp.bfloat16)
        dscores_b = dscores.astype(jnp.bfloat16)
        query_part = jnp.dot(dscores_b, key_h, preferred_element_type=jnp.float32) * score_scale
        key_portion = jnp.dot(dscores_b.T, query_h, preferred_element_type=jnp.float32) * score_scale
        value_portion = jnp.dot(weights_b.T, grad_h, preferred_element_type=jnp.float32)
        return query_part.astype(jnp.bfloat16), key_portion, value_portion

    query_part, key_portion, value_portion = lax.map(one_head, (query_heads, heads_of_key, heads_of_value, grad_heads))
    query_grad = query_part.transpose(1, 0, 2).reshape(TRAJECTORY_LEN, QUERY_HEADS * HEAD_SIZE)
    key_gradient_sum = key_portion.reshape(KEY_VALUE_HEADS, query_group_width, TRAJECTORY_LEN, HEAD_SIZE).sum(axis=1)
    value_gradient_sum = value_portion.reshape(KEY_VALUE_HEADS, query_group_width, TRAJECTORY_LEN, HEAD_SIZE).sum(axis=1)
    key_gradient = key_gradient_sum.transpose(1, 0, 2).reshape(TRAJECTORY_LEN, KEY_VALUE_HEADS * HEAD_SIZE).astype(jnp.bfloat16)
    value_gradient = value_gradient_sum.transpose(1, 0, 2).reshape(TRAJECTORY_LEN, KEY_VALUE_HEADS * HEAD_SIZE).astype(jnp.bfloat16)
    return query_grad, key_gradient, value_gradient
```

```python
import functools
import math

import jax
import jax.numpy as jnp
from jax import lax
from jax.experimental import pallas as pl
from jax.experimental.pallas import tpu as pltpu
from jax.sharding import PartitionSpec as P

HEAD_SIZE = 128
RWIN = 8
HALF = 64
RING = 4
LINE = 4
GROUP_HEADS = 8
COLS = GROUP_HEADS * HALF
SCALE = HEAD_SIZE**-0.5
SCALE2 = SCALE * math.log2(math.e)
FAR = -1e30
MESH = pl.DeviceIdType.MESH
F32 = jnp.float32
BF16 = jnp.bfloat16


def mul_nt(a, b):
    return lax.dot_general(a, b, (((1,), (1,)), ((), ())), preferred_element_type=F32)


def mul_nn(a, b):
    return lax.dot_general(a, b, (((1,), (0,)), ((), ())), preferred_element_type=F32)


def mul_tn(a, b):
    return lax.dot_general(a, b, (((0,), (0,)), ((), ())), preferred_element_type=F32)


def kernel(
    q_ref, k_ref, v_ref, g_ref, len_ref, asg_ref,
    dq_ref, dk_ref, dv_ref,
    kv, qin, gin, qcat, gcat, stats, start, dqacc, part, dextra, dqout, fin,
    s1r, s1l, r1l, r1r, s2r, s2l, r2l, r2r, s3, r3,
    local_sem, send_sem, recv_sem,
):
    blocks = asg_ref.shape[0]
    me = lax.axis_index("round")
    core, chip = lax.rem(me, 2), lax.div(me, 2)
    z, x = lax.rem(chip, LINE), lax.div(chip, LINE)
    sib = 1 - core

    def device(xx, zz, cc):
        return {"round": (xx * LINE + zz) * 2 + cc}

    def xat(k):
        return lax.rem(x + k, RING)

    def zat(k):
        return lax.rem(z + k, LINE)

    used = [0]

    def remote(src, dst, target):
        i = used[0]
        used[0] = i + 1
        return pltpu.make_async_remote_copy(
            src_ref=src, dst_ref=dst, send_sem=send_sem.at[i], recv_sem=recv_sem.at[i],
            device_id=target, device_id_type=MESH,
        )

    right, left = device(xat(1), z, core), device(xat(RING - 1), z, core)
    brother = device(x, z, sib)
    along_z = [None] + [device(x, zat(k), core) for k in range(1, LINE)]

    barrier = pltpu.get_barrier_semaphore()
    peers = [brother, right, left] + along_z[1:]
    for peer in peers:
        pl.semaphore_signal(barrier, inc=1, device_id=peer, device_id_type=MESH)
    pl.semaphore_wait(barrier, len(peers))

    def lanes(index, width):
        return pl.ds(pl.multiple_of(index * width, width), width)

    mine = z * RING + x
    own_rows, sib_rows = lanes(core, 128), lanes(sib, 128)
    wide = GROUP_HEADS * HEAD_SIZE
    swaps = [
        remote(k_ref.at[:, lanes(sib, 128)], kv.at[mine, 0, own_rows, :], brother),
        remote(v_ref.at[:, lanes(sib, 128)], kv.at[mine, 1, own_rows, :], brother),
        remote(q_ref.at[:, lanes(sib, wide)], qin.at[1], brother),
        remote(g_ref.at[:, lanes(sib, wide)], gin.at[1], brother),
    ]
    for swap in swaps:
        swap.start()
    own = [
        pltpu.make_async_copy(k_ref.at[:, lanes(core, 128)], kv.at[mine, 0, own_rows, :], local_sem.at[0]),
        pltpu.make_async_copy(v_ref.at[:, lanes(core, 128)], kv.at[mine, 1, own_rows, :], local_sem.at[1]),
        pltpu.make_async_copy(q_ref.at[:, lanes(core, wide)], qin.at[0], local_sem.at[2]),
        pltpu.make_async_copy(g_ref.at[:, lanes(core, wide)], gin.at[0], local_sem.at[3]),
    ]
    for copy in own:
        copy.start()
    own[0].wait()
    own[1].wait()
    swaps[0].wait_recv()
    swaps[1].wait_recv()

    def slot(xx, zz):
        return zz * RING + xx

    zsend = [None] + [remote(kv.at[mine], kv.at[mine], along_z[k]) for k in range(1, LINE)]
    xright = [remote(kv.at[slot(x, zat(k))], kv.at[slot(x, zat(k))], right) for k in range(LINE)]
    xleft = [remote(kv.at[slot(x, zat(k))], kv.at[slot(x, zat(k))], left) for k in range(LINE)]
    fright = [
        remote(kv.at[slot(xat(RING - 1), zat(k)), 0], kv.at[slot(xat(RING - 1), zat(k)), 0], right)
        for k in range(LINE)
    ]
    fleft = [
        remote(kv.at[slot(xat(1), zat(k)), 1], kv.at[slot(xat(1), zat(k)), 1], left)
        for k in range(LINE)
    ]
    order = [0, LINE - 1, 1, 2]
    xright[0].start()
    xleft[0].start()
    for k in (1, LINE - 1, 2):
        zsend[k].start()

    def relay(k):
        xright[k].wait_recv()
        fright[k].start()
        xleft[k].wait_recv()
        fleft[k].start()

    for n, k in enumerate(order):
        if n > 0:
            zsend[LINE - k].wait_recv()
            xright[k].start()
            xleft[k].start()
            relay(order[n - 1])
    relay(order[-1])
    for k in order:
        fright[k].wait_recv()
        fleft[k].wait_recv()
    own[2].wait()
    own[3].wait()
    swaps[2].wait_recv()
    swaps[3].wait_recv()

    pairs = [2 * chip + core, 2 * chip + sib]

    def pair_small(pair):
        first, second = asg_ref[2 * pair], asg_ref[2 * pair + 1]
        return jnp.minimum(first, second), (first > second).astype(jnp.int32)

    ends, total = [], 0
    for j in range(15):
        total = total + len_ref[j]
        ends.append(total)
    lane_row = lax.rem(lax.broadcasted_iota(jnp.int32, (8, COLS), 1), HALF)
    sub_row = lax.broadcasted_iota(jnp.int32, (8, COLS), 0)
    for p in range(2):
        small, flag = pair_small(pairs[p])
        for side in range(2):
            turned = flag == 1 - side
            for h in range(GROUP_HEADS):
                to = (p, slice(h * HALF, (h + 1) * HALF), slice(side * 128, side * 128 + 128))
                cols = slice(h * 128, h * 128 + 128)
                qcat[to] = jnp.where(turned, qin[p, HALF:, cols], qin[p, :HALF, cols])
                gcat[to] = jnp.where(turned, gin[p, HALF:, cols], gin[p, :HALF, cols])
            base = (small if side == 0 else blocks - 1 - small) * HALF
            first = jnp.zeros((8, COLS), jnp.int32)
            for j in range(15 - RWIN + 1):
                first = jnp.where(base + lane_row >= ends[j + RWIN - 1], ends[j], first)
            start[p, side] = first - sub_row
            stats[0, p, side] = jnp.full((8, COLS), FAR, F32)
            stats[1, p, side] = jnp.zeros((8, COLS), F32)
            stats[2, p, side] = jnp.zeros((8, COLS), F32)
        dqacc[p] = jnp.zeros((COLS, 256), F32)

    eight = 8 * lax.broadcasted_iota(jnp.int32, (8, 8, COLS), 0)
    never = 1 << 20

    def load_pairs(first_slot, slots):
        small_k, large_k, small_v, large_v, firsts, flags = [], [], [], [], [], []
        for t in range(2 * slots):
            at = first_slot + t // 2
            pair = (lax.rem(at, RING) * LINE + lax.div(at, RING)) * 2 + t % 2
            small, flag = pair_small(pair)
            row = (t % 2) * 128
            turned = flag == 1
            for n, small_n, large_n in ((0, small_k, large_k), (1, small_v, large_v)):
                lo, hi = kv[at, n, row : row + HALF, :], kv[at, n, row + HALF : row + 128, :]
                small_n.append(jnp.where(turned, hi, lo))
                large_n.append(jnp.where(turned, lo, hi))
            firsts.append(small)
            flags.append(flag)
        return small_k, large_k, small_v, large_v, firsts, flags

    def halves(sel, small, large):
        zero = jnp.zeros_like(small)
        return jnp.concatenate(
            [jnp.where(sel, small, zero), jnp.where(sel, zero, large)], axis=1
        )

    def units(loaded, p):
        small_k, large_k, small_v, large_v, firsts, unused_flags = loaded
        mine_small, unused_flag = pair_small(pairs[p])
        tile_a, tile_b = [], []
        sels = []
        for j in firsts:
            sel = j < mine_small
            sels.append(sel)
            tile_a.append((None, start[p, 1] - j * HALF))
            begin = jnp.where(sel, start[p, 0] - j * HALF, start[p, 1] - (blocks - 1 - j) * HALF)
            tile_b.append((sel, jnp.where(j == mine_small, never, begin)))
        keys_a = jnp.concatenate(small_k, axis=0)
        values_a = jnp.concatenate(small_v, axis=0)
        keys_b = jnp.concatenate([halves(*b) for b in zip(sels, small_k, large_k)], axis=0)
        values_b = jnp.concatenate([halves(*b) for b in zip(sels, small_v, large_v)], axis=0)
        return (keys_a, values_a, tile_a, 1), (keys_b, values_b, tile_b, 0)

    def side_of(sel, ref_at):
        if sel is None:
            return ref_at(1)
        return jnp.where(sel, ref_at(0), ref_at(1))

    def products(p, keys, values, first_side):
        width = slice(128, 256) if first_side == 1 else slice(0, 256)
        return mul_nt(keys, qcat[p, :, width]), mul_nt(values, gcat[p, :, width])

    def stats_unit(p, sel, mask, scores, dprobs):
        scores = jnp.where(mask, scores * SCALE2, FAR)
        top = side_of(sel, lambda side: stats[0, p, side])
        new_top = jnp.maximum(top, jnp.max(scores, axis=0))
        rescale = jnp.exp2(top - new_top)
        probs = jnp.exp2(scores - new_top[None])
        total = side_of(sel, lambda side: stats[1, p, side]) * rescale + jnp.sum(probs, axis=0)
        weighted = side_of(sel, lambda side: stats[2, p, side]) * rescale + jnp.sum(
            probs * dprobs, axis=0
        )
        for n, new in enumerate((new_top, total, weighted)):
            if sel is None:
                stats[n, p, 1] = new
            else:
                old = stats[n, p, 1]
                stats[n, p, 0] = jnp.where(sel, new, stats[n, p, 0])
                stats[n, p, 1] = jnp.where(sel, old, new)

    def stats_pass(first_slot, slots):
        loaded = load_pairs(first_slot, slots)
        for p in range(2):
            for keys, values, tiles, first_side in units(loaded, p):
                scores, dprobs = products(p, keys, values, first_side)
                for t, (sel, begin) in enumerate(tiles):
                    rows = slice(t * HALF, (t + 1) * HALF)
                    stats_unit(
                        p, sel, eight >= begin[None],
                        scores[rows].reshape(8, 8, COLS), dprobs[rows].reshape(8, 8, COLS),
                    )

    def grad_unit(p, sel, mask, scores, dprobs):
        scores = jnp.where(mask, scores * SCALE2, FAR)
        log_total = side_of(sel, lambda side: stats[0, p, side])
        delta = side_of(sel, lambda side: stats[1, p, side])
        probs = jnp.exp2(scores - log_total[None])
        dscores = probs * (dprobs - delta[None])
        return (
            probs.reshape(HALF, COLS).astype(BF16),
            dscores.reshape(HALF, COLS).astype(BF16),
        )

    def grad_tile(p, keys, values, tiles, first_side):
        width = slice(128, 256) if first_side == 1 else slice(0, 256)
        scores, dprobs = products(p, keys, values, first_side)
        probs_b, dscores_b = [], []
        for t, (sel, mask) in enumerate(tiles):
            rows = slice(t * HALF, (t + 1) * HALF)
            one, two = grad_unit(
                p, sel, mask,
                scores[rows].reshape(8, 8, COLS), dprobs[rows].reshape(8, 8, COLS),
            )
            probs_b.append(one)
            dscores_b.append(two)
        probs_b = jnp.concatenate(probs_b, axis=0)
        dscores_b = jnp.concatenate(dscores_b, axis=0)
        dqacc[p, :, width] += mul_tn(dscores_b, keys)
        return mul_nn(dscores_b, qcat[p, :, width]), mul_nn(probs_b, gcat[p, :, width])

    def grad_pass(first_slot, slots):
        loaded = load_pairs(first_slot, slots)
        flags = loaded[-1]
        small = [0.0, 0.0]
        large = [0.0, 0.0]
        for p in range(2):
            (ka, va, ta, unused_a), (kb, vb, tb, unused_b) = units(loaded, p)
            ta = [(sel, eight >= begin[None]) for sel, begin in ta]
            masks_b = [(sel, eight >= begin[None]) for sel, begin in tb]
            grads_a = grad_tile(p, ka, va, ta, 1)
            grads_b = grad_tile(p, kb, vb, masks_b, 0)
            for n in range(2):
                small[n] = small[n] + grads_a[n]
                zero = jnp.zeros((HALF, 128), F32)
                add_small, add_large = [], []
                for t, (sel, unused_mask) in enumerate(tb):
                    rows = slice(t * HALF, (t + 1) * HALF)
                    add_small.append(jnp.where(sel, grads_b[n][rows, :128], zero))
                    add_large.append(jnp.where(sel, zero, grads_b[n][rows, 128:]))
                small[n] = small[n] + jnp.concatenate(add_small, axis=0)
                large[n] = large[n] + jnp.concatenate(add_large, axis=0)
        for n in range(2):
            for t, flag in enumerate(flags):
                rows = slice(t * HALF, (t + 1) * HALF)
                at, row = first_slot + t // 2, (t % 2) * 128
                turned = flag == 1
                lo, hi = small[n][rows], large[n][rows]
                part[at, n, row : row + HALF, :] = jnp.where(turned, hi, lo)
                part[at, n, row + HALF : row + 128, :] = jnp.where(turned, lo, hi)

    tri = lax.broadcasted_iota(jnp.int32, (8, 8, COLS), 1) + eight <= lax.rem(
        lax.broadcasted_iota(jnp.int32, (8, 8, COLS), 2), HALF
    )

    def own_tile(p):
        rows = own_rows if p == 0 else sib_rows
        small, flag = pair_small(pairs[p])
        turned = flag == 1
        zero = jnp.zeros((HALF, 128), BF16)

        def stack(n):
            pair = kv[mine, n, rows, :]
            lo, hi = pair[:HALF], pair[HALF:]
            return jnp.concatenate(
                [
                    jnp.concatenate([jnp.where(turned, hi, lo), zero], axis=1),
                    jnp.concatenate([zero, jnp.where(turned, lo, hi)], axis=1),
                ],
                axis=0,
            )

        masks = []
        for side in range(2):
            base = (small if side == 0 else blocks - 1 - small) * HALF
            masks.append(tri & (eight >= (start[p, side] - base)[None]))
        return stack(0), stack(1), masks, flag

    def side_const(side):
        return side == 0

    for p in range(2):
        keys, values, masks, unused_flag = own_tile(p)
        scores, dprobs = products(p, keys, values, 0)
        for side in range(2):
            rows = slice(side * HALF, (side + 1) * HALF)
            s = jnp.where(masks[side], scores[rows].reshape(8, 8, COLS) * SCALE2, FAR)
            top = jnp.max(s, axis=0)
            probs = jnp.exp2(s - top[None])
            stats[0, p, side] = top
            stats[1, p, side] = jnp.sum(probs, axis=0)
            stats[2, p, side] = jnp.sum(probs * dprobs[rows].reshape(8, 8, COLS), axis=0)

    tile_slots = 2

    @pl.loop(0, RING * LINE // tile_slots)
    def _(n):
        stats_pass(n * tile_slots, tile_slots)

    for p in range(2):
        for side in range(2):
            top = stats[0, p, side]
            best = jnp.max(top, axis=0, keepdims=True)
            weight = jnp.exp2(top - best)
            total = jnp.sum(stats[1, p, side] * weight, axis=0, keepdims=True)
            weighted = jnp.sum(stats[2, p, side] * weight, axis=0, keepdims=True)
            stats[0, p, side] = jnp.broadcast_to(best + jnp.log2(total), (8, COLS))
            stats[1, p, side] = jnp.broadcast_to(weighted / total, (8, COLS))

    @pl.loop(0, RING * LINE // tile_slots)
    def _(n):
        grad_pass(n * tile_slots, tile_slots)

    for p in range(2):
        keys, values, masks, flag = own_tile(p)
        tiles = [(True, masks[0]), (False, masks[1])]
        grads = grad_tile(p, keys, values, tiles, 0)
        rows = own_rows if p == 0 else sib_rows
        for n in range(2):
            lo, hi = grads[n][:HALF, :128], grads[n][HALF:, 128:]
            turned = flag == 1
            dextra[...] = jnp.concatenate(
                [jnp.where(turned, hi, lo), jnp.where(turned, lo, hi)], axis=0
            )
            part[mine, n, rows, :] += dextra[...]

    for p in range(2):
        unused_small, flag = pair_small(pairs[p])
        turned = flag == 1
        for h in range(GROUP_HEADS):
            both = dqacc[p, h * HALF : (h + 1) * HALF, :] * SCALE
            lo, hi = both[:, :128], both[:, 128:]
            dqout[p, :HALF, h * 128 : h * 128 + 128] = jnp.where(turned, hi, lo).astype(BF16)
            dqout[p, HALF:, h * 128 : h * 128 + 128] = jnp.where(turned, lo, hi).astype(BF16)
    dq_out = remote(dqout.at[1], dq_ref.at[:, lanes(core, wide)], brother)
    dq_out.start()
    dq_own = pltpu.make_async_copy(dqout.at[0], dq_ref.at[:, lanes(core, wide)], local_sem.at[4])
    dq_own.start()

    back = [LINE - 1, 2, 1, 0]
    far_x = [xat(2), xat(1), xat(RING - 1), x]
    c1r = [remote(s1r.at[k], r1l.at[k], right) for k in range(LINE)]
    c1l = [remote(s1l.at[k], r1r.at[k], left) for k in range(LINE)]
    c2r = [remote(s2r.at[k], r2l.at[k], right) for k in range(LINE)]
    c2l = [remote(s2l.at[k], r2r.at[k], left) for k in range(LINE)]
    c3 = [None] + [remote(s3.at[k], r3.at[k], along_z[k]) for k in range(1, LINE)]
    for k in back:
        s1r[k] = part[slot(far_x[0], zat(k)), 0].astype(BF16)
        c1r[k].start()
        s1l[k] = part[slot(far_x[0], zat(k)), 1].astype(BF16)
        c1l[k].start()
    for k in back:
        to_right, to_left = slot(far_x[1], zat(k)), slot(far_x[2], zat(k))
        s2r[k, 1] = part[to_right, 1].astype(BF16)
        s2l[k, 0] = part[to_left, 0].astype(BF16)
        c1r[k].wait_recv()
        s2r[k, 0] = (part[to_right, 0] + r1l[k].astype(F32)).astype(BF16)
        c2r[k].start()
        c1l[k].wait_recv()
        s2l[k, 1] = (part[to_left, 1] + r1r[k].astype(F32)).astype(BF16)
        c2l[k].start()
    for k in back:
        c2r[k].wait_recv()
        c2l[k].wait_recv()
        whole = part[slot(x, zat(k))] + r2l[k].astype(F32) + r2r[k].astype(F32)
        if k > 0:
            s3[k] = whole.astype(BF16)
            c3[k].start()
        else:
            part[mine] = whole
    for k in range(1, LINE):
        c3[k].wait_recv()
    for n, factor in ((0, SCALE), (1, 1.0)):
        whole = part[mine, n]
        for k in range(1, LINE):
            whole = whole + r3[k, n].astype(F32)
        fin[n] = (whole * factor).astype(BF16)
    outs = [
        remote(fin.at[0, sib_rows, :], dk_ref.at[:, lanes(core, 128)], brother),
        remote(fin.at[1, sib_rows, :], dv_ref.at[:, lanes(core, 128)], brother),
    ]
    for out in outs:
        out.start()
    keep = [
        pltpu.make_async_copy(fin.at[0, own_rows, :], dk_ref.at[:, lanes(core, 128)], local_sem.at[5]),
        pltpu.make_async_copy(fin.at[1, own_rows, :], dv_ref.at[:, lanes(core, 128)], local_sem.at[6]),
    ]
    for copy in keep:
        copy.start()
    dq_own.wait()
    for copy in keep:
        copy.wait()
    dq_out.wait_recv()
    for out in outs:
        out.wait_recv()
    for copy in (
        swaps + zsend[1:] + xright + xleft + fright + fleft + [dq_out] + c1r + c1l + c2r + c2l + c3[1:] + outs
    ):
        copy.wait_send()


COPIES = 4 + 3 + 4 * LINE + 1 + 4 * LINE + 3 + 2


def per_device(q, k, v, g, lengths, assignment):
    slots = RING * LINE
    anywhere = pl.BlockSpec(memory_space=pl.ANY)
    vmem = pl.BlockSpec(memory_space=pltpu.VMEM)
    smem = pl.BlockSpec(memory_space=pltpu.SMEM)
    half = (LINE, 256, 128)
    full = (LINE, 2, 256, 128)
    return pl.pallas_call(
        kernel,
        out_shape=(
            jax.ShapeDtypeStruct(q.shape, BF16),
            jax.ShapeDtypeStruct(k.shape, BF16),
            jax.ShapeDtypeStruct(v.shape, BF16),
        ),
        in_specs=[anywhere] * 4 + [smem] * 2,
        out_specs=(vmem, vmem, vmem),
        scratch_shapes=[
            pltpu.VMEM((slots, 2, 256, 128), BF16),
            pltpu.VMEM((2, 128, 1024), BF16),
            pltpu.VMEM((2, 128, 1024), BF16),
            pltpu.VMEM((2, COLS, 256), BF16),
            pltpu.VMEM((2, COLS, 256), BF16),
            pltpu.VMEM((3, 2, 2, 8, COLS), F32),
            pltpu.VMEM((2, 2, 8, COLS), jnp.int32),
            pltpu.VMEM((2, COLS, 256), F32),
            pltpu.VMEM((slots, 2, 256, 128), F32),
            pltpu.VMEM((128, 128), F32),
            pltpu.VMEM((2, 128, 1024), BF16),
            pltpu.VMEM((2, 256, 128), BF16),
            pltpu.VMEM(half, BF16),
            pltpu.VMEM(half, BF16),
            pltpu.VMEM(half, BF16),
            pltpu.VMEM(half, BF16),
            pltpu.VMEM(full, BF16),
            pltpu.VMEM(full, BF16),
            pltpu.VMEM(full, BF16),
            pltpu.VMEM(full, BF16),
            pltpu.VMEM(full, BF16),
            pltpu.VMEM(full, BF16),
            pltpu.SemaphoreType.DMA((7,)),
            pltpu.SemaphoreType.DMA((COPIES,)),
            pltpu.SemaphoreType.DMA((COPIES,)),
        ],
        compiler_params=pltpu.CompilerParams(
            collective_id=0, has_side_effects=True, vmem_limit_bytes=50 * 1024 * 1024
        ),
    )(q, k, v, g, lengths, assignment)


def solution(mesh):
    return jax.shard_map(
        per_device,
        mesh=mesh,
        in_specs=(
            P(("rep", "round"), "head"),
            P(("rep", "round"), "head"),
            P(("rep", "round"), "head"),
            P(("rep", "round"), "head"),
            P("rep"),
            P("rep"),
        ),
        out_specs=(
            P(("rep", "round"), "head"),
            P(("rep", "round"), "head"),
            P(("rep", "round"), "head"),
        ),
        check_vma=False,
    )
```

```python
import functools
import math

import jax
import jax.numpy as jnp
from jax import lax
from jax.experimental import pallas as pl
from jax.experimental.pallas import tpu as pltpu
from jax.sharding import PartitionSpec as P

HEAD_SIZE = 128
RWIN = 8
HALF = 64
RING = 4
LINE = 4
GROUP_HEADS = 8
COLS = GROUP_HEADS * HALF
SCALE = HEAD_SIZE**-0.5
SCALE2 = SCALE * math.log2(math.e)
FAR = -1e30
MESH = pl.DeviceIdType.MESH
F32 = jnp.float32
BF16 = jnp.bfloat16


def mul_nt(a, b):
    return lax.dot_general(a, b, (((1,), (1,)), ((), ())), preferred_element_type=F32)


def mul_nn(a, b):
    return lax.dot_general(a, b, (((1,), (0,)), ((), ())), preferred_element_type=F32)


def mul_tn(a, b):
    return lax.dot_general(a, b, (((0,), (0,)), ((), ())), preferred_element_type=F32)


def kernel(
    q_ref, k_ref, v_ref, g_ref, len_ref, asg_ref,
    dq_ref, dk_ref, dv_ref,
    kv, qin, gin, qcat, gcat, stats, start, dqacc, part, dextra, dqout, fin,
    s1r, s1l, r1l, r1r, s2r, s2l, r2l, r2r, s3, r3,
    local_sem, send_sem, recv_sem,
):
    blocks = asg_ref.shape[0]
    me = lax.axis_index("round")
    core, chip = lax.rem(me, 2), lax.div(me, 2)
    z, x = lax.rem(chip, LINE), lax.div(chip, LINE)
    sib = 1 - core

    def device(xx, zz, cc):
        return {"round": (xx * LINE + zz) * 2 + cc}

    def xat(k):
        return lax.rem(x + k, RING)

    def zat(k):
        return lax.rem(z + k, LINE)

    def remote(src, dst, target, sent, got=None):
        return pltpu.make_async_remote_copy(
            src_ref=src, dst_ref=dst, send_sem=send_sem.at[sent],
            recv_sem=recv_sem.at[sent if got is None else got],
            device_id=target, device_id_type=MESH,
        )

    def z_turn(n):
        return lax.rem(z + (1 + 2 * lax.div(z, 2)) * n, LINE)

    def turn_of(there, source):
        return lax.rem((1 + 2 * lax.div(there, 2)) * (source - there + LINE), LINE)

    right, left = device(xat(1), z, core), device(xat(RING - 1), z, core)
    brother = device(x, z, sib)

    barrier = pltpu.get_barrier_semaphore()
    peers = [brother, right, left] + [device(x, zat(k), core) for k in range(1, LINE)]
    for peer in peers:
        pl.semaphore_signal(barrier, inc=1, device_id=peer, device_id_type=MESH)
    pl.semaphore_wait(barrier, len(peers))

    def lanes(index, width):
        return pl.ds(pl.multiple_of(index * width, width), width)

    mine = z * RING + x
    own_rows, sib_rows = lanes(core, 128), lanes(sib, 128)
    wide = GROUP_HEADS * HEAD_SIZE
    swaps = [
        remote(k_ref.at[:, lanes(sib, 128)], kv.at[mine, 0, own_rows, :], brother, SWAP),
        remote(v_ref.at[:, lanes(sib, 128)], kv.at[mine, 1, own_rows, :], brother, SWAP + 1),
        remote(q_ref.at[:, lanes(sib, wide)], qin.at[1], brother, SWAP + 2),
        remote(g_ref.at[:, lanes(sib, wide)], gin.at[1], brother, SWAP + 3),
    ]
    for swap in swaps:
        swap.start()
    own = [
        pltpu.make_async_copy(k_ref.at[:, lanes(core, 128)], kv.at[mine, 0, own_rows, :], local_sem.at[0]),
        pltpu.make_async_copy(v_ref.at[:, lanes(core, 128)], kv.at[mine, 1, own_rows, :], local_sem.at[1]),
        pltpu.make_async_copy(q_ref.at[:, lanes(core, wide)], qin.at[0], local_sem.at[2]),
        pltpu.make_async_copy(g_ref.at[:, lanes(core, wide)], gin.at[0], local_sem.at[3]),
    ]
    for copy in own:
        copy.start()
    own[0].wait()
    own[1].wait()
    swaps[0].wait_recv()
    swaps[1].wait_recv()

    def slot(xx, zz):
        return zz * RING + xx

    def z_copy(k):
        there = zat(k)
        return remote(
            kv.at[mine], kv.at[mine], device(x, there, core), ZED + k, ZED + turn_of(there, z)
        )

    def z_wait(n):
        block = kv.at[slot(x, z_turn(n))]
        remote(block, block, right, ZED + n).wait_recv()

    def x_copies(n):
        block = kv.at[slot(x, z_turn(n))]
        return remote(block, block, right, XR + n), remote(block, block, left, XL + n)

    def relay_copies(n):
        block_k = kv.at[slot(xat(RING - 1), z_turn(n)), 0]
        block_v = kv.at[slot(xat(1), z_turn(n)), 1]
        return remote(block_k, block_k, right, FR + n), remote(block_v, block_v, left, FL + n)

    def start_x(n):
        for copy in x_copies(n):
            copy.start()

    def relay(n):
        for arrived, onward in zip(x_copies(n), relay_copies(n)):
            arrived.wait_recv()
            onward.start()

    start_x(0)
    for k in (1, LINE - 1, 2):
        z_copy(k).start()
    own[2].wait()
    own[3].wait()

    pairs = [2 * chip + core, 2 * chip + sib]

    def pair_small(pair):
        first, second = asg_ref[2 * pair], asg_ref[2 * pair + 1]
        return jnp.minimum(first, second), (first > second).astype(jnp.int32)

    ends, total = [], 0
    for j in range(15):
        total = total + len_ref[j]
        ends.append(total)
    lane_row = lax.rem(lax.broadcasted_iota(jnp.int32, (8, COLS), 1), HALF)
    sub_row = lax.broadcasted_iota(jnp.int32, (8, COLS), 0)
    for p in range(2):
        small, flag = pair_small(pairs[p])
        if p == 1:
            swaps[2].wait_recv()
            swaps[3].wait_recv()
        for side in range(2):
            turned = flag == 1 - side
            for h in range(GROUP_HEADS):
                to = (p, slice(h * HALF, (h + 1) * HALF), slice(side * 128, side * 128 + 128))
                cols = slice(h * 128, h * 128 + 128)
                qcat[to] = jnp.where(turned, qin[p, HALF:, cols], qin[p, :HALF, cols])
                gcat[to] = jnp.where(turned, gin[p, HALF:, cols], gin[p, :HALF, cols])
            base = (small if side == 0 else blocks - 1 - small) * HALF
            first = jnp.zeros((8, COLS), jnp.int32)
            for j in range(15 - RWIN + 1):
                first = jnp.where(base + lane_row >= ends[j + RWIN - 1], ends[j], first)
            start[p, side] = first - sub_row
        dqacc[p] = jnp.zeros((COLS, 256), F32)

    eight = 8 * lax.broadcasted_iota(jnp.int32, (8, 8, COLS), 0)
    never = 1 << 20

    def load_pairs(slots):
        small_k, large_k, small_v, large_v, firsts, flags = [], [], [], [], [], []
        for t in range(2 * len(slots)):
            at = slots[t // 2]
            pair = (lax.rem(at, RING) * LINE + lax.div(at, RING)) * 2 + t % 2
            small, flag = pair_small(pair)
            row = (t % 2) * 128
            turned = flag == 1
            for n, small_n, large_n in ((0, small_k, large_k), (1, small_v, large_v)):
                lo, hi = kv[at, n, row : row + HALF, :], kv[at, n, row + HALF : row + 128, :]
                small_n.append(jnp.where(turned, hi, lo))
                large_n.append(jnp.where(turned, lo, hi))
            firsts.append(small)
            flags.append(flag)
        return small_k, large_k, small_v, large_v, firsts, flags

    def halves(sel, small, large):
        zero = jnp.zeros_like(small)
        return jnp.concatenate(
            [jnp.where(sel, small, zero), jnp.where(sel, zero, large)], axis=1
        )

    def units(loaded, p):
        small_k, large_k, small_v, large_v, firsts, unused_flags = loaded
        mine_small, unused_flag = pair_small(pairs[p])
        tile_a, tile_b = [], []
        sels = []
        for j in firsts:
            sel = j < mine_small
            sels.append(sel)
            tile_a.append((None, start[p, 1] - j * HALF))
            begin = jnp.where(sel, start[p, 0] - j * HALF, start[p, 1] - (blocks - 1 - j) * HALF)
            tile_b.append((sel, jnp.where(j == mine_small, never, begin)))
        keys_a = jnp.concatenate(small_k, axis=0)
        values_a = jnp.concatenate(small_v, axis=0)
        keys_b = jnp.concatenate([halves(*b) for b in zip(sels, small_k, large_k)], axis=0)
        values_b = jnp.concatenate([halves(*b) for b in zip(sels, small_v, large_v)], axis=0)
        return (keys_a, values_a, tile_a, 1), (keys_b, values_b, tile_b, 0)

    def side_of(sel, ref_at):
        if sel is None:
            return ref_at(1)
        return jnp.where(sel, ref_at(0), ref_at(1))

    def products(p, keys, values, first_side):
        width = slice(128, 256) if first_side == 1 else slice(0, 256)
        return mul_nt(keys, qcat[p, :, width]), mul_nt(values, gcat[p, :, width])

    def stats_unit(p, sel, mask, scores, dprobs):
        scores = jnp.where(mask, scores * SCALE2, FAR)
        top = side_of(sel, lambda side: stats[0, p, side])
        new_top = jnp.maximum(top, jnp.max(scores, axis=0))
        rescale = jnp.exp2(top - new_top)
        probs = jnp.exp2(scores - new_top[None])
        total = side_of(sel, lambda side: stats[1, p, side]) * rescale + jnp.sum(probs, axis=0)
        weighted = side_of(sel, lambda side: stats[2, p, side]) * rescale + jnp.sum(
            probs * dprobs, axis=0
        )
        for n, new in enumerate((new_top, total, weighted)):
            if sel is None:
                stats[n, p, 1] = new
            else:
                old = stats[n, p, 1]
                stats[n, p, 0] = jnp.where(sel, new, stats[n, p, 0])
                stats[n, p, 1] = jnp.where(sel, old, new)

    def stats_pass(slots):
        loaded = load_pairs(slots)
        for p in range(2):
            for keys, values, tiles, first_side in units(loaded, p):
                scores, dprobs = products(p, keys, values, first_side)
                for t, (sel, begin) in enumerate(tiles):
                    rows = slice(t * HALF, (t + 1) * HALF)
                    stats_unit(
                        p, sel, eight >= begin[None],
                        scores[rows].reshape(8, 8, COLS), dprobs[rows].reshape(8, 8, COLS),
                    )

    def grad_unit(p, sel, mask, scores, dprobs):
        scores = jnp.where(mask, scores * SCALE2, FAR)
        log_total = side_of(sel, lambda side: stats[0, p, side])
        delta = side_of(sel, lambda side: stats[1, p, side])
        probs = jnp.exp2(scores - log_total[None])
        dscores = probs * (dprobs - delta[None])
        return (
            probs.reshape(HALF, COLS).astype(BF16),
            dscores.reshape(HALF, COLS).astype(BF16),
        )

    def grad_tile(p, keys, values, tiles, first_side):
        width = slice(128, 256) if first_side == 1 else slice(0, 256)
        scores, dprobs = products(p, keys, values, first_side)
        probs_b, dscores_b = [], []
        for t, (sel, mask) in enumerate(tiles):
            rows = slice(t * HALF, (t + 1) * HALF)
            one, two = grad_unit(
                p, sel, mask,
                scores[rows].reshape(8, 8, COLS), dprobs[rows].reshape(8, 8, COLS),
            )
            probs_b.append(one)
            dscores_b.append(two)
        probs_b = jnp.concatenate(probs_b, axis=0)
        dscores_b = jnp.concatenate(dscores_b, axis=0)
        dqacc[p, :, width] += mul_tn(dscores_b, keys)
        return mul_nn(dscores_b, qcat[p, :, width]), mul_nn(probs_b, gcat[p, :, width])

    def grad_pass(slots):
        loaded = load_pairs(slots)
        flags = loaded[-1]
        small = [0.0, 0.0]
        large = [0.0, 0.0]
        for p in range(2):
            (ka, va, ta, unused_a), (kb, vb, tb, unused_b) = units(loaded, p)
            ta = [(sel, eight >= begin[None]) for sel, begin in ta]
            masks_b = [(sel, eight >= begin[None]) for sel, begin in tb]
            grads_a = grad_tile(p, ka, va, ta, 1)
            grads_b = grad_tile(p, kb, vb, masks_b, 0)
            for n in range(2):
                small[n] = small[n] + grads_a[n]
                zero = jnp.zeros((HALF, 128), F32)
                add_small, add_large = [], []
                for t, (sel, unused_mask) in enumerate(tb):
                    rows = slice(t * HALF, (t + 1) * HALF)
                    add_small.append(jnp.where(sel, grads_b[n][rows, :128], zero))
                    add_large.append(jnp.where(sel, zero, grads_b[n][rows, 128:]))
                small[n] = small[n] + jnp.concatenate(add_small, axis=0)
                large[n] = large[n] + jnp.concatenate(add_large, axis=0)
        for n in range(2):
            for t, flag in enumerate(flags):
                rows = slice(t * HALF, (t + 1) * HALF)
                at, row = slots[t // 2], (t % 2) * 128
                turned = flag == 1
                lo, hi = small[n][rows], large[n][rows]
                part[at, n, row : row + HALF, :] = jnp.where(turned, hi, lo)
                part[at, n, row + HALF : row + 128, :] = jnp.where(turned, lo, hi)

    tri = lax.broadcasted_iota(jnp.int32, (8, 8, COLS), 1) + eight <= lax.rem(
        lax.broadcasted_iota(jnp.int32, (8, 8, COLS), 2), HALF
    )

    def own_tile(p):
        rows = own_rows if p == 0 else sib_rows
        small, flag = pair_small(pairs[p])
        turned = flag == 1
        zero = jnp.zeros((HALF, 128), BF16)

        def stack(n):
            pair = kv[mine, n, rows, :]
            lo, hi = pair[:HALF], pair[HALF:]
            return jnp.concatenate(
                [
                    jnp.concatenate([jnp.where(turned, hi, lo), zero], axis=1),
                    jnp.concatenate([zero, jnp.where(turned, lo, hi)], axis=1),
                ],
                axis=0,
            )

        masks = []
        for side in range(2):
            base = (small if side == 0 else blocks - 1 - small) * HALF
            masks.append(tri & (eight >= (start[p, side] - base)[None]))
        return stack(0), stack(1), masks, flag

    def side_const(side):
        return side == 0

    for p in range(2):
        keys, values, masks, unused_flag = own_tile(p)
        scores, dprobs = products(p, keys, values, 0)
        for side in range(2):
            rows = slice(side * HALF, (side + 1) * HALF)
            s = jnp.where(masks[side], scores[rows].reshape(8, 8, COLS) * SCALE2, FAR)
            top = jnp.max(s, axis=0)
            probs = jnp.exp2(s - top[None])
            stats[0, p, side] = top
            stats[1, p, side] = jnp.sum(probs, axis=0)
            stats[2, p, side] = jnp.sum(probs * dprobs[rows].reshape(8, 8, COLS), axis=0)

    z_wait(1)
    start_x(1)

    @pl.loop(0, LINE)
    def _(n):
        @pl.when(n < LINE - 2)
        def _():
            z_wait(n + 2)
            start_x(n + 2)

        relay(n)
        zz = z_turn(n)
        stats_pass([slot(x, zz), slot(xat(1), zz)])
        for copy in relay_copies(n):
            copy.wait_recv()
        stats_pass([slot(xat(RING - 1), zz), slot(xat(2), zz)])

    for p in range(2):
        for side in range(2):
            top = stats[0, p, side]
            best = jnp.max(top, axis=0, keepdims=True)
            weight = jnp.exp2(top - best)
            total = jnp.sum(stats[1, p, side] * weight, axis=0, keepdims=True)
            weighted = jnp.sum(stats[2, p, side] * weight, axis=0, keepdims=True)
            stats[0, p, side] = jnp.broadcast_to(best + jnp.log2(total), (8, COLS))
            stats[1, p, side] = jnp.broadcast_to(weighted / total, (8, COLS))

    def far_copies(n):
        return remote(s1r.at[n], r1l.at[n], right, C1R + n), remote(s1l.at[n], r1r.at[n], left, C1L + n)

    def near_copies(n):
        return remote(s2r.at[n], r2l.at[n], right, C2R + n), remote(s2l.at[n], r2r.at[n], left, C2L + n)

    def last_copy(n):
        there = z_turn(n)
        turn = turn_of(there, z)
        return remote(s3.at[n], r3.at[turn], device(x, there, core), C3 + n, C3 + turn)

    def send_far(n):
        far = slot(xat(2), z_turn(n))
        s1r[n] = part[far, 0].astype(BF16)
        s1l[n] = part[far, 1].astype(BF16)
        for copy in far_copies(n):
            copy.start()

    def send_near(n):
        to_right, to_left = slot(xat(1), z_turn(n)), slot(xat(RING - 1), z_turn(n))
        arrived = far_copies(n)
        onward = near_copies(n)
        s2r[n, 1] = part[to_right, 1].astype(BF16)
        s2l[n, 0] = part[to_left, 0].astype(BF16)
        arrived[0].wait_recv()
        s2r[n, 0] = (part[to_right, 0] + r1l[n].astype(F32)).astype(BF16)
        onward[0].start()
        arrived[1].wait_recv()
        s2l[n, 1] = (part[to_left, 1] + r1r[n].astype(F32)).astype(BF16)
        onward[1].start()

    def x_total(n):
        for copy in near_copies(n):
            copy.wait_recv()
        return part[slot(x, z_turn(n))] + r2l[n].astype(F32) + r2r[n].astype(F32)

    @pl.loop(0, LINE)
    def _(i):
        n = LINE - 1 - i
        zz = z_turn(n)
        grad_pass([slot(xat(2), zz), slot(xat(1), zz)])
        send_far(n)

        @pl.when(i > 0)
        def _():
            s3[n + 1] = x_total(n + 1).astype(BF16)
            last_copy(n + 1).start()

        grad_pass([slot(xat(RING - 1), zz), slot(x, zz)])
        send_near(n)

    for p in range(2):
        keys, values, masks, flag = own_tile(p)
        tiles = [(True, masks[0]), (False, masks[1])]
        grads = grad_tile(p, keys, values, tiles, 0)
        rows = own_rows if p == 0 else sib_rows
        for n in range(2):
            lo, hi = grads[n][:HALF, :128], grads[n][HALF:, 128:]
            turned = flag == 1
            dextra[...] = jnp.concatenate(
                [jnp.where(turned, hi, lo), jnp.where(turned, lo, hi)], axis=0
            )
            part[mine, n, rows, :] += dextra[...]

    for p in range(2):
        unused_small, flag = pair_small(pairs[p])
        turned = flag == 1
        for h in range(GROUP_HEADS):
            both = dqacc[p, h * HALF : (h + 1) * HALF, :] * SCALE
            lo, hi = both[:, :128], both[:, 128:]
            dqout[p, :HALF, h * 128 : h * 128 + 128] = jnp.where(turned, hi, lo).astype(BF16)
            dqout[p, HALF:, h * 128 : h * 128 + 128] = jnp.where(turned, lo, hi).astype(BF16)
    dq_out = remote(dqout.at[1], dq_ref.at[:, lanes(core, wide)], brother, DQ)
    dq_out.start()
    dq_own = pltpu.make_async_copy(dqout.at[0], dq_ref.at[:, lanes(core, wide)], local_sem.at[4])
    dq_own.start()

    part[mine] = x_total(0)
    for turn in range(1, LINE):
        remote(s3.at[0], r3.at[turn], right, C3 + turn).wait_recv()
    for n, factor in ((0, SCALE), (1, 1.0)):
        whole = part[mine, n]
        for k in range(1, LINE):
            whole = whole + r3[k, n].astype(F32)
        fin[n] = (whole * factor).astype(BF16)
    outs = [
        remote(fin.at[0, sib_rows, :], dk_ref.at[:, lanes(core, 128)], brother, OUT),
        remote(fin.at[1, sib_rows, :], dv_ref.at[:, lanes(core, 128)], brother, OUT + 1),
    ]
    for out in outs:
        out.start()
    keep = [
        pltpu.make_async_copy(fin.at[0, own_rows, :], dk_ref.at[:, lanes(core, 128)], local_sem.at[5]),
        pltpu.make_async_copy(fin.at[1, own_rows, :], dv_ref.at[:, lanes(core, 128)], local_sem.at[6]),
    ]
    for copy in keep:
        copy.start()
    dq_own.wait()
    for copy in keep:
        copy.wait()
    dq_out.wait_recv()
    for out in outs:
        out.wait_recv()
    for copy in swaps + outs + [dq_out]:
        copy.wait_send()
    for n in range(LINE):
        for copy in x_copies(n) + relay_copies(n) + far_copies(n) + near_copies(n):
            copy.wait_send()
    for n in range(1, LINE):
        z_copy(n).wait_send()
        last_copy(n).wait_send()


SWAP, OUT, DQ, ZED = 0, 4, 6, 7
XR, XL, FR, FL, C1R, C1L, C2R, C2L, C3 = range(ZED + LINE, ZED + 10 * LINE, LINE)
COPIES = ZED + 10 * LINE


def per_device(q, k, v, g, lengths, assignment):
    slots = RING * LINE
    anywhere = pl.BlockSpec(memory_space=pl.ANY)
    vmem = pl.BlockSpec(memory_space=pltpu.VMEM)
    smem = pl.BlockSpec(memory_space=pltpu.SMEM)
    half = (LINE, 256, 128)
    full = (LINE, 2, 256, 128)
    return pl.pallas_call(
        kernel,
        out_shape=(
            jax.ShapeDtypeStruct(q.shape, BF16),
            jax.ShapeDtypeStruct(k.shape, BF16),
            jax.ShapeDtypeStruct(v.shape, BF16),
        ),
        in_specs=[anywhere] * 4 + [smem] * 2,
        out_specs=(vmem, vmem, vmem),
        scratch_shapes=[
            pltpu.VMEM((slots, 2, 256, 128), BF16),
            pltpu.VMEM((2, 128, 1024), BF16),
            pltpu.VMEM((2, 128, 1024), BF16),
            pltpu.VMEM((2, COLS, 256), BF16),
            pltpu.VMEM((2, COLS, 256), BF16),
            pltpu.VMEM((3, 2, 2, 8, COLS), F32),
            pltpu.VMEM((2, 2, 8, COLS), jnp.int32),
            pltpu.VMEM((2, COLS, 256), F32),
            pltpu.VMEM((slots, 2, 256, 128), F32),
            pltpu.VMEM((128, 128), F32),
            pltpu.VMEM((2, 128, 1024), BF16),
            pltpu.VMEM((2, 256, 128), BF16),
            pltpu.VMEM(half, BF16),
            pltpu.VMEM(half, BF16),
            pltpu.VMEM(half, BF16),
            pltpu.VMEM(half, BF16),
            pltpu.VMEM(full, BF16),
            pltpu.VMEM(full, BF16),
            pltpu.VMEM(full, BF16),
            pltpu.VMEM(full, BF16),
            pltpu.VMEM(full, BF16),
            pltpu.VMEM(full, BF16),
            pltpu.SemaphoreType.DMA((7,)),
            pltpu.SemaphoreType.DMA((COPIES,)),
            pltpu.SemaphoreType.DMA((COPIES,)),
        ],
        compiler_params=pltpu.CompilerParams(
            collective_id=0, has_side_effects=True, vmem_limit_bytes=50 * 1024 * 1024
        ),
    )(q, k, v, g, lengths, assignment)


def solution(mesh):
    return jax.shard_map(
        per_device,
        mesh=mesh,
        in_specs=(
            P(("rep", "round"), "head"),
            P(("rep", "round"), "head"),
            P(("rep", "round"), "head"),
            P(("rep", "round"), "head"),
            P("rep"),
            P("rep"),
        ),
        out_specs=(
            P(("rep", "round"), "head"),
            P(("rep", "round"), "head"),
            P(("rep", "round"), "head"),
        ),
        check_vma=False,
    )
```

```python
import functools
import math

import jax
import jax.numpy as jnp
from jax import lax
from jax.experimental import pallas as pl
from jax.experimental.pallas import tpu as pltpu
from jax.sharding import PartitionSpec as P

HEAD_SIZE = 128
RWIN = 8
HALF = 64
RING = 4
LINE = 4
GROUP_HEADS = 8
COLS = GROUP_HEADS * HALF
SCALE = HEAD_SIZE**-0.5
SCALE2 = SCALE * math.log2(math.e)
FAR = -1e30
MESH = pl.DeviceIdType.MESH
F32 = jnp.float32
BF16 = jnp.bfloat16


def mul_nt(a, b):
    return lax.dot_general(a, b, (((1,), (1,)), ((), ())), preferred_element_type=F32)


def mul_nn(a, b):
    return lax.dot_general(a, b, (((1,), (0,)), ((), ())), preferred_element_type=F32)


def mul_tn(a, b):
    return lax.dot_general(a, b, (((0,), (0,)), ((), ())), preferred_element_type=F32)


def kernel(
    q_ref, k_ref, v_ref, g_ref, len_ref, asg_ref,
    dq_ref, dk_ref, dv_ref,
    kv, qin, gin, qcat, gcat, stats, start, dqacc, part, dextra, dqout, fin,
    s1r, s1l, r1l, r1r, s2r, s2l, r2l, r2r, s3, r3,
    local_sem, send_sem, recv_sem,
):
    blocks = asg_ref.shape[0]
    me = lax.axis_index("round")
    core, chip = lax.rem(me, 2), lax.div(me, 2)
    z, x = lax.rem(chip, LINE), lax.div(chip, LINE)
    sib = 1 - core

    def device(xx, zz, cc):
        return {"round": (xx * LINE + zz) * 2 + cc}

    def xat(k):
        return lax.rem(x + k, RING)

    def zat(k):
        return lax.rem(z + k, LINE)

    def remote(src, dst, target, sent, got=None):
        return pltpu.make_async_remote_copy(
            src_ref=src, dst_ref=dst, send_sem=send_sem.at[sent],
            recv_sem=recv_sem.at[sent if got is None else got],
            device_id=target, device_id_type=MESH,
        )

    def z_turn(n):
        low = jnp.minimum(z, LINE - 1 - z)
        inner = jnp.where(n == 0, 1, jnp.where(n == 1, 2, jnp.where(n == 2, 0, 3)))
        at = jnp.where(low == 0, n, inner)
        return jnp.where(z >= LINE // 2, LINE - 1 - at, at)

    right, left = device(xat(1), z, core), device(xat(RING - 1), z, core)
    brother = device(x, z, sib)

    barrier = pltpu.get_barrier_semaphore()
    peers = [brother, right, left] + [device(x, zat(k), core) for k in range(1, LINE)]
    for peer in peers:
        pl.semaphore_signal(barrier, inc=1, device_id=peer, device_id_type=MESH)
    pl.semaphore_wait(barrier, len(peers))

    def lanes(index, width):
        return pl.ds(pl.multiple_of(index * width, width), width)

    mine = z * RING + x
    own_rows, sib_rows = lanes(core, 128), lanes(sib, 128)
    wide = GROUP_HEADS * HEAD_SIZE
    swaps = [
        remote(k_ref.at[:, lanes(sib, 128)], kv.at[mine, 0, own_rows, :], brother, SWAP),
        remote(v_ref.at[:, lanes(sib, 128)], kv.at[mine, 1, own_rows, :], brother, SWAP + 1),
        remote(q_ref.at[:, lanes(sib, wide)], qin.at[1], brother, SWAP + 2),
        remote(g_ref.at[:, lanes(sib, wide)], gin.at[1], brother, SWAP + 3),
    ]
    for swap in swaps:
        swap.start()
    own = [
        pltpu.make_async_copy(k_ref.at[:, lanes(core, 128)], kv.at[mine, 0, own_rows, :], local_sem.at[0]),
        pltpu.make_async_copy(v_ref.at[:, lanes(core, 128)], kv.at[mine, 1, own_rows, :], local_sem.at[1]),
        pltpu.make_async_copy(q_ref.at[:, lanes(core, wide)], qin.at[0], local_sem.at[2]),
        pltpu.make_async_copy(g_ref.at[:, lanes(core, wide)], gin.at[0], local_sem.at[3]),
    ]
    for copy in own:
        copy.start()

    def slot(xx, zz):
        return zz * RING + xx

    up, down = device(x, jnp.minimum(z + 1, LINE - 1), core), device(x, jnp.maximum(z - 1, 0), core)

    def z_piece(zz, n, target):
        piece = kv.at[slot(x, zz), n]
        return remote(piece, piece, target, ZED + 8 * n + zz, ZED + 8 * n + zz)

    def z_onward(zz, n, do):
        piece = kv.at[slot(x, zz), n]

        @pl.when((zz <= z) & (z < LINE - 1))
        def _():
            do(remote(piece, piece, up, ZED + 8 * n + zz))

        @pl.when((zz >= z) & (z > 0))
        def _():
            do(remote(piece, piece, down, ZED + 8 * n + 4 + zz, ZED + 8 * n + zz))

    def x_piece(zz, n):
        piece = kv.at[slot(x, zz), n]
        return (
            remote(piece, piece, right, XR + 4 * n + zz),
            remote(piece, piece, left, XL + 4 * n + zz),
        )

    def relay_copies(zz):
        piece_k = kv.at[slot(xat(RING - 1), zz), 0]
        piece_v = kv.at[slot(xat(1), zz), 1]
        return remote(piece_k, piece_k, right, FR + zz), remote(piece_v, piece_v, left, FL + zz)

    def send_piece(zz, n):
        for copy in x_piece(zz, n):
            copy.start()
        z_onward(zz, n, lambda copy: copy.start())

    def z_step(turn):
        zz = z_turn(turn)
        for n in range(2):
            z_piece(zz, n, up).wait_recv()
            send_piece(zz, n)

    def relay(turn):
        zz = z_turn(turn)
        onward = relay_copies(zz)
        x_piece(zz, 0)[0].wait_recv()
        onward[0].start()
        x_piece(zz, 1)[1].wait_recv()
        onward[1].start()

    def rest_of_x(turn):
        zz = z_turn(turn)
        x_piece(zz, 0)[1].wait_recv()
        x_piece(zz, 1)[0].wait_recv()

    for n in range(2):
        own[n].wait()
        swaps[n].wait_recv()
        send_piece(z, n)

    pairs = [2 * chip + core, 2 * chip + sib]

    def pair_small(pair):
        first, second = asg_ref[2 * pair], asg_ref[2 * pair + 1]
        return jnp.minimum(first, second), (first > second).astype(jnp.int32)

    ends, total = [], 0
    for j in range(15):
        total = total + len_ref[j]
        ends.append(total)
    lane_row = lax.rem(lax.broadcasted_iota(jnp.int32, (8, COLS), 1), HALF)
    sub_row = lax.broadcasted_iota(jnp.int32, (8, COLS), 0)
    for p in range(2):
        small, flag = pair_small(pairs[p])
        if p == 0:
            own[2].wait()
            own[3].wait()
        else:
            z_step(1)
            swaps[2].wait_recv()
            swaps[3].wait_recv()
        for side in range(2):
            turned = flag == 1 - side
            for h in range(GROUP_HEADS):
                to = (p, slice(h * HALF, (h + 1) * HALF), slice(side * 128, side * 128 + 128))
                cols = slice(h * 128, h * 128 + 128)
                qcat[to] = jnp.where(turned, qin[p, HALF:, cols], qin[p, :HALF, cols])
                gcat[to] = jnp.where(turned, gin[p, HALF:, cols], gin[p, :HALF, cols])
            base = (small if side == 0 else blocks - 1 - small) * HALF
            first = jnp.zeros((8, COLS), jnp.int32)
            for j in range(15 - RWIN + 1):
                first = jnp.where(base + lane_row >= ends[j + RWIN - 1], ends[j], first)
            start[p, side] = first - sub_row
        dqacc[p] = jnp.zeros((COLS, 256), F32)

    eight = 8 * lax.broadcasted_iota(jnp.int32, (8, 8, COLS), 0)
    never = 1 << 20

    def load_pairs(slots):
        small_k, large_k, small_v, large_v, firsts, flags = [], [], [], [], [], []
        for t in range(2 * len(slots)):
            at = slots[t // 2]
            pair = (lax.rem(at, RING) * LINE + lax.div(at, RING)) * 2 + t % 2
            small, flag = pair_small(pair)
            row = (t % 2) * 128
            turned = flag == 1
            for n, small_n, large_n in ((0, small_k, large_k), (1, small_v, large_v)):
                lo, hi = kv[at, n, row : row + HALF, :], kv[at, n, row + HALF : row + 128, :]
                small_n.append(jnp.where(turned, hi, lo))
                large_n.append(jnp.where(turned, lo, hi))
            firsts.append(small)
            flags.append(flag)
        return small_k, large_k, small_v, large_v, firsts, flags

    def halves(sel, small, large):
        zero = jnp.zeros_like(small)
        return jnp.concatenate(
            [jnp.where(sel, small, zero), jnp.where(sel, zero, large)], axis=1
        )

    def units(loaded, p):
        small_k, large_k, small_v, large_v, firsts, unused_flags = loaded
        mine_small, unused_flag = pair_small(pairs[p])
        tile_a, tile_b = [], []
        sels = []
        for j in firsts:
            sel = j < mine_small
            sels.append(sel)
            tile_a.append((None, start[p, 1] - j * HALF))
            begin = jnp.where(sel, start[p, 0] - j * HALF, start[p, 1] - (blocks - 1 - j) * HALF)
            tile_b.append((sel, jnp.where(j == mine_small, never, begin)))
        keys_a = jnp.concatenate(small_k, axis=0)
        values_a = jnp.concatenate(small_v, axis=0)
        keys_b = jnp.concatenate([halves(*b) for b in zip(sels, small_k, large_k)], axis=0)
        values_b = jnp.concatenate([halves(*b) for b in zip(sels, small_v, large_v)], axis=0)
        return (keys_a, values_a, tile_a, 1), (keys_b, values_b, tile_b, 0)

    def side_of(sel, ref_at):
        if sel is None:
            return ref_at(1)
        return jnp.where(sel, ref_at(0), ref_at(1))

    def products(p, keys, values, first_side):
        width = slice(128, 256) if first_side == 1 else slice(0, 256)
        return mul_nt(keys, qcat[p, :, width]), mul_nt(values, gcat[p, :, width])

    def stats_unit(p, sel, mask, scores, dprobs):
        scores = jnp.where(mask, scores * SCALE2, FAR)
        top = side_of(sel, lambda side: stats[0, p, side])
        new_top = jnp.maximum(top, jnp.max(scores, axis=0))
        rescale = jnp.exp2(top - new_top)
        probs = jnp.exp2(scores - new_top[None])
        total = side_of(sel, lambda side: stats[1, p, side]) * rescale + jnp.sum(probs, axis=0)
        weighted = side_of(sel, lambda side: stats[2, p, side]) * rescale + jnp.sum(
            probs * dprobs, axis=0
        )
        for n, new in enumerate((new_top, total, weighted)):
            if sel is None:
                stats[n, p, 1] = new
            else:
                old = stats[n, p, 1]
                stats[n, p, 0] = jnp.where(sel, new, stats[n, p, 0])
                stats[n, p, 1] = jnp.where(sel, old, new)

    def stats_pass(slots):
        loaded = load_pairs(slots)
        for p in range(2):
            for keys, values, tiles, first_side in units(loaded, p):
                scores, dprobs = products(p, keys, values, first_side)
                for t, (sel, begin) in enumerate(tiles):
                    rows = slice(t * HALF, (t + 1) * HALF)
                    stats_unit(
                        p, sel, eight >= begin[None],
                        scores[rows].reshape(8, 8, COLS), dprobs[rows].reshape(8, 8, COLS),
                    )

    def grad_unit(p, sel, mask, scores, dprobs):
        scores = jnp.where(mask, scores * SCALE2, FAR)
        log_total = side_of(sel, lambda side: stats[0, p, side])
        delta = side_of(sel, lambda side: stats[1, p, side])
        probs = jnp.exp2(scores - log_total[None])
        dscores = probs * (dprobs - delta[None])
        return (
            probs.reshape(HALF, COLS).astype(BF16),
            dscores.reshape(HALF, COLS).astype(BF16),
        )

    def grad_tile(p, keys, values, tiles, first_side):
        width = slice(128, 256) if first_side == 1 else slice(0, 256)
        scores, dprobs = products(p, keys, values, first_side)
        probs_b, dscores_b = [], []
        for t, (sel, mask) in enumerate(tiles):
            rows = slice(t * HALF, (t + 1) * HALF)
            one, two = grad_unit(
                p, sel, mask,
                scores[rows].reshape(8, 8, COLS), dprobs[rows].reshape(8, 8, COLS),
            )
            probs_b.append(one)
            dscores_b.append(two)
        probs_b = jnp.concatenate(probs_b, axis=0)
        dscores_b = jnp.concatenate(dscores_b, axis=0)
        dqacc[p, :, width] += mul_tn(dscores_b, keys)
        return mul_nn(dscores_b, qcat[p, :, width]), mul_nn(probs_b, gcat[p, :, width])

    def grad_pass(slots):
        loaded = load_pairs(slots)
        flags = loaded[-1]
        small = [0.0, 0.0]
        large = [0.0, 0.0]
        for p in range(2):
            (ka, va, ta, unused_a), (kb, vb, tb, unused_b) = units(loaded, p)
            ta = [(sel, eight >= begin[None]) for sel, begin in ta]
            masks_b = [(sel, eight >= begin[None]) for sel, begin in tb]
            grads_a = grad_tile(p, ka, va, ta, 1)
            grads_b = grad_tile(p, kb, vb, masks_b, 0)
            for n in range(2):
                small[n] = small[n] + grads_a[n]
                zero = jnp.zeros((HALF, 128), F32)
                add_small, add_large = [], []
                for t, (sel, unused_mask) in enumerate(tb):
                    rows = slice(t * HALF, (t + 1) * HALF)
                    add_small.append(jnp.where(sel, grads_b[n][rows, :128], zero))
                    add_large.append(jnp.where(sel, zero, grads_b[n][rows, 128:]))
                small[n] = small[n] + jnp.concatenate(add_small, axis=0)
                large[n] = large[n] + jnp.concatenate(add_large, axis=0)
        for n in range(2):
            for t, flag in enumerate(flags):
                rows = slice(t * HALF, (t + 1) * HALF)
                at, row = slots[t // 2], (t % 2) * 128
                turned = flag == 1
                lo, hi = small[n][rows], large[n][rows]
                part[at, n, row : row + HALF, :] = jnp.where(turned, hi, lo)
                part[at, n, row + HALF : row + 128, :] = jnp.where(turned, lo, hi)

    tri = lax.broadcasted_iota(jnp.int32, (8, 8, COLS), 1) + eight <= lax.rem(
        lax.broadcasted_iota(jnp.int32, (8, 8, COLS), 2), HALF
    )

    def own_tile(p):
        rows = own_rows if p == 0 else sib_rows
        small, flag = pair_small(pairs[p])
        turned = flag == 1
        zero = jnp.zeros((HALF, 128), BF16)

        def stack(n):
            pair = kv[mine, n, rows, :]
            lo, hi = pair[:HALF], pair[HALF:]
            return jnp.concatenate(
                [
                    jnp.concatenate([jnp.where(turned, hi, lo), zero], axis=1),
                    jnp.concatenate([zero, jnp.where(turned, lo, hi)], axis=1),
                ],
                axis=0,
            )

        masks = []
        for side in range(2):
            base = (small if side == 0 else blocks - 1 - small) * HALF
            masks.append(tri & (eight >= (start[p, side] - base)[None]))
        return stack(0), stack(1), masks, flag

    def side_const(side):
        return side == 0

    for p in range(2):
        relay(p)
        if p == 1:
            z_step(2)
        keys, values, masks, unused_flag = own_tile(p)
        scores, dprobs = products(p, keys, values, 0)
        for side in range(2):
            rows = slice(side * HALF, (side + 1) * HALF)
            s = jnp.where(masks[side], scores[rows].reshape(8, 8, COLS) * SCALE2, FAR)
            top = jnp.max(s, axis=0)
            probs = jnp.exp2(s - top[None])
            stats[0, p, side] = top
            stats[1, p, side] = jnp.sum(probs, axis=0)
            stats[2, p, side] = jnp.sum(probs * dprobs[rows].reshape(8, 8, COLS), axis=0)

    @pl.loop(0, LINE)
    def _(turn):
        rest_of_x(turn)
        zz = z_turn(turn)
        stats_pass([slot(x, zz), slot(xat(1), zz)])

        @pl.when(turn == 0)
        def _():
            z_step(LINE - 1)

        for copy in relay_copies(zz):
            copy.wait_recv()
        stats_pass([slot(xat(RING - 1), zz), slot(xat(2), zz)])

        @pl.when(turn < LINE - 2)
        def _():
            relay(turn + 2)

    for p in range(2):
        for side in range(2):
            top = stats[0, p, side]
            best = jnp.max(top, axis=0, keepdims=True)
            weight = jnp.exp2(top - best)
            total = jnp.sum(stats[1, p, side] * weight, axis=0, keepdims=True)
            weighted = jnp.sum(stats[2, p, side] * weight, axis=0, keepdims=True)
            stats[0, p, side] = jnp.broadcast_to(best + jnp.log2(total), (8, COLS))
            stats[1, p, side] = jnp.broadcast_to(weighted / total, (8, COLS))

    def far_copies(n):
        return remote(s1r.at[n], r1l.at[n], right, C1R + n), remote(s1l.at[n], r1r.at[n], left, C1L + n)

    def near_copies(n):
        return remote(s2r.at[n], r2l.at[n], right, C2R + n), remote(s2l.at[n], r2r.at[n], left, C2L + n)

    def last_copy(n):
        return remote(s3.at[n], r3.at[z], device(x, n, core), C3 + n, C3 + z)

    def send_far(turn):
        n = z_turn(turn)
        far = slot(xat(2), n)
        s1r[n] = part[far, 0].astype(BF16)
        s1l[n] = part[far, 1].astype(BF16)
        for copy in far_copies(n):
            copy.start()

    def send_near(turn):
        n = z_turn(turn)
        to_right, to_left = slot(xat(1), n), slot(xat(RING - 1), n)
        arrived = far_copies(n)
        onward = near_copies(n)
        s2r[n, 1] = part[to_right, 1].astype(BF16)
        s2l[n, 0] = part[to_left, 0].astype(BF16)
        arrived[0].wait_recv()
        s2r[n, 0] = (part[to_right, 0] + r1l[n].astype(F32)).astype(BF16)
        onward[0].start()
        arrived[1].wait_recv()
        s2l[n, 1] = (part[to_left, 1] + r1r[n].astype(F32)).astype(BF16)
        onward[1].start()

    def x_total(n):
        for copy in near_copies(n):
            copy.wait_recv()
        return part[slot(x, n)] + r2l[n].astype(F32) + r2r[n].astype(F32)

    def send_last(turn):
        n = z_turn(turn)
        s3[n] = x_total(n).astype(BF16)
        last_copy(n).start()

    @pl.loop(0, LINE)
    def _(i):
        turn = LINE - 1 - i
        zz = z_turn(turn)
        grad_pass([slot(xat(2), zz), slot(xat(1), zz)])
        send_far(turn)

        @pl.when(i > 0)
        def _():
            send_near(turn + 1)

        grad_pass([slot(xat(RING - 1), zz), slot(x, zz)])

        @pl.when(i > 1)
        def _():
            send_last(turn + 2)

    for p in range(2):
        if p == 1:
            send_near(0)
        keys, values, masks, flag = own_tile(p)
        tiles = [(True, masks[0]), (False, masks[1])]
        grads = grad_tile(p, keys, values, tiles, 0)
        rows = own_rows if p == 0 else sib_rows
        for n in range(2):
            lo, hi = grads[n][:HALF, :128], grads[n][HALF:, 128:]
            turned = flag == 1
            dextra[...] = jnp.concatenate(
                [jnp.where(turned, hi, lo), jnp.where(turned, lo, hi)], axis=0
            )
            part[mine, n, rows, :] += dextra[...]

    send_last(1)

    for p in range(2):
        unused_small, flag = pair_small(pairs[p])
        turned = flag == 1
        for h in range(GROUP_HEADS):
            both = dqacc[p, h * HALF : (h + 1) * HALF, :] * SCALE
            lo, hi = both[:, :128], both[:, 128:]
            dqout[p, :HALF, h * 128 : h * 128 + 128] = jnp.where(turned, hi, lo).astype(BF16)
            dqout[p, HALF:, h * 128 : h * 128 + 128] = jnp.where(turned, lo, hi).astype(BF16)
    dq_out = remote(dqout.at[1], dq_ref.at[:, lanes(core, wide)], brother, DQ)
    dq_out.start()
    dq_own = pltpu.make_async_copy(dqout.at[0], dq_ref.at[:, lanes(core, wide)], local_sem.at[4])
    dq_own.start()

    part[mine] = x_total(z)
    for k in range(1, LINE):
        there = zat(k)
        remote(s3.at[0], r3.at[there], right, C3 + there).wait_recv()
    for n, factor in ((0, SCALE), (1, 1.0)):
        whole = part[mine, n]
        for k in range(1, LINE):
            whole = whole + r3[zat(k), n].astype(F32)
        fin[n] = (whole * factor).astype(BF16)
    outs = [
        remote(fin.at[0, sib_rows, :], dk_ref.at[:, lanes(core, 128)], brother, OUT),
        remote(fin.at[1, sib_rows, :], dv_ref.at[:, lanes(core, 128)], brother, OUT + 1),
    ]
    for out in outs:
        out.start()
    keep = [
        pltpu.make_async_copy(fin.at[0, own_rows, :], dk_ref.at[:, lanes(core, 128)], local_sem.at[5]),
        pltpu.make_async_copy(fin.at[1, own_rows, :], dv_ref.at[:, lanes(core, 128)], local_sem.at[6]),
    ]
    for copy in keep:
        copy.start()
    dq_own.wait()
    for copy in keep:
        copy.wait()
    dq_out.wait_recv()
    for out in outs:
        out.wait_recv()
    for copy in swaps + outs + [dq_out]:
        copy.wait_send()
    for n in range(LINE):
        for copy in x_piece(n, 0) + x_piece(n, 1) + relay_copies(n) + far_copies(n) + near_copies(n):
            copy.wait_send()
        for piece in range(2):
            z_onward(n, piece, lambda copy: copy.wait_send())
    for k in range(1, LINE):
        last_copy(zat(k)).wait_send()


SWAP, OUT, DQ, ZED, XR, XL = 0, 4, 6, 8, 24, 32
FR, FL, C1R, C1L, C2R, C2L, C3 = range(40, 40 + 7 * LINE, LINE)
COPIES = 40 + 7 * LINE


def per_device(q, k, v, g, lengths, assignment):
    slots = RING * LINE
    anywhere = pl.BlockSpec(memory_space=pl.ANY)
    smem = pl.BlockSpec(memory_space=pltpu.SMEM)
    half = (LINE, 256, 128)
    full = (LINE, 2, 256, 128)
    return pl.pallas_call(
        kernel,
        out_shape=(
            jax.ShapeDtypeStruct(q.shape, BF16),
            jax.ShapeDtypeStruct(k.shape, BF16),
            jax.ShapeDtypeStruct(v.shape, BF16),
        ),
        in_specs=[anywhere] * 4 + [smem] * 2,
        out_specs=(anywhere, anywhere, anywhere),
        scratch_shapes=[
            pltpu.VMEM((slots, 2, 256, 128), BF16),
            pltpu.VMEM((2, 128, 1024), BF16),
            pltpu.VMEM((2, 128, 1024), BF16),
            pltpu.VMEM((2, COLS, 256), BF16),
            pltpu.VMEM((2, COLS, 256), BF16),
            pltpu.VMEM((3, 2, 2, 8, COLS), F32),
            pltpu.VMEM((2, 2, 8, COLS), jnp.int32),
            pltpu.VMEM((2, COLS, 256), F32),
            pltpu.VMEM((slots, 2, 256, 128), F32),
            pltpu.VMEM((128, 128), F32),
            pltpu.VMEM((2, 128, 1024), BF16),
            pltpu.VMEM((2, 256, 128), BF16),
            pltpu.VMEM(half, BF16),
            pltpu.VMEM(half, BF16),
            pltpu.VMEM(half, BF16),
            pltpu.VMEM(half, BF16),
            pltpu.VMEM(full, BF16),
            pltpu.VMEM(full, BF16),
            pltpu.VMEM(full, BF16),
            pltpu.VMEM(full, BF16),
            pltpu.VMEM(full, BF16),
            pltpu.VMEM(full, BF16),
            pltpu.SemaphoreType.DMA((7,)),
            pltpu.SemaphoreType.DMA((COPIES,)),
            pltpu.SemaphoreType.DMA((COPIES,)),
        ],
        compiler_params=pltpu.CompilerParams(
            collective_id=0, has_side_effects=True, vmem_limit_bytes=63 * 1024 * 1024
        ),
    )(q, k, v, g, lengths, assignment)


def solution(mesh):
    return jax.shard_map(
        per_device,
        mesh=mesh,
        in_specs=(
            P(("rep", "round"), "head"),
            P(("rep", "round"), "head"),
            P(("rep", "round"), "head"),
            P(("rep", "round"), "head"),
            P("rep"),
            P("rep"),
        ),
        out_specs=(
            P(("rep", "round"), "head"),
            P(("rep", "round"), "head"),
            P(("rep", "round"), "head"),
        ),
        check_vma=False,
    )
```

```python
import functools
import math

import jax
import jax.numpy as jnp
from jax import lax
from jax.experimental import pallas as pl
from jax.experimental.pallas import tpu as pltpu
from jax.sharding import PartitionSpec as P

HEAD_SIZE = 128
RWIN = 8
HALF = 64
RING = 4
LINE = 4
GROUP_HEADS = 8
COLS = GROUP_HEADS * HALF
SCALE = HEAD_SIZE**-0.5
SCALE2 = SCALE * math.log2(math.e)
FAR = -1e30
MESH = pl.DeviceIdType.MESH
F32 = jnp.float32
BF16 = jnp.bfloat16


def mul_nt(a, b):
    return lax.dot_general(a, b, (((1,), (1,)), ((), ())), preferred_element_type=F32)


def mul_nn(a, b):
    return lax.dot_general(a, b, (((1,), (0,)), ((), ())), preferred_element_type=F32)


def mul_tn(a, b):
    return lax.dot_general(a, b, (((0,), (0,)), ((), ())), preferred_element_type=F32)


def kernel(
    q_ref, k_ref, v_ref, g_ref, len_ref, asg_ref,
    dq_ref, dk_ref, dv_ref,
    kv, qin, gin, qcat, gcat, stats, start, dqacc, part, dextra, dqout, fin,
    s1r, s1l, r1l, r1r, s2r, s2l, r2l, r2r, s3, r3,
    saved, local_sem, send_sem, recv_sem,
):
    blocks = asg_ref.shape[0]
    me = lax.axis_index("round")
    core, chip = lax.rem(me, 2), lax.div(me, 2)
    z, x = lax.rem(chip, LINE), lax.div(chip, LINE)
    sib = 1 - core

    def device(xx, zz, cc):
        return {"round": (xx * LINE + zz) * 2 + cc}

    def xat(k):
        return lax.rem(x + k, RING)

    def zat(k):
        return lax.rem(z + k, LINE)

    def remote(src, dst, target, sent, got=None):
        return pltpu.make_async_remote_copy(
            src_ref=src, dst_ref=dst, send_sem=send_sem.at[sent],
            recv_sem=recv_sem.at[sent if got is None else got],
            device_id=target, device_id_type=MESH,
        )

    def z_turn(n):
        low = jnp.minimum(z, LINE - 1 - z)
        inner = jnp.where(n == 0, 1, jnp.where(n == 1, 2, jnp.where(n == 2, 0, 3)))
        at = jnp.where(low == 0, n, inner)
        return jnp.where(z >= LINE // 2, LINE - 1 - at, at)

    right, left = device(xat(1), z, core), device(xat(RING - 1), z, core)
    brother = device(x, z, sib)

    barrier = pltpu.get_barrier_semaphore()
    peers = [brother, right, left] + [device(x, zat(k), core) for k in range(1, LINE)]
    for peer in peers:
        pl.semaphore_signal(barrier, inc=1, device_id=peer, device_id_type=MESH)
    pl.semaphore_wait(barrier, len(peers))

    def lanes(index, width):
        return pl.ds(pl.multiple_of(index * width, width), width)

    mine = z * RING + x
    own_rows, sib_rows = lanes(core, 128), lanes(sib, 128)
    wide = GROUP_HEADS * HEAD_SIZE
    swaps = [
        remote(k_ref.at[:, lanes(sib, 128)], kv.at[mine, 0, own_rows, :], brother, SWAP),
        remote(v_ref.at[:, lanes(sib, 128)], kv.at[mine, 1, own_rows, :], brother, SWAP + 1),
        remote(q_ref.at[:, lanes(sib, wide)], qin.at[1], brother, SWAP + 2),
        remote(g_ref.at[:, lanes(sib, wide)], gin.at[1], brother, SWAP + 3),
    ]
    for swap in swaps:
        swap.start()
    own = [
        pltpu.make_async_copy(k_ref.at[:, lanes(core, 128)], kv.at[mine, 0, own_rows, :], local_sem.at[0]),
        pltpu.make_async_copy(v_ref.at[:, lanes(core, 128)], kv.at[mine, 1, own_rows, :], local_sem.at[1]),
        pltpu.make_async_copy(q_ref.at[:, lanes(core, wide)], qin.at[0], local_sem.at[2]),
        pltpu.make_async_copy(g_ref.at[:, lanes(core, wide)], gin.at[0], local_sem.at[3]),
    ]
    for copy in own:
        copy.start()

    def slot(xx, zz):
        return zz * RING + xx

    up, down = device(x, jnp.minimum(z + 1, LINE - 1), core), device(x, jnp.maximum(z - 1, 0), core)

    def z_piece(zz, n, target):
        piece = kv.at[slot(x, zz), n]
        return remote(piece, piece, target, ZED + 8 * n + zz, ZED + 8 * n + zz)

    def z_onward(zz, n, do):
        piece = kv.at[slot(x, zz), n]

        @pl.when((zz <= z) & (z < LINE - 1))
        def _():
            do(remote(piece, piece, up, ZED + 8 * n + zz))

        @pl.when((zz >= z) & (z > 0))
        def _():
            do(remote(piece, piece, down, ZED + 8 * n + 4 + zz, ZED + 8 * n + zz))

    def x_piece(zz, n):
        piece = kv.at[slot(x, zz), n]
        return (
            remote(piece, piece, right, XR + 4 * n + zz),
            remote(piece, piece, left, XL + 4 * n + zz),
        )

    def relay_copies(zz):
        piece_k = kv.at[slot(xat(RING - 1), zz), 0]
        piece_v = kv.at[slot(xat(1), zz), 1]
        return remote(piece_k, piece_k, right, FR + zz), remote(piece_v, piece_v, left, FL + zz)

    def send_piece(zz, n):
        for copy in x_piece(zz, n):
            copy.start()
        z_onward(zz, n, lambda copy: copy.start())

    def z_step(turn):
        zz = z_turn(turn)
        for n in range(2):
            z_piece(zz, n, up).wait_recv()
            send_piece(zz, n)

    def relay(turn):
        zz = z_turn(turn)
        onward = relay_copies(zz)
        x_piece(zz, 0)[0].wait_recv()
        onward[0].start()
        x_piece(zz, 1)[1].wait_recv()
        onward[1].start()

    def rest_of_x(turn):
        zz = z_turn(turn)
        x_piece(zz, 0)[1].wait_recv()
        x_piece(zz, 1)[0].wait_recv()

    for n in range(2):
        own[n].wait()
        swaps[n].wait_recv()
        send_piece(z, n)

    pairs = [2 * chip + core, 2 * chip + sib]

    def pair_small(pair):
        first, second = asg_ref[2 * pair], asg_ref[2 * pair + 1]
        return jnp.minimum(first, second), (first > second).astype(jnp.int32)

    ends, total = [], 0
    for j in range(15):
        total = total + len_ref[j]
        ends.append(total)
    lane_row = lax.rem(lax.broadcasted_iota(jnp.int32, (8, COLS), 1), HALF)
    sub_row = lax.broadcasted_iota(jnp.int32, (8, COLS), 0)
    for p in range(2):
        small, flag = pair_small(pairs[p])
        if p == 0:
            own[2].wait()
            own[3].wait()
        else:
            z_step(1)
            swaps[2].wait_recv()
            swaps[3].wait_recv()
        for side in range(2):
            turned = flag == 1 - side
            for h in range(GROUP_HEADS):
                to = (p, slice(h * HALF, (h + 1) * HALF), slice(side * 128, side * 128 + 128))
                cols = slice(h * 128, h * 128 + 128)
                qcat[to] = jnp.where(turned, qin[p, HALF:, cols], qin[p, :HALF, cols])
                gcat[to] = jnp.where(turned, gin[p, HALF:, cols], gin[p, :HALF, cols])
            base = (small if side == 0 else blocks - 1 - small) * HALF
            first = jnp.zeros((8, COLS), jnp.int32)
            for j in range(15 - RWIN + 1):
                first = jnp.where(base + lane_row >= ends[j + RWIN - 1], ends[j], first)
            start[p, side] = first - sub_row
        dqacc[p] = jnp.zeros((256, COLS), F32)

    eight = 8 * lax.broadcasted_iota(jnp.int32, (8, 8, COLS), 0)
    never = 1 << 20

    def load_pairs(slots):
        small_k, large_k, small_v, large_v, firsts, flags = [], [], [], [], [], []
        for t in range(2 * len(slots)):
            at = slots[t // 2]
            pair = (lax.rem(at, RING) * LINE + lax.div(at, RING)) * 2 + t % 2
            small, flag = pair_small(pair)
            row = (t % 2) * 128
            turned = flag == 1
            for n, small_n, large_n in ((0, small_k, large_k), (1, small_v, large_v)):
                lo, hi = kv[at, n, row : row + HALF, :], kv[at, n, row + HALF : row + 128, :]
                small_n.append(jnp.where(turned, hi, lo))
                large_n.append(jnp.where(turned, lo, hi))
            firsts.append(small)
            flags.append(flag)
        return small_k, large_k, small_v, large_v, firsts, flags

    def halves(sel, small, large):
        zero = jnp.zeros_like(small)
        return jnp.concatenate(
            [jnp.where(sel, small, zero), jnp.where(sel, zero, large)], axis=1
        )

    def units(loaded, p):
        small_k, large_k, small_v, large_v, firsts, unused_flags = loaded
        mine_small, unused_flag = pair_small(pairs[p])
        tile_a, tile_b = [], []
        sels = []
        for j in firsts:
            sel = j < mine_small
            sels.append(sel)
            tile_a.append((None, start[p, 1] - j * HALF))
            begin = jnp.where(sel, start[p, 0] - j * HALF, start[p, 1] - (blocks - 1 - j) * HALF)
            tile_b.append((sel, jnp.where(j == mine_small, never, begin)))
        keys_a = jnp.concatenate(small_k, axis=0)
        values_a = jnp.concatenate(small_v, axis=0)
        keys_b = jnp.concatenate([halves(*b) for b in zip(sels, small_k, large_k)], axis=0)
        values_b = jnp.concatenate([halves(*b) for b in zip(sels, small_v, large_v)], axis=0)
        return (keys_a, values_a, tile_a, 1), (keys_b, values_b, tile_b, 0)

    def side_of(sel, ref_at):
        if sel is None:
            return ref_at(1)
        return jnp.where(sel, ref_at(0), ref_at(1))

    def products(p, keys, values, first_side):
        width = slice(128, 256) if first_side == 1 else slice(0, 256)
        return mul_nt(keys, qcat[p, :, width]), mul_nt(values, gcat[p, :, width])

    def stats_unit(p, sel, scores, dprobs):
        top = side_of(sel, lambda side: stats[0, p, side])
        new_top = jnp.maximum(top, jnp.max(scores, axis=0))
        rescale = jnp.exp2(top - new_top)
        probs = jnp.exp2(scores - new_top[None])
        total = side_of(sel, lambda side: stats[1, p, side]) * rescale + jnp.sum(probs, axis=0)
        weighted = side_of(sel, lambda side: stats[2, p, side]) * rescale + jnp.sum(
            probs * dprobs, axis=0
        )
        for n, new in enumerate((new_top, total, weighted)):
            if sel is None:
                stats[n, p, 1] = new
            else:
                old = stats[n, p, 1]
                stats[n, p, 0] = jnp.where(sel, new, stats[n, p, 0])
                stats[n, p, 1] = jnp.where(sel, old, new)

    def stats_pass(at, slots):
        loaded = load_pairs(slots)
        for p in range(2):
            for ab, (keys, values, tiles, first_side) in enumerate(units(loaded, p)):
                scores, dprobs = products(p, keys, values, first_side)
                saved[at, p, ab, 1] = dprobs
                for t, (sel, begin) in enumerate(tiles):
                    rows = slice(t * HALF, (t + 1) * HALF)
                    mask = eight >= begin[None]
                    masked = jnp.where(mask, scores[rows].reshape(8, 8, COLS) * SCALE2, FAR)
                    saved[at, p, ab, 0, rows] = masked.reshape(HALF, COLS)
                    stats_unit(p, sel, masked, dprobs[rows].reshape(8, 8, COLS))

    def grad_unit(p, sel, scores, dprobs):
        log_total = side_of(sel, lambda side: stats[0, p, side])
        delta = side_of(sel, lambda side: stats[1, p, side])
        probs = jnp.exp2(scores.reshape(8, 8, COLS) - log_total[None])
        dscores = probs * (dprobs.reshape(8, 8, COLS) - delta[None])
        return (
            probs.reshape(HALF, COLS).astype(BF16),
            dscores.reshape(HALF, COLS).astype(BF16),
        )

    def grad_tile(p, keys_t, sels, first_side, load):
        width = slice(128, 256) if first_side == 1 else slice(0, 256)
        probs_b, dscores_b = [], []
        for t, sel in enumerate(sels):
            one, two = grad_unit(p, sel, *load(slice(t * HALF, (t + 1) * HALF)))
            probs_b.append(one)
            dscores_b.append(two)
        probs_b = jnp.concatenate(probs_b, axis=0)
        dscores_b = jnp.concatenate(dscores_b, axis=0)
        dqacc[p, width, :] += mul_nn(keys_t, dscores_b)
        return mul_nn(dscores_b, qcat[p, :, width]), mul_nn(probs_b, gcat[p, :, width])

    def grad_pass(at, slots):
        small_k, large_k, unused_v, unused_w, firsts, flags = load_pairs(slots)
        small = [0.0, 0.0]
        large = [0.0, 0.0]
        small_t = jnp.concatenate(small_k, axis=0).T
        for p in range(2):
            mine_small, unused_flag = pair_small(pairs[p])
            sels = [j < mine_small for j in firsts]
            both_t = jnp.concatenate([halves(*b) for b in zip(sels, small_k, large_k)], axis=0).T

            def load(ab):
                return lambda rows: (saved[at, p, ab, 0, rows], saved[at, p, ab, 1, rows])

            grads_a = grad_tile(p, small_t, [None] * len(sels), 1, load(0))
            grads_b = grad_tile(p, both_t, sels, 0, load(1))
            for n in range(2):
                small[n] = small[n] + grads_a[n]
                zero = jnp.zeros((HALF, 128), F32)
                add_small, add_large = [], []
                for t, sel in enumerate(sels):
                    rows = slice(t * HALF, (t + 1) * HALF)
                    add_small.append(jnp.where(sel, grads_b[n][rows, :128], zero))
                    add_large.append(jnp.where(sel, zero, grads_b[n][rows, 128:]))
                small[n] = small[n] + jnp.concatenate(add_small, axis=0)
                large[n] = large[n] + jnp.concatenate(add_large, axis=0)
        for n in range(2):
            for t, flag in enumerate(flags):
                rows = slice(t * HALF, (t + 1) * HALF)
                at_slot, row = slots[t // 2], (t % 2) * 128
                turned = flag == 1
                lo, hi = small[n][rows], large[n][rows]
                part[at_slot, n, row : row + HALF, :] = jnp.where(turned, hi, lo)
                part[at_slot, n, row + HALF : row + 128, :] = jnp.where(turned, lo, hi)

    tri = lax.broadcasted_iota(jnp.int32, (8, 8, COLS), 1) + eight <= lax.rem(
        lax.broadcasted_iota(jnp.int32, (8, 8, COLS), 2), HALF
    )

    def own_tile(p):
        rows = own_rows if p == 0 else sib_rows
        small, flag = pair_small(pairs[p])
        turned = flag == 1
        zero = jnp.zeros((HALF, 128), BF16)

        def stack(n):
            pair = kv[mine, n, rows, :]
            lo, hi = pair[:HALF], pair[HALF:]
            return jnp.concatenate(
                [
                    jnp.concatenate([jnp.where(turned, hi, lo), zero], axis=1),
                    jnp.concatenate([zero, jnp.where(turned, lo, hi)], axis=1),
                ],
                axis=0,
            )

        masks = []
        for side in range(2):
            base = (small if side == 0 else blocks - 1 - small) * HALF
            masks.append(tri & (eight >= (start[p, side] - base)[None]))
        return stack(0), stack(1), masks, flag

    for p in range(2):
        relay(p)
        if p == 1:
            z_step(2)
        keys, values, masks, unused_flag = own_tile(p)
        scores, dprobs = products(p, keys, values, 0)
        for side in range(2):
            rows = slice(side * HALF, (side + 1) * HALF)
            s = jnp.where(masks[side], scores[rows].reshape(8, 8, COLS) * SCALE2, FAR)
            top = jnp.max(s, axis=0)
            probs = jnp.exp2(s - top[None])
            stats[0, p, side] = top
            stats[1, p, side] = jnp.sum(probs, axis=0)
            stats[2, p, side] = jnp.sum(probs * dprobs[rows].reshape(8, 8, COLS), axis=0)

    @pl.loop(0, LINE)
    def _(turn):
        rest_of_x(turn)
        zz = z_turn(turn)
        stats_pass(2 * zz + 1, [slot(xat(RING - 1), zz), slot(x, zz)])

        @pl.when(turn == 0)
        def _():
            z_step(LINE - 1)

        for copy in relay_copies(zz):
            copy.wait_recv()
        stats_pass(2 * zz, [slot(xat(2), zz), slot(xat(1), zz)])

        @pl.when(turn < LINE - 2)
        def _():
            relay(turn + 2)

    for p in range(2):
        for side in range(2):
            top = stats[0, p, side]
            best = jnp.max(top, axis=0, keepdims=True)
            weight = jnp.exp2(top - best)
            total = jnp.sum(stats[1, p, side] * weight, axis=0, keepdims=True)
            weighted = jnp.sum(stats[2, p, side] * weight, axis=0, keepdims=True)
            stats[0, p, side] = jnp.broadcast_to(best + jnp.log2(total), (8, COLS))
            stats[1, p, side] = jnp.broadcast_to(weighted / total, (8, COLS))

    def far_copies(n):
        return remote(s1r.at[n], r1l.at[n], right, C1R + n), remote(s1l.at[n], r1r.at[n], left, C1L + n)

    def near_copies(n):
        return remote(s2r.at[n], r2l.at[n], right, C2R + n), remote(s2l.at[n], r2r.at[n], left, C2L + n)

    def last_copy(n):
        return remote(s3.at[n], r3.at[z], device(x, n, core), C3 + n, C3 + z)

    def send_far(turn):
        n = z_turn(turn)
        far = slot(xat(2), n)
        s1r[n] = part[far, 0].astype(BF16)
        s1l[n] = part[far, 1].astype(BF16)
        for copy in far_copies(n):
            copy.start()

    def send_near(turn):
        n = z_turn(turn)
        to_right, to_left = slot(xat(1), n), slot(xat(RING - 1), n)
        arrived = far_copies(n)
        onward = near_copies(n)
        s2r[n, 1] = part[to_right, 1].astype(BF16)
        s2l[n, 0] = part[to_left, 0].astype(BF16)
        arrived[0].wait_recv()
        s2r[n, 0] = (part[to_right, 0] + r1l[n].astype(F32)).astype(BF16)
        onward[0].start()
        arrived[1].wait_recv()
        s2l[n, 1] = (part[to_left, 1] + r1r[n].astype(F32)).astype(BF16)
        onward[1].start()

    def x_total(n):
        for copy in near_copies(n):
            copy.wait_recv()
        return part[slot(x, n)] + r2l[n].astype(F32) + r2r[n].astype(F32)

    def send_last(turn):
        n = z_turn(turn)
        s3[n] = x_total(n).astype(BF16)
        last_copy(n).start()

    @pl.loop(0, LINE)
    def _(i):
        turn = LINE - 1 - i
        zz = z_turn(turn)
        grad_pass(2 * zz, [slot(xat(2), zz), slot(xat(1), zz)])
        send_far(turn)

        @pl.when(i > 0)
        def _():
            send_near(turn + 1)

        grad_pass(2 * zz + 1, [slot(xat(RING - 1), zz), slot(x, zz)])

        @pl.when(i > 1)
        def _():
            send_last(turn + 2)

    for p in range(2):
        if p == 1:
            send_near(0)
        keys, values, masks, flag = own_tile(p)
        scores, dprobs = products(p, keys, values, 0)

        def load(rows):
            mask = masks[rows.start // HALF]
            return (
                jnp.where(mask, scores[rows].reshape(8, 8, COLS) * SCALE2, FAR),
                dprobs[rows],
            )

        grads = grad_tile(p, keys.T, [True, False], 0, load)
        rows = own_rows if p == 0 else sib_rows
        for n in range(2):
            lo, hi = grads[n][:HALF, :128], grads[n][HALF:, 128:]
            turned = flag == 1
            dextra[...] = jnp.concatenate(
                [jnp.where(turned, hi, lo), jnp.where(turned, lo, hi)], axis=0
            )
            part[mine, n, rows, :] += dextra[...]

    send_last(1)

    for p in range(2):
        unused_small, flag = pair_small(pairs[p])
        turned = flag == 1
        every = dqacc[p].T * SCALE
        for h in range(GROUP_HEADS):
            lo, hi = every[h * HALF : (h + 1) * HALF, :128], every[h * HALF : (h + 1) * HALF, 128:]
            dqout[p, :HALF, h * 128 : h * 128 + 128] = jnp.where(turned, hi, lo).astype(BF16)
            dqout[p, HALF:, h * 128 : h * 128 + 128] = jnp.where(turned, lo, hi).astype(BF16)
    dq_out = remote(dqout.at[1], dq_ref.at[:, lanes(core, wide)], brother, DQ)
    dq_out.start()
    dq_own = pltpu.make_async_copy(dqout.at[0], dq_ref.at[:, lanes(core, wide)], local_sem.at[4])
    dq_own.start()

    part[mine] = x_total(z)
    for k in range(1, LINE):
        there = zat(k)
        remote(s3.at[0], r3.at[there], right, C3 + there).wait_recv()
    for n, factor in ((0, SCALE), (1, 1.0)):
        whole = part[mine, n]
        for k in range(1, LINE):
            whole = whole + r3[zat(k), n].astype(F32)
        fin[n] = (whole * factor).astype(BF16)
    outs = [
        remote(fin.at[0, sib_rows, :], dk_ref.at[:, lanes(core, 128)], brother, OUT),
        remote(fin.at[1, sib_rows, :], dv_ref.at[:, lanes(core, 128)], brother, OUT + 1),
    ]
    for out in outs:
        out.start()
    keep = [
        pltpu.make_async_copy(fin.at[0, own_rows, :], dk_ref.at[:, lanes(core, 128)], local_sem.at[5]),
        pltpu.make_async_copy(fin.at[1, own_rows, :], dv_ref.at[:, lanes(core, 128)], local_sem.at[6]),
    ]
    for copy in keep:
        copy.start()
    dq_own.wait()
    for copy in keep:
        copy.wait()
    dq_out.wait_recv()
    for out in outs:
        out.wait_recv()
    for copy in swaps + outs + [dq_out]:
        copy.wait_send()
    for n in range(LINE):
        for copy in x_piece(n, 0) + x_piece(n, 1) + relay_copies(n) + far_copies(n) + near_copies(n):
            copy.wait_send()
        for piece in range(2):
            z_onward(n, piece, lambda copy: copy.wait_send())
    for k in range(1, LINE):
        last_copy(zat(k)).wait_send()


SWAP, OUT, DQ, ZED, XR, XL = 0, 4, 6, 8, 24, 32
FR, FL, C1R, C1L, C2R, C2L, C3 = range(40, 40 + 7 * LINE, LINE)
COPIES = 40 + 7 * LINE


def per_device(q, k, v, g, lengths, assignment):
    slots = RING * LINE
    anywhere = pl.BlockSpec(memory_space=pl.ANY)
    smem = pl.BlockSpec(memory_space=pltpu.SMEM)
    half = (LINE, 256, 128)
    full = (LINE, 2, 256, 128)
    return pl.pallas_call(
        kernel,
        out_shape=(
            jax.ShapeDtypeStruct(q.shape, BF16),
            jax.ShapeDtypeStruct(k.shape, BF16),
            jax.ShapeDtypeStruct(v.shape, BF16),
        ),
        in_specs=[anywhere] * 4 + [smem] * 2,
        out_specs=(anywhere, anywhere, anywhere),
        scratch_shapes=[
            pltpu.VMEM((slots, 2, 256, 128), BF16),
            pltpu.VMEM((2, 128, 1024), BF16),
            pltpu.VMEM((2, 128, 1024), BF16),
            pltpu.VMEM((2, COLS, 256), BF16),
            pltpu.VMEM((2, COLS, 256), BF16),
            pltpu.VMEM((3, 2, 2, 8, COLS), F32),
            pltpu.VMEM((2, 2, 8, COLS), jnp.int32),
            pltpu.VMEM((2, 256, COLS), F32),
            pltpu.VMEM((slots, 2, 256, 128), F32),
            pltpu.VMEM((128, 128), F32),
            pltpu.VMEM((2, 128, 1024), BF16),
            pltpu.VMEM((2, 256, 128), BF16),
            pltpu.VMEM(half, BF16),
            pltpu.VMEM(half, BF16),
            pltpu.VMEM(half, BF16),
            pltpu.VMEM(half, BF16),
            pltpu.VMEM(full, BF16),
            pltpu.VMEM(full, BF16),
            pltpu.VMEM(full, BF16),
            pltpu.VMEM(full, BF16),
            pltpu.VMEM(full, BF16),
            pltpu.VMEM(full, BF16),
            pltpu.VMEM((2 * LINE, 2, 2, 2, 4 * HALF, COLS), F32),
            pltpu.SemaphoreType.DMA((7,)),
            pltpu.SemaphoreType.DMA((COPIES,)),
            pltpu.SemaphoreType.DMA((COPIES,)),
        ],
        compiler_params=pltpu.CompilerParams(
            collective_id=0, has_side_effects=True, vmem_limit_bytes=63 * 1024 * 1024
        ),
    )(q, k, v, g, lengths, assignment)


def solution(mesh):
    return jax.shard_map(
        per_device,
        mesh=mesh,
        in_specs=(
            P(("rep", "round"), "head"),
            P(("rep", "round"), "head"),
            P(("rep", "round"), "head"),
            P(("rep", "round"), "head"),
            P("rep"),
            P("rep"),
        ),
        out_specs=(
            P(("rep", "round"), "head"),
            P(("rep", "round"), "head"),
            P(("rep", "round"), "head"),
        ),
        check_vma=False,
    )
```

```python
import functools
import math

import jax
import jax.numpy as jnp
from jax import lax
from jax.experimental import pallas as pl
from jax.experimental.pallas import tpu as pltpu
from jax.sharding import PartitionSpec as P

HEAD_SIZE = 128
RWIN = 8
HALF = 64
RING = 4
LINE = 4
GROUP_HEADS = 8
COLS = GROUP_HEADS * HALF
SCALE = HEAD_SIZE**-0.5
SCALE2 = SCALE * math.log2(math.e)
FAR = -1e30
MESH = pl.DeviceIdType.MESH
F32 = jnp.float32
BF16 = jnp.bfloat16


def mul_nt(a, b):
    return lax.dot_general(a, b, (((1,), (1,)), ((), ())), preferred_element_type=F32)


def mul_nn(a, b):
    return lax.dot_general(a, b, (((1,), (0,)), ((), ())), preferred_element_type=F32)


def mul_tn(a, b):
    return lax.dot_general(a, b, (((0,), (0,)), ((), ())), preferred_element_type=F32)


def kernel(
    q_ref, k_ref, v_ref, g_ref, len_ref, asg_ref,
    dq_ref, dk_ref, dv_ref,
    kv, qin, gin, qcat, gcat, stats, start, dqacc, part, dextra, dqout, fin,
    s1r, s1l, r1l, r1r, s2r, s2l, r2l, r2r, s3, r3,
    saved, local_sem, send_sem, recv_sem,
):
    blocks = asg_ref.shape[0]
    me = lax.axis_index("round")
    core, chip = lax.rem(me, 2), lax.div(me, 2)
    z, x = lax.rem(chip, LINE), lax.div(chip, LINE)
    sib = 1 - core

    def device(xx, zz, cc):
        return {"round": (xx * LINE + zz) * 2 + cc}

    def xat(k):
        return lax.rem(x + k, RING)

    def zat(k):
        return lax.rem(z + k, LINE)

    def remote(src, dst, target, sent, got=None):
        return pltpu.make_async_remote_copy(
            src_ref=src, dst_ref=dst, send_sem=send_sem.at[sent],
            recv_sem=recv_sem.at[sent if got is None else got],
            device_id=target, device_id_type=MESH,
        )

    def z_turn(n):
        low = jnp.minimum(z, LINE - 1 - z)
        inner = jnp.where(n == 0, 1, jnp.where(n == 1, 2, jnp.where(n == 2, 0, 3)))
        at = jnp.where(low == 0, n, inner)
        return jnp.where(z >= LINE // 2, LINE - 1 - at, at)

    right, left = device(xat(1), z, core), device(xat(RING - 1), z, core)
    brother = device(x, z, sib)

    barrier = pltpu.get_barrier_semaphore()
    peers = [brother, right, left] + [device(x, zat(k), core) for k in range(1, LINE)]
    for peer in peers:
        pl.semaphore_signal(barrier, inc=1, device_id=peer, device_id_type=MESH)
    pl.semaphore_wait(barrier, len(peers))

    def lanes(index, width):
        return pl.ds(pl.multiple_of(index * width, width), width)

    mine = z * RING + x
    own_rows, sib_rows = lanes(core, 128), lanes(sib, 128)
    wide = GROUP_HEADS * HEAD_SIZE
    swaps = [
        remote(k_ref.at[:, lanes(sib, 128)], kv.at[mine, core, 0], brother, SWAP),
        remote(v_ref.at[:, lanes(sib, 128)], kv.at[mine, core, 1], brother, SWAP + 1),
        remote(q_ref.at[:, lanes(sib, wide)], qin.at[1], brother, SWAP + 2),
        remote(g_ref.at[:, lanes(sib, wide)], gin.at[1], brother, SWAP + 3),
    ]
    own = [
        pltpu.make_async_copy(k_ref.at[:, lanes(core, 128)], kv.at[mine, core, 0], local_sem.at[0]),
        pltpu.make_async_copy(v_ref.at[:, lanes(core, 128)], kv.at[mine, core, 1], local_sem.at[1]),
        pltpu.make_async_copy(q_ref.at[:, lanes(core, wide)], qin.at[0], local_sem.at[2]),
        pltpu.make_async_copy(g_ref.at[:, lanes(core, wide)], gin.at[0], local_sem.at[3]),
    ]
    for copy in own[:2] + swaps + own[2:]:
        copy.start()

    def slot(xx, zz):
        return zz * RING + xx

    up, down = device(x, jnp.minimum(z + 1, LINE - 1), core), device(x, jnp.maximum(z - 1, 0), core)

    def z_piece(zz, n, target):
        piece = kv.at[slot(x, zz), n]
        return remote(piece, piece, target, ZED + 8 * n + zz, ZED + 8 * n + zz)

    def z_onward(zz, n, do):
        piece = kv.at[slot(x, zz), n]

        @pl.when((zz <= z) & (z < LINE - 1))
        def _():
            do(remote(piece, piece, up, ZED + 8 * n + zz))

        @pl.when((zz >= z) & (z > 0))
        def _():
            do(remote(piece, piece, down, ZED + 8 * n + 4 + zz, ZED + 8 * n + zz))

    def x_piece(zz, n):
        piece = kv.at[slot(x, zz), n]
        return (
            remote(piece, piece, right, XR + 4 * n + zz),
            remote(piece, piece, left, XL + 4 * n + zz),
        )

    def relay_copies(zz):
        piece_r = kv.at[slot(xat(RING - 1), zz), core]
        piece_l = kv.at[slot(xat(1), zz), sib]
        return remote(piece_r, piece_r, right, FR + zz), remote(piece_l, piece_l, left, FL + zz)

    def send_piece(zz, n):
        for copy in x_piece(zz, n):
            copy.start()
        z_onward(zz, n, lambda copy: copy.start())

    middle = (z > 0) & (z < LINE - 1)

    def z_step(turn):
        zz = z_turn(turn)
        for n in (core, sib):
            z_piece(zz, n, up).wait_recv()
            send_piece(zz, n)

    def relay(turn):
        zz = z_turn(turn)
        onward = relay_copies(zz)
        x_piece(zz, core)[0].wait_recv()
        onward[0].start()
        x_piece(zz, sib)[1].wait_recv()
        onward[1].start()

    def rest_of_x(turn):
        zz = z_turn(turn)
        x_piece(zz, core)[1].wait_recv()
        x_piece(zz, sib)[0].wait_recv()

    for copy in own[:2]:
        copy.wait()
    send_piece(z, core)
    for swap in swaps[:2]:
        swap.wait_recv()
    send_piece(z, sib)

    pairs = [2 * chip + core, 2 * chip + sib]

    def pair_small(pair):
        first, second = asg_ref[2 * pair], asg_ref[2 * pair + 1]
        return jnp.minimum(first, second), (first > second).astype(jnp.int32)

    ends, total = [], 0
    for j in range(15):
        total = total + len_ref[j]
        ends.append(total)
    lane_row = lax.rem(lax.broadcasted_iota(jnp.int32, (8, COLS), 1), HALF)
    sub_row = lax.broadcasted_iota(jnp.int32, (8, COLS), 0)
    for p in range(2):
        small, flag = pair_small(pairs[p])
        if p == 0:
            own[2].wait()
            own[3].wait()
        else:
            z_step(1)
            swaps[2].wait_recv()
            swaps[3].wait_recv()
        for side in range(2):
            turned = flag == 1 - side
            for h in range(GROUP_HEADS):
                to = (p, slice(h * HALF, (h + 1) * HALF), slice(side * 128, side * 128 + 128))
                cols = slice(h * 128, h * 128 + 128)
                qcat[to] = jnp.where(turned, qin[p, HALF:, cols], qin[p, :HALF, cols])
                gcat[to] = jnp.where(turned, gin[p, HALF:, cols], gin[p, :HALF, cols])
            base = (small if side == 0 else blocks - 1 - small) * HALF
            first = jnp.zeros((8, COLS), jnp.int32)
            for j in range(15 - RWIN + 1):
                first = jnp.where(base + lane_row >= ends[j + RWIN - 1], ends[j], first)
            start[p, side] = first - sub_row
        dqacc[p] = jnp.zeros((256, COLS), F32)

    eight = 8 * lax.broadcasted_iota(jnp.int32, (8, 8, COLS), 0)
    never = 1 << 20

    def load_pairs(slots):
        small_k, large_k, small_v, large_v, firsts, flags = [], [], [], [], [], []
        for t in range(2 * len(slots)):
            at = slots[t // 2]
            pair = (lax.rem(at, RING) * LINE + lax.div(at, RING)) * 2 + t % 2
            small, flag = pair_small(pair)
            turned = flag == 1
            for n, small_n, large_n in ((0, small_k, large_k), (1, small_v, large_v)):
                lo, hi = kv[at, t % 2, n, :HALF, :], kv[at, t % 2, n, HALF:, :]
                small_n.append(jnp.where(turned, hi, lo))
                large_n.append(jnp.where(turned, lo, hi))
            firsts.append(small)
            flags.append(flag)
        return small_k, large_k, small_v, large_v, firsts, flags

    def halves(sel, small, large):
        zero = jnp.zeros_like(small)
        return jnp.concatenate(
            [jnp.where(sel, small, zero), jnp.where(sel, zero, large)], axis=1
        )

    def units(loaded, p):
        small_k, large_k, small_v, large_v, firsts, unused_flags = loaded
        mine_small, unused_flag = pair_small(pairs[p])
        tile_a, tile_b = [], []
        sels = []
        for j in firsts:
            sel = j < mine_small
            sels.append(sel)
            tile_a.append((None, start[p, 1] - j * HALF))
            begin = jnp.where(sel, start[p, 0] - j * HALF, start[p, 1] - (blocks - 1 - j) * HALF)
            tile_b.append((sel, jnp.where(j == mine_small, never, begin)))
        keys_a = jnp.concatenate(small_k, axis=0)
        values_a = jnp.concatenate(small_v, axis=0)
        keys_b = jnp.concatenate([halves(*b) for b in zip(sels, small_k, large_k)], axis=0)
        values_b = jnp.concatenate([halves(*b) for b in zip(sels, small_v, large_v)], axis=0)
        return (keys_a, values_a, tile_a, 1), (keys_b, values_b, tile_b, 0)

    def side_of(sel, ref_at):
        if sel is None:
            return ref_at(1)
        return jnp.where(sel, ref_at(0), ref_at(1))

    def products(p, keys, values, first_side):
        width = slice(128, 256) if first_side == 1 else slice(0, 256)
        return mul_nt(keys, qcat[p, :, width]), mul_nt(values, gcat[p, :, width])

    def stats_unit(p, sel, scores, dprobs):
        top = side_of(sel, lambda side: stats[0, p, side])
        new_top = jnp.maximum(top, jnp.max(scores, axis=0))
        rescale = jnp.exp2(top - new_top)
        probs = jnp.exp2(scores - new_top[None])
        total = side_of(sel, lambda side: stats[1, p, side]) * rescale + jnp.sum(probs, axis=0)
        weighted = side_of(sel, lambda side: stats[2, p, side]) * rescale + jnp.sum(
            probs * dprobs, axis=0
        )
        for n, new in enumerate((new_top, total, weighted)):
            if sel is None:
                stats[n, p, 1] = new
            else:
                old = stats[n, p, 1]
                stats[n, p, 0] = jnp.where(sel, new, stats[n, p, 0])
                stats[n, p, 1] = jnp.where(sel, old, new)

    def stats_pass(at, slots):
        loaded = load_pairs(slots)
        for p in range(2):
            for ab, (keys, values, tiles, first_side) in enumerate(units(loaded, p)):
                scores, dprobs = products(p, keys, values, first_side)
                saved[at, p, ab, 1] = dprobs
                for t, (sel, begin) in enumerate(tiles):
                    rows = slice(t * HALF, (t + 1) * HALF)
                    mask = eight >= begin[None]
                    masked = jnp.where(mask, scores[rows].reshape(8, 8, COLS) * SCALE2, FAR)
                    saved[at, p, ab, 0, rows] = masked.reshape(HALF, COLS)
                    stats_unit(p, sel, masked, dprobs[rows].reshape(8, 8, COLS))

    def grad_unit(p, sel, scores, dprobs):
        log_total = side_of(sel, lambda side: stats[0, p, side])
        delta = side_of(sel, lambda side: stats[1, p, side])
        probs = jnp.exp2(scores.reshape(8, 8, COLS) - log_total[None])
        dscores = probs * (dprobs.reshape(8, 8, COLS) - delta[None])
        return (
            probs.reshape(HALF, COLS).astype(BF16),
            dscores.reshape(HALF, COLS).astype(BF16),
        )

    def grad_tile(p, keys_t, sels, first_side, load):
        width = slice(128, 256) if first_side == 1 else slice(0, 256)
        probs_b, dscores_b = [], []
        for t, sel in enumerate(sels):
            one, two = grad_unit(p, sel, *load(slice(t * HALF, (t + 1) * HALF)))
            probs_b.append(one)
            dscores_b.append(two)
        probs_b = jnp.concatenate(probs_b, axis=0)
        dscores_b = jnp.concatenate(dscores_b, axis=0)
        dqacc[p, width, :] += mul_nn(keys_t, dscores_b)
        return mul_nn(dscores_b, qcat[p, :, width]), mul_nn(probs_b, gcat[p, :, width])

    def grad_pass(at, slots):
        small_k, large_k, unused_v, unused_w, firsts, flags = load_pairs(slots)
        small = [0.0, 0.0]
        large = [0.0, 0.0]
        small_t = jnp.concatenate(small_k, axis=0).T
        for p in range(2):
            mine_small, unused_flag = pair_small(pairs[p])
            sels = [j < mine_small for j in firsts]
            both_t = jnp.concatenate([halves(*b) for b in zip(sels, small_k, large_k)], axis=0).T

            def load(ab):
                return lambda rows: (saved[at, p, ab, 0, rows], saved[at, p, ab, 1, rows])

            grads_a = grad_tile(p, small_t, [None] * len(sels), 1, load(0))
            grads_b = grad_tile(p, both_t, sels, 0, load(1))
            for n in range(2):
                small[n] = small[n] + grads_a[n]
                zero = jnp.zeros((HALF, 128), F32)
                add_small, add_large = [], []
                for t, sel in enumerate(sels):
                    rows = slice(t * HALF, (t + 1) * HALF)
                    add_small.append(jnp.where(sel, grads_b[n][rows, :128], zero))
                    add_large.append(jnp.where(sel, zero, grads_b[n][rows, 128:]))
                small[n] = small[n] + jnp.concatenate(add_small, axis=0)
                large[n] = large[n] + jnp.concatenate(add_large, axis=0)
        for n in range(2):
            for t, flag in enumerate(flags):
                rows = slice(t * HALF, (t + 1) * HALF)
                at_slot, row = slots[t // 2], (t % 2) * 128
                turned = flag == 1
                lo, hi = small[n][rows], large[n][rows]
                part[at_slot, n, row : row + HALF, :] = jnp.where(turned, hi, lo)
                part[at_slot, n, row + HALF : row + 128, :] = jnp.where(turned, lo, hi)

    tri = lax.broadcasted_iota(jnp.int32, (8, 8, COLS), 1) + eight <= lax.rem(
        lax.broadcasted_iota(jnp.int32, (8, 8, COLS), 2), HALF
    )

    def own_tile(p):
        owner = core if p == 0 else sib
        small, flag = pair_small(pairs[p])
        turned = flag == 1
        zero = jnp.zeros((HALF, 128), BF16)

        def stack(n):
            pair = kv[mine, owner, n]
            lo, hi = pair[:HALF], pair[HALF:]
            return jnp.concatenate(
                [
                    jnp.concatenate([jnp.where(turned, hi, lo), zero], axis=1),
                    jnp.concatenate([zero, jnp.where(turned, lo, hi)], axis=1),
                ],
                axis=0,
            )

        masks = []
        for side in range(2):
            base = (small if side == 0 else blocks - 1 - small) * HALF
            masks.append(tri & (eight >= (start[p, side] - base)[None]))
        return stack(0), stack(1), masks, flag

    for p in range(2):
        if p == 0:
            relay(0)
            z_step(2)
        else:

            @pl.when(middle)
            def _():
                z_step(LINE - 1)

            relay(1)
        keys, values, masks, unused_flag = own_tile(p)
        scores, dprobs = products(p, keys, values, 0)
        for side in range(2):
            rows = slice(side * HALF, (side + 1) * HALF)
            s = jnp.where(masks[side], scores[rows].reshape(8, 8, COLS) * SCALE2, FAR)
            top = jnp.max(s, axis=0)
            probs = jnp.exp2(s - top[None])
            stats[0, p, side] = top
            stats[1, p, side] = jnp.sum(probs, axis=0)
            stats[2, p, side] = jnp.sum(probs * dprobs[rows].reshape(8, 8, COLS), axis=0)

    @pl.loop(0, LINE)
    def _(turn):
        rest_of_x(turn)
        zz = z_turn(turn)
        stats_pass(2 * zz + 1, [slot(xat(RING - 1), zz), slot(x, zz)])

        @pl.when((turn == 0) & jnp.logical_not(middle))
        def _():
            z_step(LINE - 1)

        for copy in relay_copies(zz):
            copy.wait_recv()
        stats_pass(2 * zz, [slot(xat(2), zz), slot(xat(1), zz)])

        @pl.when(turn < LINE - 2)
        def _():
            relay(turn + 2)

    for p in range(2):
        for side in range(2):
            top = stats[0, p, side]
            best = jnp.max(top, axis=0, keepdims=True)
            weight = jnp.exp2(top - best)
            total = jnp.sum(stats[1, p, side] * weight, axis=0, keepdims=True)
            weighted = jnp.sum(stats[2, p, side] * weight, axis=0, keepdims=True)
            stats[0, p, side] = jnp.broadcast_to(best + jnp.log2(total), (8, COLS))
            stats[1, p, side] = jnp.broadcast_to(weighted / total, (8, COLS))

    def far_copies(n):
        return remote(s1r.at[n], r1l.at[n], right, C1R + n), remote(s1l.at[n], r1r.at[n], left, C1L + n)

    def near_copies(n):
        return remote(s2r.at[n], r2l.at[n], right, C2R + n), remote(s2l.at[n], r2r.at[n], left, C2L + n)

    def last_copy(n):
        return remote(s3.at[n], r3.at[z], device(x, n, core), C3 + n, C3 + z)

    def send_far(turn):
        n = z_turn(turn)
        far = slot(xat(2), n)
        s1r[n] = part[far, 0].astype(BF16)
        s1l[n] = part[far, 1].astype(BF16)
        for copy in far_copies(n):
            copy.start()

    def send_near(turn):
        n = z_turn(turn)
        to_right, to_left = slot(xat(1), n), slot(xat(RING - 1), n)
        arrived = far_copies(n)
        onward = near_copies(n)
        s2r[n, 1] = part[to_right, 1].astype(BF16)
        s2l[n, 0] = part[to_left, 0].astype(BF16)
        arrived[0].wait_recv()
        s2r[n, 0] = (part[to_right, 0] + r1l[n].astype(F32)).astype(BF16)
        onward[0].start()
        arrived[1].wait_recv()
        s2l[n, 1] = (part[to_left, 1] + r1r[n].astype(F32)).astype(BF16)
        onward[1].start()

    def x_total(n):
        for copy in near_copies(n):
            copy.wait_recv()
        return part[slot(x, n)] + r2l[n].astype(F32) + r2r[n].astype(F32)

    def send_last(turn):
        n = z_turn(turn)
        s3[n] = x_total(n).astype(BF16)
        last_copy(n).start()

    @pl.loop(0, LINE)
    def _(i):
        turn = LINE - 1 - i
        zz = z_turn(turn)
        grad_pass(2 * zz, [slot(xat(2), zz), slot(xat(1), zz)])
        send_far(turn)

        @pl.when(i > 0)
        def _():
            send_near(turn + 1)

        grad_pass(2 * zz + 1, [slot(xat(RING - 1), zz), slot(x, zz)])

        @pl.when(i > 1)
        def _():
            send_last(turn + 2)

    for p in range(2):
        if p == 1:
            send_near(0)
        keys, values, masks, flag = own_tile(p)
        scores, dprobs = products(p, keys, values, 0)

        def load(rows):
            mask = masks[rows.start // HALF]
            return (
                jnp.where(mask, scores[rows].reshape(8, 8, COLS) * SCALE2, FAR),
                dprobs[rows],
            )

        grads = grad_tile(p, keys.T, [True, False], 0, load)
        rows = own_rows if p == 0 else sib_rows
        for n in range(2):
            lo, hi = grads[n][:HALF, :128], grads[n][HALF:, 128:]
            turned = flag == 1
            dextra[...] = jnp.concatenate(
                [jnp.where(turned, hi, lo), jnp.where(turned, lo, hi)], axis=0
            )
            part[mine, n, rows, :] += dextra[...]

    send_last(1)

    for p in range(2):
        unused_small, flag = pair_small(pairs[p])
        turned = flag == 1
        every = dqacc[p].T * SCALE
        for h in range(GROUP_HEADS):
            lo, hi = every[h * HALF : (h + 1) * HALF, :128], every[h * HALF : (h + 1) * HALF, 128:]
            dqout[p, :HALF, h * 128 : h * 128 + 128] = jnp.where(turned, hi, lo).astype(BF16)
            dqout[p, HALF:, h * 128 : h * 128 + 128] = jnp.where(turned, lo, hi).astype(BF16)
    dq_out = remote(dqout.at[1], dq_ref.at[:, lanes(core, wide)], brother, DQ)
    dq_out.start()
    dq_own = pltpu.make_async_copy(dqout.at[0], dq_ref.at[:, lanes(core, wide)], local_sem.at[4])
    dq_own.start()

    part[mine] = x_total(z)
    for k in range(1, LINE):
        there = zat(k)
        remote(s3.at[0], r3.at[there], right, C3 + there).wait_recv()
    for n, factor in ((0, SCALE), (1, 1.0)):
        whole = part[mine, n]
        for k in range(1, LINE):
            whole = whole + r3[zat(k), n].astype(F32)
        fin[n] = (whole * factor).astype(BF16)
    outs = [
        remote(fin.at[0, sib_rows, :], dk_ref.at[:, lanes(core, 128)], brother, OUT),
        remote(fin.at[1, sib_rows, :], dv_ref.at[:, lanes(core, 128)], brother, OUT + 1),
    ]
    for out in outs:
        out.start()
    keep = [
        pltpu.make_async_copy(fin.at[0, own_rows, :], dk_ref.at[:, lanes(core, 128)], local_sem.at[5]),
        pltpu.make_async_copy(fin.at[1, own_rows, :], dv_ref.at[:, lanes(core, 128)], local_sem.at[6]),
    ]
    for copy in keep:
        copy.start()
    dq_own.wait()
    for copy in keep:
        copy.wait()
    dq_out.wait_recv()
    for out in outs:
        out.wait_recv()
    for copy in swaps + outs + [dq_out]:
        copy.wait_send()
    for n in range(LINE):
        for copy in x_piece(n, 0) + x_piece(n, 1) + relay_copies(n) + far_copies(n) + near_copies(n):
            copy.wait_send()
        for piece in range(2):
            z_onward(n, piece, lambda copy: copy.wait_send())
    for k in range(1, LINE):
        last_copy(zat(k)).wait_send()


SWAP, OUT, DQ, ZED, XR, XL = 0, 4, 6, 8, 24, 32
FR, FL, C1R, C1L, C2R, C2L, C3 = range(40, 40 + 7 * LINE, LINE)
COPIES = 40 + 7 * LINE


def per_device(q, k, v, g, lengths, assignment):
    slots = RING * LINE
    anywhere = pl.BlockSpec(memory_space=pl.ANY)
    smem = pl.BlockSpec(memory_space=pltpu.SMEM)
    half = (LINE, 256, 128)
    full = (LINE, 2, 256, 128)
    return pl.pallas_call(
        kernel,
        out_shape=(
            jax.ShapeDtypeStruct(q.shape, BF16),
            jax.ShapeDtypeStruct(k.shape, BF16),
            jax.ShapeDtypeStruct(v.shape, BF16),
        ),
        in_specs=[anywhere] * 4 + [smem] * 2,
        out_specs=(anywhere, anywhere, anywhere),
        scratch_shapes=[
            pltpu.VMEM((slots, 2, 2, 128, 128), BF16),
            pltpu.VMEM((2, 128, 1024), BF16),
            pltpu.VMEM((2, 128, 1024), BF16),
            pltpu.VMEM((2, COLS, 256), BF16),
            pltpu.VMEM((2, COLS, 256), BF16),
            pltpu.VMEM((3, 2, 2, 8, COLS), F32),
            pltpu.VMEM((2, 2, 8, COLS), jnp.int32),
            pltpu.VMEM((2, 256, COLS), F32),
            pltpu.VMEM((slots, 2, 256, 128), F32),
            pltpu.VMEM((128, 128), F32),
            pltpu.VMEM((2, 128, 1024), BF16),
            pltpu.VMEM((2, 256, 128), BF16),
            pltpu.VMEM(half, BF16),
            pltpu.VMEM(half, BF16),
            pltpu.VMEM(half, BF16),
            pltpu.VMEM(half, BF16),
            pltpu.VMEM(full, BF16),
            pltpu.VMEM(full, BF16),
            pltpu.VMEM(full, BF16),
            pltpu.VMEM(full, BF16),
            pltpu.VMEM(full, BF16),
            pltpu.VMEM(full, BF16),
            pltpu.VMEM((2 * LINE, 2, 2, 2, 4 * HALF, COLS), F32),
            pltpu.SemaphoreType.DMA((7,)),
            pltpu.SemaphoreType.DMA((COPIES,)),
            pltpu.SemaphoreType.DMA((COPIES,)),
        ],
        compiler_params=pltpu.CompilerParams(
            collective_id=0, has_side_effects=True, vmem_limit_bytes=63 * 1024 * 1024
        ),
    )(q, k, v, g, lengths, assignment)


def solution(mesh):
    return jax.shard_map(
        per_device,
        mesh=mesh,
        in_specs=(
            P(("rep", "round"), "head"),
            P(("rep", "round"), "head"),
            P(("rep", "round"), "head"),
            P(("rep", "round"), "head"),
            P("rep"),
            P("rep"),
        ),
        out_specs=(
            P(("rep", "round"), "head"),
            P(("rep", "round"), "head"),
            P(("rep", "round"), "head"),
        ),
        check_vma=False,
    )
```

```python
import functools
import math

import jax
import jax.numpy as jnp
from jax import lax
from jax.experimental import pallas as pl
from jax.experimental.pallas import tpu as pltpu
from jax.sharding import PartitionSpec as P

HEAD_SIZE = 128
RWIN = 8
HALF = 64
RING = 4
LINE = 4
GROUP_HEADS = 8
COLS = GROUP_HEADS * HALF
SCALE = HEAD_SIZE**-0.5
SCALE2 = SCALE * math.log2(math.e)
FAR = -1e30
MESH = pl.DeviceIdType.MESH
F32 = jnp.float32
BF16 = jnp.bfloat16


def mul_nt(a, b):
    return lax.dot_general(a, b, (((1,), (1,)), ((), ())), preferred_element_type=F32)


def mul_nn(a, b):
    return lax.dot_general(a, b, (((1,), (0,)), ((), ())), preferred_element_type=F32)


def mul_tn(a, b):
    return lax.dot_general(a, b, (((0,), (0,)), ((), ())), preferred_element_type=F32)


def kernel(
    q_ref, k_ref, v_ref, g_ref, len_ref, asg_ref,
    dq_ref, dk_ref, dv_ref,
    kv, qin, gin, qcat, gcat, stats, start, dqacc, part, dextra, dqout, fin,
    s1r, s1l, r1l, r1r, s2r, s2l, r2l, r2r, s3, r3,
    saved, local_sem, send_sem, recv_sem,
):
    blocks = asg_ref.shape[0]
    me = lax.axis_index("round")
    core, chip = lax.rem(me, 2), lax.div(me, 2)
    z, x = lax.rem(chip, LINE), lax.div(chip, LINE)
    sib = 1 - core

    def device(xx, zz, cc):
        return {"round": (xx * LINE + zz) * 2 + cc}

    def xat(k):
        return lax.rem(x + k, RING)

    def zat(k):
        return lax.rem(z + k, LINE)

    def remote(src, dst, target, sent, got=None):
        return pltpu.make_async_remote_copy(
            src_ref=src, dst_ref=dst, send_sem=send_sem.at[sent],
            recv_sem=recv_sem.at[sent if got is None else got],
            device_id=target, device_id_type=MESH,
        )

    def z_turn(n):
        low = jnp.minimum(z, LINE - 1 - z)
        inner = jnp.where(n == 0, 1, jnp.where(n == 1, 2, jnp.where(n == 2, 0, 3)))
        at = jnp.where(low == 0, n, inner)
        return jnp.where(z >= LINE // 2, LINE - 1 - at, at)

    right, left = device(xat(1), z, core), device(xat(RING - 1), z, core)
    brother = device(x, z, sib)

    barrier = pltpu.get_barrier_semaphore()
    peers = [brother, right, left] + [device(x, zat(k), core) for k in range(1, LINE)]
    for peer in peers:
        pl.semaphore_signal(barrier, inc=1, device_id=peer, device_id_type=MESH)
    pl.semaphore_wait(barrier, len(peers))

    def lanes(index, width):
        return pl.ds(pl.multiple_of(index * width, width), width)

    mine = z * RING + x
    own_rows, sib_rows = lanes(core, 128), lanes(sib, 128)
    wide = GROUP_HEADS * HEAD_SIZE
    swaps = [
        remote(k_ref.at[:, lanes(sib, 128)], kv.at[mine, core, 0], brother, SWAP),
        remote(v_ref.at[:, lanes(sib, 128)], kv.at[mine, core, 1], brother, SWAP + 1),
        remote(q_ref.at[:, lanes(sib, wide)], qin.at[1], brother, SWAP + 2),
        remote(g_ref.at[:, lanes(sib, wide)], gin.at[1], brother, SWAP + 3),
    ]
    own = [
        pltpu.make_async_copy(k_ref.at[:, lanes(core, 128)], kv.at[mine, core, 0], local_sem.at[0]),
        pltpu.make_async_copy(v_ref.at[:, lanes(core, 128)], kv.at[mine, core, 1], local_sem.at[1]),
        pltpu.make_async_copy(q_ref.at[:, lanes(core, wide)], qin.at[0], local_sem.at[2]),
        pltpu.make_async_copy(g_ref.at[:, lanes(core, wide)], gin.at[0], local_sem.at[3]),
    ]
    for copy in own[:2] + swaps + own[2:]:
        copy.start()

    def slot(xx, zz):
        return zz * RING + xx

    up, down = device(x, jnp.minimum(z + 1, LINE - 1), core), device(x, jnp.maximum(z - 1, 0), core)

    def z_piece(zz, n, target):
        piece = kv.at[slot(x, zz), n]
        return remote(piece, piece, target, ZED + 8 * n + zz, ZED + 8 * n + zz)

    def z_onward(zz, n, do):
        piece = kv.at[slot(x, zz), n]

        @pl.when((zz <= z) & (z < LINE - 1))
        def _():
            do(remote(piece, piece, up, ZED + 8 * n + zz))

        @pl.when((zz >= z) & (z > 0))
        def _():
            do(remote(piece, piece, down, ZED + 8 * n + 4 + zz, ZED + 8 * n + zz))

    def x_piece(zz, n):
        piece = kv.at[slot(x, zz), n]
        return (
            remote(piece, piece, right, XR + 4 * n + zz),
            remote(piece, piece, left, XL + 4 * n + zz),
        )

    def relay_copies(zz):
        piece_r = kv.at[slot(xat(RING - 1), zz), core]
        piece_l = kv.at[slot(xat(1), zz), sib]
        return remote(piece_r, piece_r, right, FR + zz), remote(piece_l, piece_l, left, FL + zz)

    def send_piece(zz, n):
        for copy in x_piece(zz, n):
            copy.start()
        z_onward(zz, n, lambda copy: copy.start())

    middle = (z > 0) & (z < LINE - 1)

    def z_step(turn):
        zz = z_turn(turn)
        for n in (core, sib):
            z_piece(zz, n, up).wait_recv()
            send_piece(zz, n)

    def relay(turn):
        zz = z_turn(turn)
        onward = relay_copies(zz)
        x_piece(zz, core)[0].wait_recv()
        onward[0].start()
        x_piece(zz, sib)[1].wait_recv()
        onward[1].start()

    def far_block(zz, target, k):
        block = kv.at[slot(xat(2), zz)]
        return remote(block, block, device(x, target, core), FAR_Z + k, FAR_Z)

    def far_sends(do):
        @pl.when(jnp.logical_not(middle))
        def _():
            do(far_block(z, LINE - 1 - z, 0))
            do(far_block(z, jnp.where(z == 0, 2, 1), 1))

    def rest_of_x(turn):
        zz = z_turn(turn)
        x_piece(zz, core)[1].wait_recv()
        x_piece(zz, sib)[0].wait_recv()

    for copy in own[:2]:
        copy.wait()
    send_piece(z, core)
    for swap in swaps[:2]:
        swap.wait_recv()
    send_piece(z, sib)

    pairs = [2 * chip + core, 2 * chip + sib]

    def pair_small(pair):
        first, second = asg_ref[2 * pair], asg_ref[2 * pair + 1]
        return jnp.minimum(first, second), (first > second).astype(jnp.int32)

    ends, total = [], 0
    for j in range(15):
        total = total + len_ref[j]
        ends.append(total)
    lane_row = lax.rem(lax.broadcasted_iota(jnp.int32, (8, COLS), 1), HALF)
    sub_row = lax.broadcasted_iota(jnp.int32, (8, COLS), 0)
    for p in range(2):
        small, flag = pair_small(pairs[p])
        if p == 0:
            own[2].wait()
            own[3].wait()
        else:
            z_step(1)
            swaps[2].wait_recv()
            swaps[3].wait_recv()
        for side in range(2):
            turned = flag == 1 - side
            for h in range(GROUP_HEADS):
                to = (p, slice(h * HALF, (h + 1) * HALF), slice(side * 128, side * 128 + 128))
                cols = slice(h * 128, h * 128 + 128)
                qcat[to] = jnp.where(turned, qin[p, HALF:, cols], qin[p, :HALF, cols])
                gcat[to] = jnp.where(turned, gin[p, HALF:, cols], gin[p, :HALF, cols])
            base = (small if side == 0 else blocks - 1 - small) * HALF
            first = jnp.zeros((8, COLS), jnp.int32)
            for j in range(15 - RWIN + 1):
                first = jnp.where(base + lane_row >= ends[j + RWIN - 1], ends[j], first)
            start[p, side] = first - sub_row
        dqacc[p] = jnp.zeros((256, COLS), F32)

    eight = 8 * lax.broadcasted_iota(jnp.int32, (8, 8, COLS), 0)
    never = 1 << 20

    def load_pairs(slots):
        small_k, large_k, small_v, large_v, firsts, flags = [], [], [], [], [], []
        for t in range(2 * len(slots)):
            at = slots[t // 2]
            pair = (lax.rem(at, RING) * LINE + lax.div(at, RING)) * 2 + t % 2
            small, flag = pair_small(pair)
            turned = flag == 1
            for n, small_n, large_n in ((0, small_k, large_k), (1, small_v, large_v)):
                lo, hi = kv[at, t % 2, n, :HALF, :], kv[at, t % 2, n, HALF:, :]
                small_n.append(jnp.where(turned, hi, lo))
                large_n.append(jnp.where(turned, lo, hi))
            firsts.append(small)
            flags.append(flag)
        return small_k, large_k, small_v, large_v, firsts, flags

    def halves(sel, small, large):
        zero = jnp.zeros_like(small)
        return jnp.concatenate(
            [jnp.where(sel, small, zero), jnp.where(sel, zero, large)], axis=1
        )

    def units(loaded, p):
        small_k, large_k, small_v, large_v, firsts, unused_flags = loaded
        mine_small, unused_flag = pair_small(pairs[p])
        tile_a, tile_b = [], []
        sels = []
        for j in firsts:
            sel = j < mine_small
            sels.append(sel)
            tile_a.append((None, start[p, 1] - j * HALF))
            begin = jnp.where(sel, start[p, 0] - j * HALF, start[p, 1] - (blocks - 1 - j) * HALF)
            tile_b.append((sel, jnp.where(j == mine_small, never, begin)))
        keys_a = jnp.concatenate(small_k, axis=0)
        values_a = jnp.concatenate(small_v, axis=0)
        keys_b = jnp.concatenate([halves(*b) for b in zip(sels, small_k, large_k)], axis=0)
        values_b = jnp.concatenate([halves(*b) for b in zip(sels, small_v, large_v)], axis=0)
        return (keys_a, values_a, tile_a, 1), (keys_b, values_b, tile_b, 0)

    def side_of(sel, ref_at):
        if sel is None:
            return ref_at(1)
        return jnp.where(sel, ref_at(0), ref_at(1))

    def products(p, keys, values, first_side):
        width = slice(128, 256) if first_side == 1 else slice(0, 256)
        return mul_nt(keys, qcat[p, :, width]), mul_nt(values, gcat[p, :, width])

    def stats_unit(p, sel, scores, dprobs):
        top = side_of(sel, lambda side: stats[0, p, side])
        new_top = jnp.maximum(top, jnp.max(scores, axis=0))
        rescale = jnp.exp2(top - new_top)
        probs = jnp.exp2(scores - new_top[None])
        total = side_of(sel, lambda side: stats[1, p, side]) * rescale + jnp.sum(probs, axis=0)
        weighted = side_of(sel, lambda side: stats[2, p, side]) * rescale + jnp.sum(
            probs * dprobs, axis=0
        )
        for n, new in enumerate((new_top, total, weighted)):
            if sel is None:
                stats[n, p, 1] = new
            else:
                old = stats[n, p, 1]
                stats[n, p, 0] = jnp.where(sel, new, stats[n, p, 0])
                stats[n, p, 1] = jnp.where(sel, old, new)

    def stats_pass(at, slots):
        loaded = load_pairs(slots)
        for p in range(2):
            for ab, (keys, values, tiles, first_side) in enumerate(units(loaded, p)):
                scores, dprobs = products(p, keys, values, first_side)
                saved[at, p, ab, 1] = dprobs
                for t, (sel, begin) in enumerate(tiles):
                    rows = slice(t * HALF, (t + 1) * HALF)
                    mask = eight >= begin[None]
                    masked = jnp.where(mask, scores[rows].reshape(8, 8, COLS) * SCALE2, FAR)
                    saved[at, p, ab, 0, rows] = masked.reshape(HALF, COLS)
                    stats_unit(p, sel, masked, dprobs[rows].reshape(8, 8, COLS))

    def grad_unit(p, sel, scores, dprobs):
        log_total = side_of(sel, lambda side: stats[0, p, side])
        delta = side_of(sel, lambda side: stats[1, p, side])
        probs = jnp.exp2(scores.reshape(8, 8, COLS) - log_total[None])
        dscores = probs * (dprobs.reshape(8, 8, COLS) - delta[None])
        return (
            probs.reshape(HALF, COLS).astype(BF16),
            dscores.reshape(HALF, COLS).astype(BF16),
        )

    def grad_tile(p, keys_t, sels, first_side, load):
        width = slice(128, 256) if first_side == 1 else slice(0, 256)
        probs_b, dscores_b = [], []
        for t, sel in enumerate(sels):
            one, two = grad_unit(p, sel, *load(slice(t * HALF, (t + 1) * HALF)))
            probs_b.append(one)
            dscores_b.append(two)
        probs_b = jnp.concatenate(probs_b, axis=0)
        dscores_b = jnp.concatenate(dscores_b, axis=0)
        dqacc[p, width, :] += mul_nn(keys_t, dscores_b)
        return mul_nn(dscores_b, qcat[p, :, width]), mul_nn(probs_b, gcat[p, :, width])

    def grad_pass(at, slots):
        small_k, large_k, unused_v, unused_w, firsts, flags = load_pairs(slots)
        small = [0.0, 0.0]
        large = [0.0, 0.0]
        small_t = jnp.concatenate(small_k, axis=0).T
        for p in range(2):
            mine_small, unused_flag = pair_small(pairs[p])
            sels = [j < mine_small for j in firsts]
            both_t = jnp.concatenate([halves(*b) for b in zip(sels, small_k, large_k)], axis=0).T

            def load(ab):
                return lambda rows: (saved[at, p, ab, 0, rows], saved[at, p, ab, 1, rows])

            grads_a = grad_tile(p, small_t, [None] * len(sels), 1, load(0))
            grads_b = grad_tile(p, both_t, sels, 0, load(1))
            for n in range(2):
                small[n] = small[n] + grads_a[n]
                zero = jnp.zeros((HALF, 128), F32)
                add_small, add_large = [], []
                for t, sel in enumerate(sels):
                    rows = slice(t * HALF, (t + 1) * HALF)
                    add_small.append(jnp.where(sel, grads_b[n][rows, :128], zero))
                    add_large.append(jnp.where(sel, zero, grads_b[n][rows, 128:]))
                small[n] = small[n] + jnp.concatenate(add_small, axis=0)
                large[n] = large[n] + jnp.concatenate(add_large, axis=0)
        for n in range(2):
            for t, flag in enumerate(flags):
                rows = slice(t * HALF, (t + 1) * HALF)
                at_slot, row = slots[t // 2], (t % 2) * 128
                turned = flag == 1
                lo, hi = small[n][rows], large[n][rows]
                part[at_slot, n, row : row + HALF, :] = jnp.where(turned, hi, lo)
                part[at_slot, n, row + HALF : row + 128, :] = jnp.where(turned, lo, hi)

    tri = lax.broadcasted_iota(jnp.int32, (8, 8, COLS), 1) + eight <= lax.rem(
        lax.broadcasted_iota(jnp.int32, (8, 8, COLS), 2), HALF
    )

    def own_tile(p):
        owner = core if p == 0 else sib
        small, flag = pair_small(pairs[p])
        turned = flag == 1
        zero = jnp.zeros((HALF, 128), BF16)

        def stack(n):
            pair = kv[mine, owner, n]
            lo, hi = pair[:HALF], pair[HALF:]
            return jnp.concatenate(
                [
                    jnp.concatenate([jnp.where(turned, hi, lo), zero], axis=1),
                    jnp.concatenate([zero, jnp.where(turned, lo, hi)], axis=1),
                ],
                axis=0,
            )

        masks = []
        for side in range(2):
            base = (small if side == 0 else blocks - 1 - small) * HALF
            masks.append(tri & (eight >= (start[p, side] - base)[None]))
        return stack(0), stack(1), masks, flag

    for p in range(2):
        if p == 0:
            relay(0)
            z_step(2)
        else:

            @pl.when(middle)
            def _():
                z_step(LINE - 1)

            relay(1)
        keys, values, masks, unused_flag = own_tile(p)
        scores, dprobs = products(p, keys, values, 0)
        for side in range(2):
            rows = slice(side * HALF, (side + 1) * HALF)
            s = jnp.where(masks[side], scores[rows].reshape(8, 8, COLS) * SCALE2, FAR)
            top = jnp.max(s, axis=0)
            probs = jnp.exp2(s - top[None])
            stats[0, p, side] = top
            stats[1, p, side] = jnp.sum(probs, axis=0)
            stats[2, p, side] = jnp.sum(probs * dprobs[rows].reshape(8, 8, COLS), axis=0)

    def far_tile(zz):
        return 2 * zz, [slot(xat(2), zz), slot(x, zz)]

    def near_tile(zz):
        return 2 * zz + 1, [slot(xat(RING - 1), zz), slot(xat(1), zz)]

    @pl.loop(0, LINE - 1)
    def _(turn):
        rest_of_x(turn)
        zz = z_turn(turn)
        stats_pass(*near_tile(zz))

        @pl.when((turn == 0) & jnp.logical_not(middle))
        def _():
            z_step(LINE - 1)

        for copy in relay_copies(zz):
            copy.wait_recv()

        @pl.when(turn == 0)
        def _():
            far_sends(lambda copy: copy.start())

        stats_pass(*far_tile(zz))

        @pl.when(turn == 0)
        def _():
            relay(2)

    last = z_turn(LINE - 1)
    far_block(last, z, 0).wait_recv()
    stats_pass(*far_tile(last))
    for n in range(2):
        for copy in x_piece(last, n):
            copy.wait_recv()
    stats_pass(*near_tile(last))

    for p in range(2):
        for side in range(2):
            top = stats[0, p, side]
            best = jnp.max(top, axis=0, keepdims=True)
            weight = jnp.exp2(top - best)
            total = jnp.sum(stats[1, p, side] * weight, axis=0, keepdims=True)
            weighted = jnp.sum(stats[2, p, side] * weight, axis=0, keepdims=True)
            stats[0, p, side] = jnp.broadcast_to(best + jnp.log2(total), (8, COLS))
            stats[1, p, side] = jnp.broadcast_to(weighted / total, (8, COLS))

    def far_copies(n):
        return remote(s1r.at[n], r1l.at[n], right, C1R + n), remote(s1l.at[n], r1r.at[n], left, C1L + n)

    def near_copies(n):
        return remote(s2r.at[n], r2l.at[n], right, C2R + n), remote(s2l.at[n], r2r.at[n], left, C2L + n)

    def last_copy(n):
        return remote(s3.at[n], r3.at[z], device(x, n, core), C3 + n, C3 + z)

    def send_far(turn):
        n = z_turn(turn)
        far = slot(xat(2), n)
        s1r[n] = part[far, 0].astype(BF16)
        s1l[n] = part[far, 1].astype(BF16)
        for copy in far_copies(n):
            copy.start()

    def send_near(turn):
        n = z_turn(turn)
        to_right, to_left = slot(xat(1), n), slot(xat(RING - 1), n)
        arrived = far_copies(n)
        onward = near_copies(n)
        s2r[n, 1] = part[to_right, 1].astype(BF16)
        s2l[n, 0] = part[to_left, 0].astype(BF16)
        arrived[0].wait_recv()
        s2r[n, 0] = (part[to_right, 0] + r1l[n].astype(F32)).astype(BF16)
        onward[0].start()
        arrived[1].wait_recv()
        s2l[n, 1] = (part[to_left, 1] + r1r[n].astype(F32)).astype(BF16)
        onward[1].start()

    def x_total(n):
        for copy in near_copies(n):
            copy.wait_recv()
        return part[slot(x, n)] + r2l[n].astype(F32) + r2r[n].astype(F32)

    def send_last(turn):
        n = z_turn(turn)
        s3[n] = x_total(n).astype(BF16)
        last_copy(n).start()

    @pl.loop(0, LINE)
    def _(i):
        turn = LINE - 1 - i
        zz = z_turn(turn)
        grad_pass(*far_tile(zz))
        send_far(turn)

    @pl.loop(0, LINE)
    def _(i):
        turn = LINE - 1 - i
        zz = z_turn(turn)
        grad_pass(*near_tile(zz))
        send_near(turn)

    for p in range(2):
        keys, values, masks, flag = own_tile(p)
        scores, dprobs = products(p, keys, values, 0)

        def load(rows):
            mask = masks[rows.start // HALF]
            return (
                jnp.where(mask, scores[rows].reshape(8, 8, COLS) * SCALE2, FAR),
                dprobs[rows],
            )

        grads = grad_tile(p, keys.T, [True, False], 0, load)
        rows = own_rows if p == 0 else sib_rows
        for n in range(2):
            lo, hi = grads[n][:HALF, :128], grads[n][HALF:, 128:]
            turned = flag == 1
            dextra[...] = jnp.concatenate(
                [jnp.where(turned, hi, lo), jnp.where(turned, lo, hi)], axis=0
            )
            part[mine, n, rows, :] += dextra[...]

    for p in range(2):
        unused_small, flag = pair_small(pairs[p])
        turned = flag == 1
        every = dqacc[p].T * SCALE
        for h in range(GROUP_HEADS):
            lo, hi = every[h * HALF : (h + 1) * HALF, :128], every[h * HALF : (h + 1) * HALF, 128:]
            dqout[p, :HALF, h * 128 : h * 128 + 128] = jnp.where(turned, hi, lo).astype(BF16)
            dqout[p, HALF:, h * 128 : h * 128 + 128] = jnp.where(turned, lo, hi).astype(BF16)
    dq_out = remote(dqout.at[1], dq_ref.at[core], brother, DQ)
    dq_out.start()
    dq_own = pltpu.make_async_copy(dqout.at[0], dq_ref.at[core], local_sem.at[4])
    dq_own.start()

    for turn in (3, 2, 1):
        send_last(turn)
    part[mine] = x_total(z)
    for k in range(1, LINE):
        there = zat(k)
        remote(s3.at[0], r3.at[there], right, C3 + there).wait_recv()
    for n, factor in ((0, SCALE), (1, 1.0)):
        whole = part[mine, n]
        for k in range(1, LINE):
            whole = whole + r3[zat(k), n].astype(F32)
        fin[n] = (whole * factor).astype(BF16)
    outs = [
        remote(fin.at[0, sib_rows, :], dk_ref.at[core], brother, OUT),
        remote(fin.at[1, sib_rows, :], dv_ref.at[core], brother, OUT + 1),
    ]
    for out in outs:
        out.start()
    keep = [
        pltpu.make_async_copy(fin.at[0, own_rows, :], dk_ref.at[core], local_sem.at[5]),
        pltpu.make_async_copy(fin.at[1, own_rows, :], dv_ref.at[core], local_sem.at[6]),
    ]
    for copy in keep:
        copy.start()
    dq_own.wait()
    for copy in keep:
        copy.wait()
    dq_out.wait_recv()
    for out in outs:
        out.wait_recv()
    for copy in swaps + outs + [dq_out]:
        copy.wait_send()
    for n in range(LINE):
        for copy in x_piece(n, 0) + x_piece(n, 1) + near_copies(n):
            copy.wait_send()
        for piece in range(2):
            z_onward(n, piece, lambda copy: copy.wait_send())
    for turn in (0, 1, 2):
        for copy in relay_copies(z_turn(turn)):
            copy.wait_send()
    for turn in range(LINE):
        for copy in far_copies(z_turn(turn)):
            copy.wait_send()
    far_sends(lambda copy: copy.wait_send())
    for k in range(1, LINE):
        last_copy(zat(k)).wait_send()


SWAP, OUT, DQ, ZED, XR, XL = 0, 4, 6, 8, 24, 32
FR, FL, C1R, C1L, C2R, C2L, C3 = range(40, 40 + 7 * LINE, LINE)
FAR_Z = 40 + 7 * LINE
COPIES = FAR_Z + 2


def per_device(q, k, v, g, lengths, assignment):
    slots = RING * LINE
    anywhere = pl.BlockSpec(memory_space=pl.ANY)
    smem = pl.BlockSpec(memory_space=pltpu.SMEM)
    half = (LINE, 256, 128)
    full = (LINE, 2, 256, 128)
    halves = pl.pallas_call(
        kernel,
        out_shape=(
            jax.ShapeDtypeStruct((2, 128, 1024), BF16),
            jax.ShapeDtypeStruct((2, 128, 128), BF16),
            jax.ShapeDtypeStruct((2, 128, 128), BF16),
        ),
        in_specs=[anywhere] * 4 + [smem] * 2,
        out_specs=(anywhere, anywhere, anywhere),
        scratch_shapes=[
            pltpu.VMEM((slots, 2, 2, 128, 128), BF16),
            pltpu.VMEM((2, 128, 1024), BF16),
            pltpu.VMEM((2, 128, 1024), BF16),
            pltpu.VMEM((2, COLS, 256), BF16),
            pltpu.VMEM((2, COLS, 256), BF16),
            pltpu.VMEM((3, 2, 2, 8, COLS), F32),
            pltpu.VMEM((2, 2, 8, COLS), jnp.int32),
            pltpu.VMEM((2, 256, COLS), F32),
            pltpu.VMEM((slots, 2, 256, 128), F32),
            pltpu.VMEM((128, 128), F32),
            pltpu.VMEM((2, 128, 1024), BF16),
            pltpu.VMEM((2, 256, 128), BF16),
            pltpu.VMEM(half, BF16),
            pltpu.VMEM(half, BF16),
            pltpu.VMEM(half, BF16),
            pltpu.VMEM(half, BF16),
            pltpu.VMEM(full, BF16),
            pltpu.VMEM(full, BF16),
            pltpu.VMEM(full, BF16),
            pltpu.VMEM(full, BF16),
            pltpu.VMEM(full, BF16),
            pltpu.VMEM(full, BF16),
            pltpu.VMEM((2 * LINE, 2, 2, 2, 4 * HALF, COLS), F32),
            pltpu.SemaphoreType.DMA((7,)),
            pltpu.SemaphoreType.DMA((COPIES,)),
            pltpu.SemaphoreType.DMA((COPIES,)),
        ],
        compiler_params=pltpu.CompilerParams(
            collective_id=0, has_side_effects=True, vmem_limit_bytes=63 * 1024 * 1024
        ),
    )(q, k, v, g, lengths, assignment)
    dq, dk, dv = halves
    dq = dq.transpose(1, 0, 2).reshape(q.shape)
    return dq, jnp.concatenate([dk[0], dk[1]], axis=1), jnp.concatenate([dv[0], dv[1]], axis=1)


def solution(mesh):
    return jax.shard_map(
        per_device,
        mesh=mesh,
        in_specs=(
            P(("rep", "round"), "head"),
            P(("rep", "round"), "head"),
            P(("rep", "round"), "head"),
            P(("rep", "round"), "head"),
            P("rep"),
            P("rep"),
        ),
        out_specs=(
            P(("rep", "round"), "head"),
            P(("rep", "round"), "head"),
            P(("rep", "round"), "head"),
        ),
        check_vma=False,
    )
```

```python
import functools
import math

import jax
import jax.numpy as jnp
from jax import lax
from jax.experimental import pallas as pl
from jax.experimental.pallas import tpu as pltpu
from jax.sharding import PartitionSpec as P

HEAD_SIZE = 128
RWIN = 8
HALF = 64
RING = 4
LINE = 4
GROUP_HEADS = 8
COLS = GROUP_HEADS * HALF
SCALE = HEAD_SIZE**-0.5
SCALE2 = SCALE * math.log2(math.e)
FAR = -1e30
MESH = pl.DeviceIdType.MESH
F32 = jnp.float32
BF16 = jnp.bfloat16


def mul_nt(a, b):
    return lax.dot_general(a, b, (((1,), (1,)), ((), ())), preferred_element_type=F32)


def mul_nn(a, b):
    return lax.dot_general(a, b, (((1,), (0,)), ((), ())), preferred_element_type=F32)


def mul_tn(a, b):
    return lax.dot_general(a, b, (((0,), (0,)), ((), ())), preferred_element_type=F32)


def kernel(
    q_ref, k_ref, v_ref, g_ref, len_ref, asg_ref,
    dq_ref, dk_ref, dv_ref,
    kv, qin, gin, qcat, gcat, stats, start, dqacc, part, dextra, dqout, fin,
    s1r, s1l, r1l, r1r, s2r, s2l, r2l, r2r, s3, r3,
    saved, local_sem, send_sem, recv_sem,
):
    blocks = asg_ref.shape[0]
    me = lax.axis_index("round")
    core, chip = lax.rem(me, 2), lax.div(me, 2)
    z, x = lax.rem(chip, LINE), lax.div(chip, LINE)
    sib = 1 - core

    def device(xx, zz, cc):
        return {"round": (xx * LINE + zz) * 2 + cc}

    def xat(k):
        return lax.rem(x + k, RING)

    def zat(k):
        return lax.rem(z + k, LINE)

    def remote(src, dst, target, sent, got=None):
        return pltpu.make_async_remote_copy(
            src_ref=src, dst_ref=dst, send_sem=send_sem.at[sent],
            recv_sem=recv_sem.at[sent if got is None else got],
            device_id=target, device_id_type=MESH,
        )

    def z_turn(n):
        low = jnp.minimum(z, LINE - 1 - z)
        inner = jnp.where(n == 0, 1, jnp.where(n == 1, 2, jnp.where(n == 2, 0, 3)))
        at = jnp.where(low == 0, n, inner)
        return jnp.where(z >= LINE // 2, LINE - 1 - at, at)

    right, left = device(xat(1), z, core), device(xat(RING - 1), z, core)
    brother = device(x, z, sib)

    barrier = pltpu.get_barrier_semaphore()
    peers = [brother, right, left] + [device(x, zat(k), core) for k in range(1, LINE)]
    for peer in peers:
        pl.semaphore_signal(barrier, inc=1, device_id=peer, device_id_type=MESH)
    pl.semaphore_wait(barrier, len(peers))

    def lanes(index, width):
        return pl.ds(pl.multiple_of(index * width, width), width)

    mine = z * RING + x
    own_rows, sib_rows = lanes(core, 128), lanes(sib, 128)
    wide = GROUP_HEADS * HEAD_SIZE
    swaps = [
        remote(k_ref.at[:, lanes(sib, 128)], kv.at[mine, core, 0], brother, SWAP),
        remote(v_ref.at[:, lanes(sib, 128)], kv.at[mine, core, 1], brother, SWAP + 1),
        remote(q_ref.at[:, lanes(sib, wide)], qin.at[1], brother, SWAP + 2),
        remote(g_ref.at[:, lanes(sib, wide)], gin.at[1], brother, SWAP + 3),
    ]
    own = [
        pltpu.make_async_copy(k_ref.at[:, lanes(core, 128)], kv.at[mine, core, 0], local_sem.at[0]),
        pltpu.make_async_copy(v_ref.at[:, lanes(core, 128)], kv.at[mine, core, 1], local_sem.at[1]),
        pltpu.make_async_copy(q_ref.at[:, lanes(core, wide)], qin.at[0], local_sem.at[2]),
        pltpu.make_async_copy(g_ref.at[:, lanes(core, wide)], gin.at[0], local_sem.at[3]),
    ]
    for copy in own[:2] + swaps + own[2:]:
        copy.start()

    def slot(xx, zz):
        return zz * RING + xx

    up, down = device(x, jnp.minimum(z + 1, LINE - 1), core), device(x, jnp.maximum(z - 1, 0), core)

    def z_piece(zz, n, target):
        piece = kv.at[slot(x, zz), n]
        return remote(piece, piece, target, ZED + 8 * n + zz, ZED + 8 * n + zz)

    def z_onward(zz, n, do):
        piece = kv.at[slot(x, zz), n]

        @pl.when((zz <= z) & (z < LINE - 1))
        def _():
            do(remote(piece, piece, up, ZED + 8 * n + zz))

        @pl.when((zz >= z) & (z > 0))
        def _():
            do(remote(piece, piece, down, ZED + 8 * n + 4 + zz, ZED + 8 * n + zz))

    def x_piece(zz, n):
        piece = kv.at[slot(x, zz), n]
        return (
            remote(piece, piece, right, XR + 4 * n + zz),
            remote(piece, piece, left, XL + 4 * n + zz),
        )

    def relay_copies(zz):
        piece_r = kv.at[slot(xat(RING - 1), zz), core]
        piece_l = kv.at[slot(xat(1), zz), sib]
        return remote(piece_r, piece_r, right, FR + zz), remote(piece_l, piece_l, left, FL + zz)

    def send_piece(zz, n):
        z_onward(zz, n, lambda copy: copy.start())
        for copy in x_piece(zz, n):
            copy.start()

    middle = (z > 0) & (z < LINE - 1)

    def z_step(turn):
        zz = z_turn(turn)
        for n in (core, sib):
            z_piece(zz, n, up).wait_recv()
            send_piece(zz, n)

    def relay(turn):
        zz = z_turn(turn)
        onward = relay_copies(zz)
        x_piece(zz, core)[0].wait_recv()
        onward[0].start()
        x_piece(zz, sib)[1].wait_recv()
        onward[1].start()

    def far_block(zz, target, k):
        block = kv.at[slot(xat(2), zz)]
        return remote(block, block, device(x, target, core), FAR_Z + k, FAR_Z)

    def far_sends(do):
        @pl.when(jnp.logical_not(middle))
        def _():
            do(far_block(z, LINE - 1 - z, 0))
            do(far_block(z, jnp.where(z == 0, 2, 1), 1))

    def rest_of_x(turn):
        zz = z_turn(turn)
        x_piece(zz, core)[1].wait_recv()
        x_piece(zz, sib)[0].wait_recv()

    for copy in own[:2]:
        copy.wait()
    send_piece(z, core)
    for swap in swaps[:2]:
        swap.wait_recv()
    send_piece(z, sib)

    pairs = [2 * chip + core, 2 * chip + sib]

    def pair_small(pair):
        first, second = asg_ref[2 * pair], asg_ref[2 * pair + 1]
        return jnp.minimum(first, second), (first > second).astype(jnp.int32)

    ends, total = [], 0
    for j in range(15):
        total = total + len_ref[j]
        ends.append(total)
    lane_row = lax.rem(lax.broadcasted_iota(jnp.int32, (8, COLS), 1), HALF)
    sub_row = lax.broadcasted_iota(jnp.int32, (8, COLS), 0)
    for p in range(2):
        small, flag = pair_small(pairs[p])
        if p == 0:
            own[2].wait()
            own[3].wait()
        else:
            z_step(1)
            swaps[2].wait_recv()
            swaps[3].wait_recv()
        for side in range(2):
            turned = flag == 1 - side
            for h in range(GROUP_HEADS):
                to = (p, slice(h * HALF, (h + 1) * HALF), slice(side * 128, side * 128 + 128))
                cols = slice(h * 128, h * 128 + 128)
                qcat[to] = jnp.where(turned, qin[p, HALF:, cols], qin[p, :HALF, cols])
                gcat[to] = jnp.where(turned, gin[p, HALF:, cols], gin[p, :HALF, cols])
            base = (small if side == 0 else blocks - 1 - small) * HALF
            first = jnp.zeros((8, COLS), jnp.int32)
            for j in range(15 - RWIN + 1):
                first = jnp.where(base + lane_row >= ends[j + RWIN - 1], ends[j], first)
            start[p, side] = first - sub_row
        dqacc[p] = jnp.zeros((256, COLS), F32)

    eight = 8 * lax.broadcasted_iota(jnp.int32, (8, 8, COLS), 0)
    never = 1 << 20

    def load_pairs(slots):
        small_k, large_k, small_v, large_v, firsts, flags = [], [], [], [], [], []
        for t in range(2 * len(slots)):
            at = slots[t // 2]
            pair = (lax.rem(at, RING) * LINE + lax.div(at, RING)) * 2 + t % 2
            small, flag = pair_small(pair)
            turned = flag == 1
            for n, small_n, large_n in ((0, small_k, large_k), (1, small_v, large_v)):
                lo, hi = kv[at, t % 2, n, :HALF, :], kv[at, t % 2, n, HALF:, :]
                small_n.append(jnp.where(turned, hi, lo))
                large_n.append(jnp.where(turned, lo, hi))
            firsts.append(small)
            flags.append(flag)
        return small_k, large_k, small_v, large_v, firsts, flags

    def halves(sel, small, large):
        zero = jnp.zeros_like(small)
        return jnp.concatenate(
            [jnp.where(sel, small, zero), jnp.where(sel, zero, large)], axis=1
        )

    def units(loaded, p):
        small_k, large_k, small_v, large_v, firsts, unused_flags = loaded
        mine_small, unused_flag = pair_small(pairs[p])
        tile_a, tile_b = [], []
        sels = []
        for j in firsts:
            sel = j < mine_small
            sels.append(sel)
            tile_a.append((None, start[p, 1] - j * HALF))
            begin = jnp.where(sel, start[p, 0] - j * HALF, start[p, 1] - (blocks - 1 - j) * HALF)
            tile_b.append((sel, jnp.where(j == mine_small, never, begin)))
        keys_a = jnp.concatenate(small_k, axis=0)
        values_a = jnp.concatenate(small_v, axis=0)
        keys_b = jnp.concatenate([halves(*b) for b in zip(sels, small_k, large_k)], axis=0)
        values_b = jnp.concatenate([halves(*b) for b in zip(sels, small_v, large_v)], axis=0)
        return (keys_a, values_a, tile_a, 1), (keys_b, values_b, tile_b, 0)

    def side_of(sel, ref_at):
        if sel is None:
            return ref_at(1)
        return jnp.where(sel, ref_at(0), ref_at(1))

    def products(p, keys, values, first_side):
        width = slice(128, 256) if first_side == 1 else slice(0, 256)
        return mul_nt(keys, qcat[p, :, width]), mul_nt(values, gcat[p, :, width])

    def stats_unit(p, sel, scores, dprobs):
        top = side_of(sel, lambda side: stats[0, p, side])
        new_top = jnp.maximum(top, jnp.max(scores, axis=0))
        rescale = jnp.exp2(top - new_top)
        probs = jnp.exp2(scores - new_top[None])
        total = side_of(sel, lambda side: stats[1, p, side]) * rescale + jnp.sum(probs, axis=0)
        weighted = side_of(sel, lambda side: stats[2, p, side]) * rescale + jnp.sum(
            probs * dprobs, axis=0
        )
        for n, new in enumerate((new_top, total, weighted)):
            if sel is None:
                stats[n, p, 1] = new
            else:
                old = stats[n, p, 1]
                stats[n, p, 0] = jnp.where(sel, new, stats[n, p, 0])
                stats[n, p, 1] = jnp.where(sel, old, new)

    def stats_pass(at, slots):
        loaded = load_pairs(slots)
        for p in range(2):
            for ab, (keys, values, tiles, first_side) in enumerate(units(loaded, p)):
                scores, dprobs = products(p, keys, values, first_side)
                saved[at, p, ab, 1] = dprobs
                for t, (sel, begin) in enumerate(tiles):
                    rows = slice(t * HALF, (t + 1) * HALF)
                    mask = eight >= begin[None]
                    masked = jnp.where(mask, scores[rows].reshape(8, 8, COLS) * SCALE2, FAR)
                    saved[at, p, ab, 0, rows] = masked.reshape(HALF, COLS)
                    stats_unit(p, sel, masked, dprobs[rows].reshape(8, 8, COLS))

    def grad_unit(p, sel, scores, dprobs):
        log_total = side_of(sel, lambda side: stats[0, p, side])
        delta = side_of(sel, lambda side: stats[1, p, side])
        probs = jnp.exp2(scores.reshape(8, 8, COLS) - log_total[None])
        dscores = probs * (dprobs.reshape(8, 8, COLS) - delta[None])
        return (
            probs.reshape(HALF, COLS).astype(BF16),
            dscores.reshape(HALF, COLS).astype(BF16),
        )

    def grad_tile(p, keys_t, sels, first_side, load):
        width = slice(128, 256) if first_side == 1 else slice(0, 256)
        probs_b, dscores_b = [], []
        for t, sel in enumerate(sels):
            one, two = grad_unit(p, sel, *load(slice(t * HALF, (t + 1) * HALF)))
            probs_b.append(one)
            dscores_b.append(two)
        probs_b = jnp.concatenate(probs_b, axis=0)
        dscores_b = jnp.concatenate(dscores_b, axis=0)
        dqacc[p, width, :] += mul_nn(keys_t, dscores_b)
        return mul_nn(dscores_b, qcat[p, :, width]), mul_nn(probs_b, gcat[p, :, width])

    def grad_pass(at, slots):
        small_k, large_k, unused_v, unused_w, firsts, flags = load_pairs(slots)
        small = [0.0, 0.0]
        large = [0.0, 0.0]
        small_t = jnp.concatenate(small_k, axis=0).T
        for p in range(2):
            mine_small, unused_flag = pair_small(pairs[p])
            sels = [j < mine_small for j in firsts]
            both_t = jnp.concatenate([halves(*b) for b in zip(sels, small_k, large_k)], axis=0).T

            def load(ab):
                return lambda rows: (saved[at, p, ab, 0, rows], saved[at, p, ab, 1, rows])

            grads_a = grad_tile(p, small_t, [None] * len(sels), 1, load(0))
            grads_b = grad_tile(p, both_t, sels, 0, load(1))
            for n in range(2):
                small[n] = small[n] + grads_a[n]
                zero = jnp.zeros((HALF, 128), F32)
                add_small, add_large = [], []
                for t, sel in enumerate(sels):
                    rows = slice(t * HALF, (t + 1) * HALF)
                    add_small.append(jnp.where(sel, grads_b[n][rows, :128], zero))
                    add_large.append(jnp.where(sel, zero, grads_b[n][rows, 128:]))
                small[n] = small[n] + jnp.concatenate(add_small, axis=0)
                large[n] = large[n] + jnp.concatenate(add_large, axis=0)
        for n in range(2):
            for t, flag in enumerate(flags):
                rows = slice(t * HALF, (t + 1) * HALF)
                at_slot, row = slots[t // 2], (t % 2) * 128
                turned = flag == 1
                lo, hi = small[n][rows], large[n][rows]
                part[at_slot, n, row : row + HALF, :] = jnp.where(turned, hi, lo)
                part[at_slot, n, row + HALF : row + 128, :] = jnp.where(turned, lo, hi)

    tri = lax.broadcasted_iota(jnp.int32, (8, 8, COLS), 1) + eight <= lax.rem(
        lax.broadcasted_iota(jnp.int32, (8, 8, COLS), 2), HALF
    )

    def own_tile(p):
        owner = core if p == 0 else sib
        small, flag = pair_small(pairs[p])
        turned = flag == 1
        zero = jnp.zeros((HALF, 128), BF16)

        def stack(n):
            pair = kv[mine, owner, n]
            lo, hi = pair[:HALF], pair[HALF:]
            return jnp.concatenate(
                [
                    jnp.concatenate([jnp.where(turned, hi, lo), zero], axis=1),
                    jnp.concatenate([zero, jnp.where(turned, lo, hi)], axis=1),
                ],
                axis=0,
            )

        masks = []
        for side in range(2):
            base = (small if side == 0 else blocks - 1 - small) * HALF
            masks.append(tri & (eight >= (start[p, side] - base)[None]))
        return stack(0), stack(1), masks, flag

    for p in range(2):
        if p == 0:
            relay(0)
            z_step(2)
        else:

            @pl.when(middle)
            def _():
                z_step(LINE - 1)

            relay(1)
        keys, values, masks, unused_flag = own_tile(p)
        scores, dprobs = products(p, keys, values, 0)
        for side in range(2):
            rows = slice(side * HALF, (side + 1) * HALF)
            s = jnp.where(masks[side], scores[rows].reshape(8, 8, COLS) * SCALE2, FAR)
            top = jnp.max(s, axis=0)
            probs = jnp.exp2(s - top[None])
            stats[0, p, side] = top
            stats[1, p, side] = jnp.sum(probs, axis=0)
            stats[2, p, side] = jnp.sum(probs * dprobs[rows].reshape(8, 8, COLS), axis=0)

    def far_tile(zz):
        return 2 * zz, [slot(xat(2), zz), slot(x, zz)]

    def near_tile(zz):
        return 2 * zz + 1, [slot(xat(RING - 1), zz), slot(xat(1), zz)]

    @pl.loop(0, LINE - 1)
    def _(turn):
        rest_of_x(turn)
        zz = z_turn(turn)
        stats_pass(*near_tile(zz))

        @pl.when((turn == 0) & jnp.logical_not(middle))
        def _():
            z_step(LINE - 1)

        for copy in relay_copies(zz):
            copy.wait_recv()

        @pl.when(turn == 0)
        def _():
            far_sends(lambda copy: copy.start())

        stats_pass(*far_tile(zz))

        @pl.when(turn == 0)
        def _():
            relay(2)

    last = z_turn(LINE - 1)
    far_block(last, z, 0).wait_recv()
    stats_pass(*far_tile(last))
    for n in range(2):
        for copy in x_piece(last, n):
            copy.wait_recv()
    stats_pass(*near_tile(last))

    for p in range(2):
        for side in range(2):
            top = stats[0, p, side]
            best = jnp.max(top, axis=0, keepdims=True)
            weight = jnp.exp2(top - best)
            total = jnp.sum(stats[1, p, side] * weight, axis=0, keepdims=True)
            weighted = jnp.sum(stats[2, p, side] * weight, axis=0, keepdims=True)
            stats[0, p, side] = jnp.broadcast_to(best + jnp.log2(total), (8, COLS))
            stats[1, p, side] = jnp.broadcast_to(weighted / total, (8, COLS))

    def far_copies(n):
        return remote(s1r.at[n], r1l.at[n], right, C1R + n), remote(s1l.at[n], r1r.at[n], left, C1L + n)

    def near_copies(n):
        return remote(s2r.at[n], r2l.at[n], right, C2R + n), remote(s2l.at[n], r2r.at[n], left, C2L + n)

    def last_copy(n):
        return remote(s3.at[n], r3.at[z], device(x, n, core), C3 + n, C3 + z)

    def send_far(turn):
        n = z_turn(turn)
        far = slot(xat(2), n)
        s1r[n] = part[far, 0].astype(BF16)
        s1l[n] = part[far, 1].astype(BF16)
        for copy in far_copies(n):
            copy.start()

    def send_near(turn):
        n = z_turn(turn)
        to_right, to_left = slot(xat(1), n), slot(xat(RING - 1), n)
        arrived = far_copies(n)
        onward = near_copies(n)
        s2r[n, 1] = part[to_right, 1].astype(BF16)
        s2l[n, 0] = part[to_left, 0].astype(BF16)
        arrived[0].wait_recv()
        s2r[n, 0] = (part[to_right, 0] + r1l[n].astype(F32)).astype(BF16)
        onward[0].start()
        arrived[1].wait_recv()
        s2l[n, 1] = (part[to_left, 1] + r1r[n].astype(F32)).astype(BF16)
        onward[1].start()

    def x_total(n):
        for copy in near_copies(n):
            copy.wait_recv()
        return part[slot(x, n)] + r2l[n].astype(F32) + r2r[n].astype(F32)

    def send_last(turn):
        n = z_turn(turn)
        s3[n] = x_total(n).astype(BF16)
        last_copy(n).start()

    @pl.loop(0, LINE)
    def _(i):
        turn = LINE - 1 - i
        zz = z_turn(turn)
        grad_pass(*far_tile(zz))
        send_far(turn)

    @pl.loop(0, LINE)
    def _(i):
        turn = LINE - 1 - i
        zz = z_turn(turn)
        grad_pass(*near_tile(zz))
        send_near(turn)

    for p in range(2):
        keys, values, masks, flag = own_tile(p)
        scores, dprobs = products(p, keys, values, 0)

        def load(rows):
            mask = masks[rows.start // HALF]
            return (
                jnp.where(mask, scores[rows].reshape(8, 8, COLS) * SCALE2, FAR),
                dprobs[rows],
            )

        grads = grad_tile(p, keys.T, [True, False], 0, load)
        rows = own_rows if p == 0 else sib_rows
        for n in range(2):
            lo, hi = grads[n][:HALF, :128], grads[n][HALF:, 128:]
            turned = flag == 1
            dextra[...] = jnp.concatenate(
                [jnp.where(turned, hi, lo), jnp.where(turned, lo, hi)], axis=0
            )
            part[mine, n, rows, :] += dextra[...]

    send_last(3)

    for p in range(2):
        unused_small, flag = pair_small(pairs[p])
        turned = flag == 1
        every = dqacc[p].T * SCALE
        for h in range(GROUP_HEADS):
            lo, hi = every[h * HALF : (h + 1) * HALF, :128], every[h * HALF : (h + 1) * HALF, 128:]
            dqout[p, :HALF, h * 128 : h * 128 + 128] = jnp.where(turned, hi, lo).astype(BF16)
            dqout[p, HALF:, h * 128 : h * 128 + 128] = jnp.where(turned, lo, hi).astype(BF16)
    send_last(2)
    dq_out = remote(dqout.at[1], dq_ref.at[core], brother, DQ)
    dq_out.start()
    dq_own = pltpu.make_async_copy(dqout.at[0], dq_ref.at[core], local_sem.at[4])
    dq_own.start()

    send_last(1)
    part[mine] = x_total(z)
    for k in range(1, LINE):
        there = zat(k)
        remote(s3.at[0], r3.at[there], right, C3 + there).wait_recv()
    for n, factor in ((0, SCALE), (1, 1.0)):
        whole = part[mine, n]
        for k in range(1, LINE):
            whole = whole + r3[zat(k), n].astype(F32)
        fin[n] = (whole * factor).astype(BF16)
    outs = [
        remote(fin.at[0, sib_rows, :], dk_ref.at[core], brother, OUT),
        remote(fin.at[1, sib_rows, :], dv_ref.at[core], brother, OUT + 1),
    ]
    for out in outs:
        out.start()
    keep = [
        pltpu.make_async_copy(fin.at[0, own_rows, :], dk_ref.at[core], local_sem.at[5]),
        pltpu.make_async_copy(fin.at[1, own_rows, :], dv_ref.at[core], local_sem.at[6]),
    ]
    for copy in keep:
        copy.start()
    dq_own.wait()
    for copy in keep:
        copy.wait()
    dq_out.wait_recv()
    for out in outs:
        out.wait_recv()
    for copy in swaps + outs + [dq_out]:
        copy.wait_send()
    for n in range(LINE):
        for copy in x_piece(n, 0) + x_piece(n, 1) + near_copies(n):
            copy.wait_send()
        for piece in range(2):
            z_onward(n, piece, lambda copy: copy.wait_send())
    for turn in (0, 1, 2):
        for copy in relay_copies(z_turn(turn)):
            copy.wait_send()
    for turn in range(LINE):
        for copy in far_copies(z_turn(turn)):
            copy.wait_send()
    far_sends(lambda copy: copy.wait_send())
    for k in range(1, LINE):
        last_copy(zat(k)).wait_send()


SWAP, OUT, DQ, ZED, XR, XL = 0, 4, 6, 8, 24, 32
FR, FL, C1R, C1L, C2R, C2L, C3 = range(40, 40 + 7 * LINE, LINE)
FAR_Z = 40 + 7 * LINE
COPIES = FAR_Z + 2


def per_device(q, k, v, g, lengths, assignment):
    slots = RING * LINE
    anywhere = pl.BlockSpec(memory_space=pl.ANY)
    smem = pl.BlockSpec(memory_space=pltpu.SMEM)
    half = (LINE, 256, 128)
    full = (LINE, 2, 256, 128)
    halves = pl.pallas_call(
        kernel,
        out_shape=(
            jax.ShapeDtypeStruct((2, 128, 1024), BF16),
            jax.ShapeDtypeStruct((2, 128, 128), BF16),
            jax.ShapeDtypeStruct((2, 128, 128), BF16),
        ),
        in_specs=[anywhere] * 4 + [smem] * 2,
        out_specs=(anywhere, anywhere, anywhere),
        scratch_shapes=[
            pltpu.VMEM((slots, 2, 2, 128, 128), BF16),
            pltpu.VMEM((2, 128, 1024), BF16),
            pltpu.VMEM((2, 128, 1024), BF16),
            pltpu.VMEM((2, COLS, 256), BF16),
            pltpu.VMEM((2, COLS, 256), BF16),
            pltpu.VMEM((3, 2, 2, 8, COLS), F32),
            pltpu.VMEM((2, 2, 8, COLS), jnp.int32),
            pltpu.VMEM((2, 256, COLS), F32),
            pltpu.VMEM((slots, 2, 256, 128), F32),
            pltpu.VMEM((128, 128), F32),
            pltpu.VMEM((2, 128, 1024), BF16),
            pltpu.VMEM((2, 256, 128), BF16),
            pltpu.VMEM(half, BF16),
            pltpu.VMEM(half, BF16),
            pltpu.VMEM(half, BF16),
            pltpu.VMEM(half, BF16),
            pltpu.VMEM(full, BF16),
            pltpu.VMEM(full, BF16),
            pltpu.VMEM(full, BF16),
            pltpu.VMEM(full, BF16),
            pltpu.VMEM(full, BF16),
            pltpu.VMEM(full, BF16),
            pltpu.VMEM((2 * LINE, 2, 2, 2, 4 * HALF, COLS), F32),
            pltpu.SemaphoreType.DMA((7,)),
            pltpu.SemaphoreType.DMA((COPIES,)),
            pltpu.SemaphoreType.DMA((COPIES,)),
        ],
        compiler_params=pltpu.CompilerParams(
            collective_id=0, has_side_effects=True, vmem_limit_bytes=63 * 1024 * 1024
        ),
    )(q, k, v, g, lengths, assignment)
    dq, dk, dv = halves
    dq = dq.transpose(1, 0, 2).reshape(q.shape)
    return dq, jnp.concatenate([dk[0], dk[1]], axis=1), jnp.concatenate([dv[0], dv[1]], axis=1)


def solution(mesh):
    return jax.shard_map(
        per_device,
        mesh=mesh,
        in_specs=(
            P(("rep", "round"), "head"),
            P(("rep", "round"), "head"),
            P(("rep", "round"), "head"),
            P(("rep", "round"), "head"),
            P("rep"),
            P("rep"),
        ),
        out_specs=(
            P(("rep", "round"), "head"),
            P(("rep", "round"), "head"),
            P(("rep", "round"), "head"),
        ),
        check_vma=False,
    )
```

```python
import functools
import math

import jax
import jax.numpy as jnp
from jax import lax
from jax.experimental import pallas as pl
from jax.experimental.pallas import tpu as pltpu
from jax.sharding import PartitionSpec as P

HEAD_SIZE = 128
RWIN = 8
HALF = 64
RING = 4
LINE = 4
GROUP_HEADS = 8
COLS = GROUP_HEADS * HALF
SCALE = HEAD_SIZE**-0.5
SCALE2 = SCALE * math.log2(math.e)
FAR = -1e30
MESH = pl.DeviceIdType.MESH
F32 = jnp.float32
BF16 = jnp.bfloat16


def mul_nt(a, b):
    return lax.dot_general(a, b, (((1,), (1,)), ((), ())), preferred_element_type=F32)


def mul_nn(a, b):
    return lax.dot_general(a, b, (((1,), (0,)), ((), ())), preferred_element_type=F32)


def mul_tn(a, b):
    return lax.dot_general(a, b, (((0,), (0,)), ((), ())), preferred_element_type=F32)


def kernel(
    q_ref, k_ref, v_ref, g_ref, len_ref, asg_ref,
    dq_ref, dk_ref, dv_ref,
    kv, qin, gin, qcat, gcat, stats, start, dqacc, part, dextra, dqout, fin,
    s1r, s1l, r1l, r1r, s2r, s2l, r2l, r2r, s3, r3,
    saved, local_sem, send_sem, recv_sem,
):
    blocks = asg_ref.shape[0]
    me = lax.axis_index("round")
    core, chip = lax.rem(me, 2), lax.div(me, 2)
    z, x = lax.rem(chip, LINE), lax.div(chip, LINE)
    sib = 1 - core

    def device(xx, zz, cc):
        return {"round": (xx * LINE + zz) * 2 + cc}

    def xat(k):
        return lax.rem(x + k, RING)

    def zat(k):
        return lax.rem(z + k, LINE)

    def remote(src, dst, target, sent, got=None):
        return pltpu.make_async_remote_copy(
            src_ref=src, dst_ref=dst, send_sem=send_sem.at[sent],
            recv_sem=recv_sem.at[sent if got is None else got],
            device_id=target, device_id_type=MESH,
        )

    def z_turn(n):
        low = jnp.minimum(z, LINE - 1 - z)
        inner = jnp.where(n == 0, 1, jnp.where(n == 1, 2, jnp.where(n == 2, 0, 3)))
        at = jnp.where(low == 0, n, inner)
        return jnp.where(z >= LINE // 2, LINE - 1 - at, at)

    right, left = device(xat(1), z, core), device(xat(RING - 1), z, core)
    brother = device(x, z, sib)

    barrier = pltpu.get_barrier_semaphore()
    peers = [brother, right, left] + [device(x, zat(k), core) for k in range(1, LINE)]
    for peer in peers:
        pl.semaphore_signal(barrier, inc=1, device_id=peer, device_id_type=MESH)
    pl.semaphore_wait(barrier, len(peers))

    def lanes(index, width):
        return pl.ds(pl.multiple_of(index * width, width), width)

    mine = z * RING + x
    own_rows, sib_rows = lanes(core, 128), lanes(sib, 128)
    wide = GROUP_HEADS * HEAD_SIZE
    swaps = [
        remote(k_ref.at[:, lanes(sib, 128)], kv.at[mine, core, 0], brother, SWAP),
        remote(v_ref.at[:, lanes(sib, 128)], kv.at[mine, core, 1], brother, SWAP + 1),
        remote(q_ref.at[:, lanes(sib, wide)], qin.at[1], brother, SWAP + 2),
        remote(g_ref.at[:, lanes(sib, wide)], gin.at[1], brother, SWAP + 3),
    ]
    own = [
        pltpu.make_async_copy(k_ref.at[:, lanes(core, 128)], kv.at[mine, core, 0], local_sem.at[0]),
        pltpu.make_async_copy(v_ref.at[:, lanes(core, 128)], kv.at[mine, core, 1], local_sem.at[1]),
        pltpu.make_async_copy(q_ref.at[:, lanes(core, wide)], qin.at[0], local_sem.at[2]),
        pltpu.make_async_copy(g_ref.at[:, lanes(core, wide)], gin.at[0], local_sem.at[3]),
    ]
    for copy in own[:2] + swaps + own[2:]:
        copy.start()

    def slot(xx, zz):
        return zz * RING + xx

    up, down = device(x, jnp.minimum(z + 1, LINE - 1), core), device(x, jnp.maximum(z - 1, 0), core)

    def z_piece(zz, n, target):
        piece = kv.at[slot(x, zz), n]
        return remote(piece, piece, target, ZED + 8 * n + zz, ZED + 8 * n + zz)

    def z_onward(zz, n, do):
        piece = kv.at[slot(x, zz), n]

        @pl.when((zz <= z) & (z < LINE - 1))
        def _():
            do(remote(piece, piece, up, ZED + 8 * n + zz))

        @pl.when((zz >= z) & (z > 0))
        def _():
            do(remote(piece, piece, down, ZED + 8 * n + 4 + zz, ZED + 8 * n + zz))

    def x_piece(zz, n):
        piece = kv.at[slot(x, zz), n]
        return (
            remote(piece, piece, right, XR + 4 * n + zz),
            remote(piece, piece, left, XL + 4 * n + zz),
        )

    def relay_copies(zz):
        piece_r = kv.at[slot(xat(RING - 1), zz), core]
        piece_l = kv.at[slot(xat(1), zz), sib]
        return remote(piece_r, piece_r, right, FR + zz), remote(piece_l, piece_l, left, FL + zz)

    def send_piece(zz, n):
        for copy in x_piece(zz, n):
            copy.start()
        z_onward(zz, n, lambda copy: copy.start())

    middle = (z > 0) & (z < LINE - 1)

    def z_step(turn):
        zz = z_turn(turn)
        for n in (core, sib):
            z_piece(zz, n, up).wait_recv()
            send_piece(zz, n)

    def relay(turn):
        zz = z_turn(turn)
        onward = relay_copies(zz)
        x_piece(zz, core)[0].wait_recv()
        onward[0].start()
        x_piece(zz, sib)[1].wait_recv()
        onward[1].start()

    def far_block(zz, target, k):
        block = kv.at[slot(xat(2), zz)]
        return remote(block, block, device(x, target, core), FAR_Z + k, FAR_Z)

    def far_sends(do):
        @pl.when(jnp.logical_not(middle))
        def _():
            do(far_block(z, LINE - 1 - z, 0))
            do(far_block(z, jnp.where(z == 0, 2, 1), 1))

    def rest_of_x(turn):
        zz = z_turn(turn)
        x_piece(zz, core)[1].wait_recv()
        x_piece(zz, sib)[0].wait_recv()

    for copy in own[:2]:
        copy.wait()
    send_piece(z, core)
    for swap in swaps[:2]:
        swap.wait_recv()
    send_piece(z, sib)

    pairs = [2 * chip + core, 2 * chip + sib]

    def pair_small(pair):
        first, second = asg_ref[2 * pair], asg_ref[2 * pair + 1]
        return jnp.minimum(first, second), (first > second).astype(jnp.int32)

    ends, total = [], 0
    for j in range(15):
        total = total + len_ref[j]
        ends.append(total)
    lane_row = lax.rem(lax.broadcasted_iota(jnp.int32, (8, COLS), 1), HALF)
    sub_row = lax.broadcasted_iota(jnp.int32, (8, COLS), 0)
    for p in range(2):
        small, flag = pair_small(pairs[p])
        if p == 0:
            own[2].wait()
            own[3].wait()
        else:
            z_step(1)
            swaps[2].wait_recv()
            swaps[3].wait_recv()
        for side in range(2):
            turned = flag == 1 - side
            for h in range(GROUP_HEADS):
                to = (p, slice(h * HALF, (h + 1) * HALF), slice(side * 128, side * 128 + 128))
                cols = slice(h * 128, h * 128 + 128)
                qcat[to] = jnp.where(turned, qin[p, HALF:, cols], qin[p, :HALF, cols])
                gcat[to] = jnp.where(turned, gin[p, HALF:, cols], gin[p, :HALF, cols])
            base = (small if side == 0 else blocks - 1 - small) * HALF
            first = jnp.zeros((8, COLS), jnp.int32)
            for j in range(15 - RWIN + 1):
                first = jnp.where(base + lane_row >= ends[j + RWIN - 1], ends[j], first)
            start[p, side] = first - sub_row
        dqacc[p] = jnp.zeros((256, COLS), F32)

    eight = 8 * lax.broadcasted_iota(jnp.int32, (8, 8, COLS), 0)
    never = 1 << 20

    def load_pairs(slots):
        small_k, large_k, small_v, large_v, firsts, flags = [], [], [], [], [], []
        for t in range(2 * len(slots)):
            at = slots[t // 2]
            pair = (lax.rem(at, RING) * LINE + lax.div(at, RING)) * 2 + t % 2
            small, flag = pair_small(pair)
            turned = flag == 1
            for n, small_n, large_n in ((0, small_k, large_k), (1, small_v, large_v)):
                lo, hi = kv[at, t % 2, n, :HALF, :], kv[at, t % 2, n, HALF:, :]
                small_n.append(jnp.where(turned, hi, lo))
                large_n.append(jnp.where(turned, lo, hi))
            firsts.append(small)
            flags.append(flag)
        return small_k, large_k, small_v, large_v, firsts, flags

    def halves(sel, small, large):
        zero = jnp.zeros_like(small)
        return jnp.concatenate(
            [jnp.where(sel, small, zero), jnp.where(sel, zero, large)], axis=1
        )

    def units(loaded, p):
        small_k, large_k, small_v, large_v, firsts, unused_flags = loaded
        mine_small, unused_flag = pair_small(pairs[p])
        tile_a, tile_b = [], []
        sels = []
        for j in firsts:
            sel = j < mine_small
            sels.append(sel)
            tile_a.append((None, start[p, 1] - j * HALF))
            begin = jnp.where(sel, start[p, 0] - j * HALF, start[p, 1] - (blocks - 1 - j) * HALF)
            tile_b.append((sel, jnp.where(j == mine_small, never, begin)))
        keys_a = jnp.concatenate(small_k, axis=0)
        values_a = jnp.concatenate(small_v, axis=0)
        keys_b = jnp.concatenate([halves(*b) for b in zip(sels, small_k, large_k)], axis=0)
        values_b = jnp.concatenate([halves(*b) for b in zip(sels, small_v, large_v)], axis=0)
        return (keys_a, values_a, tile_a, 1), (keys_b, values_b, tile_b, 0)

    def side_of(sel, ref_at):
        if sel is None:
            return ref_at(1)
        return jnp.where(sel, ref_at(0), ref_at(1))

    def products(p, keys, values, first_side):
        width = slice(128, 256) if first_side == 1 else slice(0, 256)
        return mul_nt(keys, qcat[p, :, width]), mul_nt(values, gcat[p, :, width])

    def stats_unit(p, sel, scores, dprobs):
        top = side_of(sel, lambda side: stats[0, p, side])
        new_top = jnp.maximum(top, jnp.max(scores, axis=0))
        rescale = jnp.exp2(top - new_top)
        probs = jnp.exp2(scores - new_top[None])
        total = side_of(sel, lambda side: stats[1, p, side]) * rescale + jnp.sum(probs, axis=0)
        weighted = side_of(sel, lambda side: stats[2, p, side]) * rescale + jnp.sum(
            probs * dprobs, axis=0
        )
        for n, new in enumerate((new_top, total, weighted)):
            if sel is None:
                stats[n, p, 1] = new
            else:
                old = stats[n, p, 1]
                stats[n, p, 0] = jnp.where(sel, new, stats[n, p, 0])
                stats[n, p, 1] = jnp.where(sel, old, new)

    def stats_pass(at, slots):
        loaded = load_pairs(slots)
        for p in range(2):
            for ab, (keys, values, tiles, first_side) in enumerate(units(loaded, p)):
                scores, dprobs = products(p, keys, values, first_side)
                saved[at, p, ab, 1] = dprobs
                for t, (sel, begin) in enumerate(tiles):
                    rows = slice(t * HALF, (t + 1) * HALF)
                    mask = eight >= begin[None]
                    masked = jnp.where(mask, scores[rows].reshape(8, 8, COLS) * SCALE2, FAR)
                    saved[at, p, ab, 0, rows] = masked.reshape(HALF, COLS)
                    stats_unit(p, sel, masked, dprobs[rows].reshape(8, 8, COLS))

    def grad_unit(p, sel, scores, dprobs):
        log_total = side_of(sel, lambda side: stats[0, p, side])
        delta = side_of(sel, lambda side: stats[1, p, side])
        probs = jnp.exp2(scores.reshape(8, 8, COLS) - log_total[None])
        dscores = probs * (dprobs.reshape(8, 8, COLS) - delta[None])
        return (
            probs.reshape(HALF, COLS).astype(BF16),
            dscores.reshape(HALF, COLS).astype(BF16),
        )

    def grad_tile(p, keys_t, sels, first_side, load):
        width = slice(128, 256) if first_side == 1 else slice(0, 256)
        probs_b, dscores_b = [], []
        for t, sel in enumerate(sels):
            one, two = grad_unit(p, sel, *load(slice(t * HALF, (t + 1) * HALF)))
            probs_b.append(one)
            dscores_b.append(two)
        probs_b = jnp.concatenate(probs_b, axis=0)
        dscores_b = jnp.concatenate(dscores_b, axis=0)
        dqacc[p, width, :] += mul_nn(keys_t, dscores_b)
        return mul_nn(dscores_b, qcat[p, :, width]), mul_nn(probs_b, gcat[p, :, width])

    def grad_pass(at, slots):
        small_k, large_k, unused_v, unused_w, firsts, flags = load_pairs(slots)
        small = [0.0, 0.0]
        large = [0.0, 0.0]
        small_t = jnp.concatenate(small_k, axis=0).T
        for p in range(2):
            mine_small, unused_flag = pair_small(pairs[p])
            sels = [j < mine_small for j in firsts]
            both_t = jnp.concatenate([halves(*b) for b in zip(sels, small_k, large_k)], axis=0).T

            def load(ab):
                return lambda rows: (saved[at, p, ab, 0, rows], saved[at, p, ab, 1, rows])

            grads_a = grad_tile(p, small_t, [None] * len(sels), 1, load(0))
            grads_b = grad_tile(p, both_t, sels, 0, load(1))
            for n in range(2):
                small[n] = small[n] + grads_a[n]
                zero = jnp.zeros((HALF, 128), F32)
                add_small, add_large = [], []
                for t, sel in enumerate(sels):
                    rows = slice(t * HALF, (t + 1) * HALF)
                    add_small.append(jnp.where(sel, grads_b[n][rows, :128], zero))
                    add_large.append(jnp.where(sel, zero, grads_b[n][rows, 128:]))
                small[n] = small[n] + jnp.concatenate(add_small, axis=0)
                large[n] = large[n] + jnp.concatenate(add_large, axis=0)
        for n in range(2):
            for t, flag in enumerate(flags):
                rows = slice(t * HALF, (t + 1) * HALF)
                at_slot, row = slots[t // 2], (t % 2) * 128
                turned = flag == 1
                lo, hi = small[n][rows], large[n][rows]
                part[at_slot, n, row : row + HALF, :] = jnp.where(turned, hi, lo)
                part[at_slot, n, row + HALF : row + 128, :] = jnp.where(turned, lo, hi)

    tri = lax.broadcasted_iota(jnp.int32, (8, 8, COLS), 1) + eight <= lax.rem(
        lax.broadcasted_iota(jnp.int32, (8, 8, COLS), 2), HALF
    )

    def own_tile(p):
        owner = core if p == 0 else sib
        small, flag = pair_small(pairs[p])
        turned = flag == 1
        zero = jnp.zeros((HALF, 128), BF16)

        def stack(n):
            pair = kv[mine, owner, n]
            lo, hi = pair[:HALF], pair[HALF:]
            return jnp.concatenate(
                [
                    jnp.concatenate([jnp.where(turned, hi, lo), zero], axis=1),
                    jnp.concatenate([zero, jnp.where(turned, lo, hi)], axis=1),
                ],
                axis=0,
            )

        masks = []
        for side in range(2):
            base = (small if side == 0 else blocks - 1 - small) * HALF
            masks.append(tri & (eight >= (start[p, side] - base)[None]))
        return stack(0), stack(1), masks, flag

    for p in range(2):
        if p == 0:
            relay(0)
            z_step(2)
        else:

            @pl.when(middle)
            def _():
                z_step(LINE - 1)

            relay(1)
        keys, values, masks, unused_flag = own_tile(p)
        scores, dprobs = products(p, keys, values, 0)
        for side in range(2):
            rows = slice(side * HALF, (side + 1) * HALF)
            s = jnp.where(masks[side], scores[rows].reshape(8, 8, COLS) * SCALE2, FAR)
            top = jnp.max(s, axis=0)
            probs = jnp.exp2(s - top[None])
            stats[0, p, side] = top
            stats[1, p, side] = jnp.sum(probs, axis=0)
            stats[2, p, side] = jnp.sum(probs * dprobs[rows].reshape(8, 8, COLS), axis=0)

    @pl.loop(0, LINE)
    def _(turn):
        rest_of_x(turn)
        zz = z_turn(turn)

        @pl.when(turn == LINE - 1)
        def _():
            x_piece(zz, core)[0].wait_recv()
            x_piece(zz, sib)[1].wait_recv()

        stats_pass(2 * zz + 1, [slot(xat(RING - 1), zz), slot(x, zz)])

        @pl.when((turn == 0) & jnp.logical_not(middle))
        def _():
            z_step(LINE - 1)

        @pl.when(turn < LINE - 1)
        def _():
            for copy in relay_copies(zz):
                copy.wait_recv()

        @pl.when(turn == LINE - 1)
        def _():
            far_block(zz, z, 0).wait_recv()

        @pl.when(turn == 0)
        def _():
            far_sends(lambda copy: copy.start())

        stats_pass(2 * zz, [slot(xat(2), zz), slot(xat(1), zz)])

        @pl.when(turn == 0)
        def _():
            relay(2)

    for p in range(2):
        for side in range(2):
            top = stats[0, p, side]
            best = jnp.max(top, axis=0, keepdims=True)
            weight = jnp.exp2(top - best)
            total = jnp.sum(stats[1, p, side] * weight, axis=0, keepdims=True)
            weighted = jnp.sum(stats[2, p, side] * weight, axis=0, keepdims=True)
            stats[0, p, side] = jnp.broadcast_to(best + jnp.log2(total), (8, COLS))
            stats[1, p, side] = jnp.broadcast_to(weighted / total, (8, COLS))

    def far_copies(n):
        return remote(s1r.at[n], r1l.at[n], right, C1R + n), remote(s1l.at[n], r1r.at[n], left, C1L + n)

    def near_copies(n):
        return remote(s2r.at[n], r2l.at[n], right, C2R + n), remote(s2l.at[n], r2r.at[n], left, C2L + n)

    def last_copy(n):
        return remote(s3.at[n], r3.at[z], device(x, n, core), C3 + n, C3 + z)

    def send_far(turn):
        n = z_turn(turn)
        far = slot(xat(2), n)
        s1r[n] = part[far, 0].astype(BF16)
        s1l[n] = part[far, 1].astype(BF16)
        for copy in far_copies(n):
            copy.start()

    def send_near(turn):
        n = z_turn(turn)
        to_right, to_left = slot(xat(1), n), slot(xat(RING - 1), n)
        arrived = far_copies(n)
        onward = near_copies(n)
        s2r[n, 1] = part[to_right, 1].astype(BF16)
        s2l[n, 0] = part[to_left, 0].astype(BF16)
        arrived[0].wait_recv()
        s2r[n, 0] = (part[to_right, 0] + r1l[n].astype(F32)).astype(BF16)
        onward[0].start()
        arrived[1].wait_recv()
        s2l[n, 1] = (part[to_left, 1] + r1r[n].astype(F32)).astype(BF16)
        onward[1].start()

    def x_total(n):
        for copy in near_copies(n):
            copy.wait_recv()
        return part[slot(x, n)] + r2l[n].astype(F32) + r2r[n].astype(F32)

    def send_last(turn):
        n = z_turn(turn)
        s3[n] = x_total(n).astype(BF16)
        last_copy(n).start()

    @pl.loop(0, LINE)
    def _(i):
        turn = LINE - 1 - i
        zz = z_turn(turn)
        grad_pass(2 * zz, [slot(xat(2), zz), slot(xat(1), zz)])
        send_far(turn)

    @pl.loop(0, LINE)
    def _(i):
        turn = LINE - 1 - i
        zz = z_turn(turn)
        grad_pass(2 * zz + 1, [slot(xat(RING - 1), zz), slot(x, zz)])
        send_near(turn)

    for p in range(2):
        keys, values, masks, flag = own_tile(p)
        scores, dprobs = products(p, keys, values, 0)

        def load(rows):
            mask = masks[rows.start // HALF]
            return (
                jnp.where(mask, scores[rows].reshape(8, 8, COLS) * SCALE2, FAR),
                dprobs[rows],
            )

        grads = grad_tile(p, keys.T, [True, False], 0, load)
        rows = own_rows if p == 0 else sib_rows
        for n in range(2):
            lo, hi = grads[n][:HALF, :128], grads[n][HALF:, 128:]
            turned = flag == 1
            dextra[...] = jnp.concatenate(
                [jnp.where(turned, hi, lo), jnp.where(turned, lo, hi)], axis=0
            )
            part[mine, n, rows, :] += dextra[...]

    for p in range(2):
        unused_small, flag = pair_small(pairs[p])
        turned = flag == 1
        every = dqacc[p].T * SCALE
        for h in range(GROUP_HEADS):
            lo, hi = every[h * HALF : (h + 1) * HALF, :128], every[h * HALF : (h + 1) * HALF, 128:]
            dqout[p, :HALF, h * 128 : h * 128 + 128] = jnp.where(turned, hi, lo).astype(BF16)
            dqout[p, HALF:, h * 128 : h * 128 + 128] = jnp.where(turned, lo, hi).astype(BF16)
    dq_out = remote(dqout.at[1], dq_ref.at[core], brother, DQ)
    dq_out.start()
    dq_own = pltpu.make_async_copy(dqout.at[0], dq_ref.at[core], local_sem.at[4])
    dq_own.start()

    for turn in (3, 2, 1):
        send_last(turn)
    part[mine] = x_total(z)
    for k in range(1, LINE):
        there = zat(k)
        remote(s3.at[0], r3.at[there], right, C3 + there).wait_recv()
    for n, factor in ((0, SCALE), (1, 1.0)):
        whole = part[mine, n]
        for k in range(1, LINE):
            whole = whole + r3[zat(k), n].astype(F32)
        fin[n] = (whole * factor).astype(BF16)
    outs = [
        remote(fin.at[0, sib_rows, :], dk_ref.at[core], brother, OUT),
        remote(fin.at[1, sib_rows, :], dv_ref.at[core], brother, OUT + 1),
    ]
    for out in outs:
        out.start()
    keep = [
        pltpu.make_async_copy(fin.at[0, own_rows, :], dk_ref.at[core], local_sem.at[5]),
        pltpu.make_async_copy(fin.at[1, own_rows, :], dv_ref.at[core], local_sem.at[6]),
    ]
    for copy in keep:
        copy.start()
    dq_own.wait()
    for copy in keep:
        copy.wait()
    dq_out.wait_recv()
    for out in outs:
        out.wait_recv()
    for copy in swaps + outs + [dq_out]:
        copy.wait_send()
    for n in range(LINE):
        for copy in x_piece(n, 0) + x_piece(n, 1) + near_copies(n):
            copy.wait_send()
        for piece in range(2):
            z_onward(n, piece, lambda copy: copy.wait_send())
    for turn in (0, 1, 2):
        for copy in relay_copies(z_turn(turn)):
            copy.wait_send()
    for turn in range(LINE):
        for copy in far_copies(z_turn(turn)):
            copy.wait_send()
    far_sends(lambda copy: copy.wait_send())
    for k in range(1, LINE):
        last_copy(zat(k)).wait_send()


SWAP, OUT, DQ, ZED, XR, XL = 0, 4, 6, 8, 24, 32
FR, FL, C1R, C1L, C2R, C2L, C3 = range(40, 40 + 7 * LINE, LINE)
FAR_Z = 40 + 7 * LINE
COPIES = FAR_Z + 2


def per_device(q, k, v, g, lengths, assignment):
    slots = RING * LINE
    anywhere = pl.BlockSpec(memory_space=pl.ANY)
    smem = pl.BlockSpec(memory_space=pltpu.SMEM)
    half = (LINE, 256, 128)
    full = (LINE, 2, 256, 128)
    halves = pl.pallas_call(
        kernel,
        out_shape=(
            jax.ShapeDtypeStruct((2, 128, 1024), BF16),
            jax.ShapeDtypeStruct((2, 128, 128), BF16),
            jax.ShapeDtypeStruct((2, 128, 128), BF16),
        ),
        in_specs=[anywhere] * 4 + [smem] * 2,
        out_specs=(anywhere, anywhere, anywhere),
        scratch_shapes=[
            pltpu.VMEM((slots, 2, 2, 128, 128), BF16),
            pltpu.VMEM((2, 128, 1024), BF16),
            pltpu.VMEM((2, 128, 1024), BF16),
            pltpu.VMEM((2, COLS, 256), BF16),
            pltpu.VMEM((2, COLS, 256), BF16),
            pltpu.VMEM((3, 2, 2, 8, COLS), F32),
            pltpu.VMEM((2, 2, 8, COLS), jnp.int32),
            pltpu.VMEM((2, 256, COLS), F32),
            pltpu.VMEM((slots, 2, 256, 128), F32),
            pltpu.VMEM((128, 128), F32),
            pltpu.VMEM((2, 128, 1024), BF16),
            pltpu.VMEM((2, 256, 128), BF16),
            pltpu.VMEM(half, BF16),
            pltpu.VMEM(half, BF16),
            pltpu.VMEM(half, BF16),
            pltpu.VMEM(half, BF16),
            pltpu.VMEM(full, BF16),
            pltpu.VMEM(full, BF16),
            pltpu.VMEM(full, BF16),
            pltpu.VMEM(full, BF16),
            pltpu.VMEM(full, BF16),
            pltpu.VMEM(full, BF16),
            pltpu.VMEM((2 * LINE, 2, 2, 2, 4 * HALF, COLS), F32),
            pltpu.SemaphoreType.DMA((7,)),
            pltpu.SemaphoreType.DMA((COPIES,)),
            pltpu.SemaphoreType.DMA((COPIES,)),
        ],
        compiler_params=pltpu.CompilerParams(
            collective_id=0, has_side_effects=True, vmem_limit_bytes=63 * 1024 * 1024
        ),
    )(q, k, v, g, lengths, assignment)
    return tuple(jnp.concatenate([out[0], out[1]], axis=1) for out in halves)


def solution(mesh):
    return jax.shard_map(
        per_device,
        mesh=mesh,
        in_specs=(
            P(("rep", "round"), "head"),
            P(("rep", "round"), "head"),
            P(("rep", "round"), "head"),
            P(("rep", "round"), "head"),
            P("rep"),
            P("rep"),
        ),
        out_specs=(
            P(("rep", "round"), "head"),
            P(("rep", "round"), "head"),
            P(("rep", "round"), "head"),
        ),
        check_vma=False,
    )
```
